256 devices in a mesh: fsdp: 4 (over y_lo, core), ctx: 64 (over z, y_hi, x).
Axes of the slice: x: 4, y: 4 (y_hi: 2, y_lo: 2; y = y_hi * 2 + y_lo), z: 8, core: 2. Of those that a mesh axis runs over, the one named last changes fastest.
Arguments:
- tokens: bfloat16 [4, 8192, 2048], P('fsdp', 'ctx'), may hold values from -6 to 6
- norm_gain: float32 [2048], replicated, may hold values from 0.5 to 1.5
- in_weight: bfloat16 [2048, 6144], P(('fsdp', 'ctx')), may hold values from -0.125 to 0.125
- short_filter: float32 [3, 6144], replicated, may hold values from -3.5 to 3.5
- rates: float32 [2048, 16], P('ctx'), may hold values from 3.0517578e-05 to 0.033333335
- residues: float32 [2048, 16], P('ctx'), may hold values from -1.5 to 1.5
- skip: float32 [2048], P('ctx'), may hold values from 0.5 to 2
Outputs:
- mixed: bfloat16 [4, 2048, 8192], P('fsdp', None, 'ctx')
The draws below stay inside these ranges and needn't reach their ends.
All inputs are finite; a program needn't handle non-finite values.
Results may differ from the reference program's by a relative error of at most 0.0092.
Values may be sent and summed in bfloat16 or wider, within the bound.
No kernel may reach another device: no remote copies, remote signals or barrier semaphores. Data moves between devices by JAX's collectives and lax.ppermute only.
A program may use at most 128 MiB of HBM per device.

```python
import math
import jax
import jax.numpy as jnp
from jax import lax

D = 2048
C = 2048
POLES = 16
TAPS = 3
SEQS = 4
LEN = 8192


def shard_levels(rng, shape, pieces, smallest, top_value):
    def one(dim, shards_of):
        draws = jax.random.uniform(jax.random.fold_in(jax.random.fold_in(rng, 6), dim), (shards_of,), jnp.float32, smallest / len(pieces), top_value / len(pieces))
        return jnp.repeat(jnp.exp(draws), shape[dim] // shards_of).reshape((-1,) + (1,) * (len(shape) - dim - 1))

    loudness = one(*pieces[0])
    for cut in pieces[1:]:
        loudness = loudness * one(*cut)
    return loudness


def scatter_about(stream_key, shape, scale, limit, cuts=(), held_as=jnp.bfloat16):
    drawn = scale * jax.random.normal(stream_key, shape, jnp.float32)
    if cuts:
        drawn = drawn * shard_levels(stream_key, shape, cuts, -0.22, 0.18)
    return jnp.clip(drawn, -limit, limit).astype(held_as)


def setup_inputs(seed: int = 0) -> dict:
    splits = jax.random.split(jax.random.key(seed), 8)
    return {
        "tokens": scatter_about(splits[0], (SEQS, LEN, D), 1.0, 6.0, ((0, 4), (1, 64))),
        "norm_gain": jnp.clip(1.0 + 0.1 * jax.random.normal(splits[1], (D,), jnp.float32), 0.5, 1.5),
        "in_weight": scatter_about(splits[2], (D, 3 * C), D ** -0.5, 0.125, ((0, 256),)),
        "short_filter": scatter_about(splits[3], (TAPS, 3 * C), TAPS ** -0.5, 3.5, (), jnp.float32),
        "rates": jnp.clip(jnp.exp(math.log(0.033333335) - 6.9960104 * jax.random.uniform(splits[4], (C, POLES), jnp.float32) ** shard_levels(splits[4], (C, POLES), ((0, 64),), -0.2, 0.2)), 3.0517578125e-05, 0.033333335),
        "residues": scatter_about(splits[5], (C, POLES), POLES ** -0.5, 1.5, ((0, 64),), jnp.float32),
        "skip": jnp.clip(0.5 + 1.5 * jax.random.uniform(splits[6], (C,), jnp.float32) ** shard_levels(splits[6], (C,), ((0, 64),), -0.2, 0.2), 0.5, 2.0),
    }


def settle(values):
    return lax.optimization_barrier(values.astype(jnp.bfloat16))

def kernel_rows(rate_rows, residue_rows, length):
    positions = jnp.arange(length).astype(jnp.float32)

    def add_pole(pole_index, running):
        decay = lax.dynamic_slice_in_dim(rate_rows, pole_index, 1, 1)
        weight_col = lax.dynamic_slice_in_dim(residue_rows, pole_index, 1, 1)
        return running + weight_col * jnp.sqrt(2.0 * decay) * jnp.exp(-decay * positions[None, :])
    start_rows = jnp.zeros((rate_rows.shape[0], length), jnp.float32)
    return lax.fori_loop(0, rate_rows.shape[1], add_pole, start_rows)

def reference(tokens, norm_gain, in_weight, short_filter, rates, residues, skip):
    block = min(C, 256)

    def one_sequence(token_rows):
        values = token_rows.astype(jnp.float32)
        inv_rms = lax.rsqrt(lax.optimization_barrier(jnp.mean(values * values, axis=1, keepdims=True)) + 1e-06)
        normed = (values * inv_rms * norm_gain[None, :]).astype(jnp.bfloat16)
        projected = jnp.dot(normed, in_weight, preferred_element_type=jnp.float32).astype(jnp.bfloat16)
        padded = jnp.pad(projected.astype(jnp.float32), ((2, 0), (0, 0)))
        featured = short_filter[0][None, :] * padded[2:] + short_filter[1][None, :] * padded[1:-1] + short_filter[2][None, :] * padded[:-2]
        queries = featured[:, :C]
        keys_part = featured[:, C:2 * C]
        values_part = featured[:, 2 * C:]
        carried = settle(keys_part * values_part).astype(jnp.float32)
        gate = settle(queries).astype(jnp.float32)
        signal = carried.T.reshape(C // block, block, LEN)
        rate_blocks = rates.reshape(C // block, block, POLES)
        residue_blocks = residues.reshape(C // block, block, POLES)

        def conv_block(items):
            sig_block, rate_rows, residue_rows = items
            kernel = kernel_rows(rate_rows, residue_rows, LEN)
            spectrum = jnp.fft.rfft(sig_block, n=2 * LEN, axis=1) * jnp.fft.rfft(kernel, n=2 * LEN, axis=1)
            return jnp.fft.irfft(spectrum, n=2 * LEN, axis=1)[:, :LEN].astype(jnp.float32)
        conv = lax.map(conv_block, (signal, rate_blocks, residue_blocks)).reshape(C, LEN)
        response = settle(conv + skip[:, None] * carried.T).astype(jnp.float32)
        return (gate.T * response).astype(jnp.bfloat16)
    return jnp.stack([one_sequence(tokens[seq_index]) for seq_index in range(SEQS)])
```

```python
import functools

import jax
import jax.numpy as jnp
from jax import lax
from jax.experimental import pallas as pl
from jax.experimental.pallas import tpu as pltpu
from jax.sharding import Mesh, PartitionSpec as P

F32 = jnp.float32
BF16 = jnp.bfloat16
NX, NY, NZ = 4, 4, 8
GROUPS = 16
POLES = 16
HERE = 128
CHUNK = 16
LANES = 128
CH = 512
HALO = 16
ROWS = HALO + NX * HERE
D = 2048
COLS = 3 * CH
VMEM_LIMIT = 50 * 1024 * 1024


def params(**kw):
    return pltpu.CompilerParams(vmem_limit_bytes=VMEM_LIMIT, **kw)


def norm_kernel(tok_ref, gain_ref, out_ref, scr):
    x = tok_ref[...].astype(F32)
    inv = lax.rsqrt(jnp.mean(x * x, axis=1, keepdims=True) + 1e-6)
    for k in range(D // LANES):
        lanes = slice(k * LANES, (k + 1) * LANES)
        scr[k] = x[:, lanes] * inv * gain_ref[:, lanes]
    for k in range(D // LANES):
        for j in range(0, CHUNK, 2):
            pair = [scr[k, pl.ds(j + i, 8, stride=CHUNK), :] for i in range(2)]
            out_ref[8 * j : 8 * j + 16, k * LANES : (k + 1) * LANES] = jnp.concatenate(
                pair, axis=0
            ).astype(BF16)


def normalise(tokens, gain):
    return pl.pallas_call(
        norm_kernel,
        out_shape=jax.ShapeDtypeStruct((HERE, D), BF16),
        scratch_shapes=[pltpu.VMEM((D // LANES, HERE, LANES), F32)],
        compiler_params=params(),
    )(tokens, gain)


def rounded(v):
    return v.astype(BF16).astype(F32)


def project_kernel(
    n0, n1, n2, n3, halo,
    w00, w01, w02, w03, w10, w11, w12, w13,
    taps, rates, residues, skip,
    gate_ref, local_ref, chunk_ref, state_ref,
    lhs, w, proj, decay_s, taps_s, carry, sems,
):
    x = lax.axis_index("x")
    z = lax.axis_index("z")
    y = lax.axis_index("yh") * 2 + lax.axis_index("yl")
    core = lax.axis_index("co")
    copies = []

    def copy(src, dst):
        c = pltpu.make_async_copy(src, dst, sems.at[len(copies)])
        c.start()
        copies.append(c)

    copy(halo, lhs.at[pl.ds(0, HALO)])
    for d, piece in enumerate((n0, n1, n2, n3)):
        row = pl.multiple_of(HALO + lax.rem(x + NX - d, NX) * HERE, 16)
        copy(piece, lhs.at[pl.ds(row, HERE)])
    for r, pieces in enumerate(((w00, w01, w02, w03), (w10, w11, w12, w13))):
        for e, piece in enumerate(pieces):
            yy = lax.rem(y + NY - e, NY)
            base = lax.rem(yy, 2) * 1024 + lax.rem(core + r, 2) * 512 + (yy // 2) * 32
            for d in range(NZ):
                row = pl.multiple_of(base + lax.rem(z + NZ - d, NZ) * 64, 32)
                copy(piece.at[d], w.at[pl.ds(row, 32)])

    rate = rates[...]
    weight = residues[...] * jnp.sqrt(2.0 * rate)
    decay = jnp.exp(-rate)
    decay_s[...] = decay
    power = weight
    for i in range(CHUNK):
        row = jnp.sum(power, axis=0, keepdims=True)
        taps_s[i : i + 1, :] = row + skip[...] if i == 0 else row
        power = power * decay

    for c in copies:
        c.wait()

    @pl.loop(0, COLS // 256)
    def _(n):
        cols = pl.ds(pl.multiple_of(n * 256, 256), 256)
        proj[:, cols] = rounded(jnp.dot(lhs[...], w[:, cols], preferred_element_type=F32))

    sub = lax.broadcasted_iota(jnp.int32, (8, LANES), 0)

    def down(v, by):
        return jnp.where(sub >= by, pltpu.roll(v, by, 0), 0.0)

    @pl.loop(0, CH // LANES)
    def _(l):
        lane0 = pl.multiple_of(l * LANES, LANES)
        here = pl.ds(lane0, LANES)
        carry[...] = jnp.zeros_like(carry)

        @pl.loop(0, NX)
        def _(p):
            row0 = pl.multiple_of(p * HERE, 16)

            def featured(s):
                lanes = pl.ds(pl.multiple_of(s * CH + lane0, LANES), LANES)
                before = [proj[pl.ds(row0 + 8 * i, 8), lanes] for i in range(2)]
                rows = [proj[pl.ds(row0 + HALO + 8 * j, 8), lanes] for j in range(CHUNK)]
                t = [taps[i : i + 1, lanes] for i in range(3)]
                prev = [
                    jnp.where(sub == 0, pltpu.roll(before[i], 1, 0), pltpu.roll(rows[14 + i], 1, 0))
                    for i in range(2)
                ]
                ext = prev + rows
                return [
                    t[0] * ext[j + 2] + t[1] * ext[j + 1] + t[2] * ext[j] for j in range(CHUNK)
                ]

            queries = featured(0)
            for j in range(0, CHUNK, 2):
                gate_ref[pl.ds(pl.multiple_of(row0 + 8 * j, 16), 16), here] = jnp.concatenate(
                    queries[j : j + 2], axis=0
                ).astype(BF16)
            keys, values = featured(1), featured(2)
            carried = [rounded(a * b) for a, b in zip(keys, values)]

            k = [taps_s[i : i + 1, here] for i in range(CHUNK)]
            for j in range(CHUNK):
                acc = k[0] * carried[j]
                for i in range(j):
                    acc = acc + k[j - i] * carried[i]
                local_ref[pl.ds(row0 + 8 * j, 8), here] = acc

            for m in range(POLES):
                e = decay_s[m : m + 1, here]
                s = carried[0]
                for j in range(1, CHUNK):
                    s = s * e + carried[j]
                a1 = jnp.exp(-float(CHUNK) * rates[m : m + 1, here])
                a2 = a1 * a1
                a4 = a2 * a2
                s = s + a1 * down(s, 1)
                s = s + a2 * down(s, 2)
                s = s + a4 * down(s, 4)
                start = carry[m]
                s = s + jnp.exp(
                    -float(CHUNK) * rates[m : m + 1, here] * (sub + 1).astype(F32)
                ) * start
                chunk_ref[m, pl.ds(pl.multiple_of(p * 8, 8), 8), here] = jnp.where(
                    sub == 0, start, pltpu.roll(s, 1, 0)
                )
                carry[m] = jnp.broadcast_to(s[7:8, :], (8, LANES))

        for m in range(POLES):
            state_ref[m : m + 1, here] = carry[m, 0:1, :]


def project(normed, halo, weights, taps, rates, residues, skip):
    any_spec = pl.BlockSpec(memory_space=pl.ANY)
    vmem = pl.BlockSpec(memory_space=pltpu.VMEM)
    return pl.pallas_call(
        project_kernel,
        in_specs=[any_spec] * 13 + [vmem] * 4,
        out_specs=[vmem] * 4,
        out_shape=[
            jax.ShapeDtypeStruct((NX * HERE, CH), BF16),
            jax.ShapeDtypeStruct((NX * HERE, CH), F32),
            jax.ShapeDtypeStruct((POLES, NX * HERE // CHUNK, CH), F32),
            jax.ShapeDtypeStruct((POLES, CH), F32),
        ],
        scratch_shapes=[
            pltpu.VMEM((ROWS, D), BF16),
            pltpu.VMEM((D, COLS), BF16),
            pltpu.VMEM((ROWS, COLS), F32),
            pltpu.VMEM((POLES, CH), F32),
            pltpu.VMEM((CHUNK, CH), F32),
            pltpu.VMEM((POLES, 8, LANES), F32),
            pltpu.SemaphoreType.DMA((69,)),
        ],
        compiler_params=params(),
        cost_estimate=pl.CostEstimate(
            flops=2 * ROWS * D * COLS, bytes_accessed=12_000_000, transcendentals=0
        ),
    )(*normed, halo, *weights, taps, rates, residues, skip)


def finish_kernel(
    states, rates, residues, local, chunk, gate, o0, o1, o2, o3, scr, start_s, decay_s, weight_s
):
    x = lax.axis_index("x")
    g = lax.axis_index("z") * 2 + lax.axis_index("yh")
    rate = rates[...]
    span = jnp.exp(-float(NX * HERE) * rate)
    total = jnp.zeros((POLES, CH), F32)
    for i in range(GROUPS - 1):
        total = jnp.where(i < g, total * span + states[i], total)
    start_s[...] = total
    decay = jnp.exp(-rate)
    decay_s[...] = decay
    weight_s[...] = residues[...] * jnp.sqrt(2.0 * rate) * decay
    sub = lax.broadcasted_iota(jnp.int32, (8, LANES), 0)
    for d, out in enumerate((o0, o1, o2, o3)):
        p = lax.rem(x + d, NX)

        @pl.loop(0, CH // LANES)
        def _(l, p=p, out=out):
            here = pl.ds(pl.multiple_of(l * LANES, LANES), LANES)
            row0 = pl.multiple_of(p * HERE, 16)
            age = -float(CHUNK) * (p * 8 + sub).astype(F32)
            v, e = [], []
            for m in range(POLES):
                fade = jnp.exp(rates[m : m + 1, here] * age)
                at = chunk[m, pl.ds(pl.multiple_of(p * 8, 8), 8), here]
                v.append((at + fade * start_s[m : m + 1, here]) * weight_s[m : m + 1, here])
                e.append(decay_s[m : m + 1, here])
            for j in range(0, CHUNK, 2):
                gates = gate[pl.ds(pl.multiple_of(row0 + 8 * j, 16), 16), here].astype(F32)
                for i in range(2):
                    parts = list(v)
                    while len(parts) > 1:
                        parts = [a + b for a, b in zip(parts[::2], parts[1::2])]
                    response = rounded(local[pl.ds(row0 + 8 * (j + i), 8), here] + parts[0])
                    scr[pl.ds(j + i, 8, stride=CHUNK), :] = gates[8 * i : 8 * i + 8] * response
                    v = [a * b for a, b in zip(v, e)]
            out[here, :] = scr[...].T.astype(BF16)


def finish(states, rates, residues, local, chunk, gate):
    vmem = pl.BlockSpec(memory_space=pltpu.VMEM)
    return pl.pallas_call(
        finish_kernel,
        in_specs=[vmem] * 6,
        out_specs=[vmem] * NX,
        out_shape=[jax.ShapeDtypeStruct((CH, HERE), BF16)] * NX,
        scratch_shapes=[
            pltpu.VMEM((HERE, LANES), F32),
            pltpu.VMEM((POLES, CH), F32),
            pltpu.VMEM((POLES, CH), F32),
            pltpu.VMEM((POLES, CH), F32),
        ],
        compiler_params=params(),
    )(states, rates, residues, local, chunk, gate)


def place_kernel(p0, p1, p2, p3, out):
    x = lax.axis_index("x")
    for d, piece in enumerate((p0, p1, p2, p3)):
        at = lax.rem(x + NX - d, NX)
        for i in range(GROUPS):
            out[i, at] = piece[32 * i : 32 * i + 32, :]


def place(pieces):
    out = pl.pallas_call(
        place_kernel,
        out_shape=jax.ShapeDtypeStruct((GROUPS, NX, 32, HERE), BF16),
        compiler_params=params(),
    )(*pieces)
    return out.reshape(1, GROUPS * NX * 32, HERE)


def ring(size, by):
    return [(i, (i + by) % size) for i in range(size)]


def along_y(value, by):
    def flat(y):
        return (y % 2) * 2 + y // 2

    return lax.ppermute(value, ("yl", "yh"), [(flat(a), flat(b)) for a, b in ring(NY, by)])


def body(tokens, norm_gain, in_weight, short_filter, rates, residues, skip):
    x = lax.axis_index("x")
    own = normalise(tokens[0], norm_gain[None, :])
    others = {d: lax.ppermute(own, "x", ring(NX, d)) for d in (2, 1, 3)}
    normed = [own] + [others[d] for d in (1, 2, 3)]

    tails = jnp.stack([piece[HERE - HALO :] for piece in normed])
    tail = lax.dynamic_index_in_dim(tails, lax.rem(x + 1, NX), 0, keepdims=False)
    halo = lax.ppermute(tail, ("z", "yh"), [(i, i + 1) for i in range(GROUPS - 1)])

    blocks = in_weight.reshape(8, 3, GROUPS, NX, 32).transpose(3, 0, 1, 2, 4).reshape(NX, 8, COLS)
    unit = lax.all_to_all(blocks, "x", split_axis=0, concat_axis=0, tiled=True).reshape(32, COLS)
    along_z = {d: lax.ppermute(unit, "z", ring(NZ, d)) for d in (4, 3, 5, 2, 6, 1, 7)}
    plane = jnp.stack([unit] + [along_z[d] for d in range(1, NZ)])
    swap = [(0, 1), (1, 0)]
    planes = {0: plane}
    for e in (2, 1, 3):
        planes[e] = along_y(plane, e)
    sibling = {e: lax.ppermute(planes[e], "co", swap) for e in (0, 1, 3, 2)}
    weights = [planes[e] for e in range(NY)] + [sibling[e] for e in range(NY)]

    mine = jnp.concatenate(
        [
            rates.T.reshape(4, LANES),
            residues.T.reshape(4, LANES),
            jnp.pad(skip, (0, LANES - 32)).reshape(1, LANES),
        ]
    )
    table = lax.all_to_all(
        jnp.broadcast_to(mine[None], (GROUPS,) + mine.shape),
        ("z", "yh"),
        split_axis=0,
        concat_axis=0,
        tiled=True,
    )
    rate_table = table[:, 0:4].reshape(GROUPS, POLES, 32).transpose(1, 0, 2).reshape(POLES, CH)
    residue_table = table[:, 4:8].reshape(GROUPS, POLES, 32).transpose(1, 0, 2).reshape(POLES, CH)
    skip_row = table[:, 8, :32].reshape(1, CH)
    taps = short_filter.reshape(3, 3, GROUPS, NX, 32)
    taps = lax.dynamic_index_in_dim(taps, x, 3, keepdims=False).reshape(3, COLS)

    gate, local, chunk, state = project(
        normed, halo, weights, taps, rate_table, residue_table, skip_row
    )
    states = lax.all_to_all(
        jnp.broadcast_to(state[None], (GROUPS,) + state.shape),
        ("z", "yh"),
        split_axis=0,
        concat_axis=0,
        tiled=True,
    )
    pieces = finish(states, rate_table, residue_table, local, chunk, gate)
    arrived = {d: lax.ppermute(pieces[d], "x", ring(NX, d)) for d in (2, 1, 3)}
    return place([pieces[0]] + [arrived[d] for d in (1, 2, 3)])


def solution(mesh):
    fine = Mesh(mesh.devices.reshape(2, 2, NZ, 2, NX), ("yl", "co", "z", "yh", "x"))
    fsdp, ctx = ("yl", "co"), ("z", "yh", "x")
    in_specs = (
        P(fsdp, ctx, None),
        P(),
        P(fsdp + ctx, None),
        P(),
        P(ctx, None),
        P(ctx, None),
        P(ctx),
    )
    return jax.shard_map(
        body, mesh=fine, in_specs=in_specs, out_specs=P(fsdp, None, ctx), check_vma=False
    )
```

```python
import functools

import jax
import jax.numpy as jnp
from jax import lax
from jax.experimental import pallas as pl
from jax.experimental.pallas import tpu as pltpu
from jax.sharding import Mesh, PartitionSpec as P

F32 = jnp.float32
BF16 = jnp.bfloat16
NX, NZ = 4, 8
PIECES = 8
POLES = 16
HERE = 128
CHUNK = 16
LANES = 128
CH = 256
HALO = 16
SPAN = PIECES * HERE
ROWS = HALO + SPAN
D = 2048
COLS = 3 * CH
VMEM_LIMIT = 50 * 1024 * 1024


def params(**kw):
    return pltpu.CompilerParams(vmem_limit_bytes=VMEM_LIMIT, **kw)


def norm_kernel(tok_ref, gain_ref, out_ref, scr):
    x = tok_ref[...].astype(F32)
    inv = lax.rsqrt(jnp.mean(x * x, axis=1, keepdims=True) + 1e-6)
    for k in range(D // LANES):
        lanes = slice(k * LANES, (k + 1) * LANES)
        scr[k] = x[:, lanes] * inv * gain_ref[:, lanes]
    for k in range(D // LANES):
        for j in range(0, CHUNK, 2):
            pair = [scr[k, pl.ds(j + i, 8, stride=CHUNK), :] for i in range(2)]
            out_ref[8 * j : 8 * j + 16, k * LANES : (k + 1) * LANES] = jnp.concatenate(
                pair, axis=0
            ).astype(BF16)


def normalise(tokens, gain):
    return pl.pallas_call(
        norm_kernel,
        out_shape=jax.ShapeDtypeStruct((HERE, D), BF16),
        scratch_shapes=[pltpu.VMEM((D // LANES, HERE, LANES), F32)],
        compiler_params=params(),
    )(tokens, gain)


def rounded(v):
    return v.astype(BF16).astype(F32)


def project_kernel(
    a0, a1, a2, a3, b0, b1, b2, b3, halo, w00, w01, w10, w11,
    taps, rates, residues, skip,
    gate_ref, local_ref, chunk_ref, state_ref,
    lhs, w, proj, decay_s, taps_s, carry, sems,
):
    x = lax.axis_index("x")
    yh = lax.axis_index("yh")
    yl = lax.axis_index("yl")
    core = lax.axis_index("co")
    copies = []

    def copy(src, dst):
        c = pltpu.make_async_copy(src, dst, sems.at[len(copies)])
        c.start()
        copies.append(c)

    for r, pieces in enumerate(((w00, w01), (w10, w11))):
        for e, piece in enumerate(pieces):
            row = lax.rem(yl + e, 2) * 1024 + lax.rem(core + r, 2) * 512
            copy(piece, w.at[pl.ds(pl.multiple_of(row, 512), 512)])
    copy(halo, lhs.at[pl.ds(0, HALO)])
    for e, pieces in enumerate(((a0, a1, a2, a3), (b0, b1, b2, b3))):
        for d, piece in enumerate(pieces):
            at = lax.rem(yh + e, 2) * NX + lax.rem(x + NX - d, NX)
            copy(piece, lhs.at[pl.ds(pl.multiple_of(HALO + at * HERE, 16), HERE)])

    rate = rates[...]
    weight = residues[...] * jnp.sqrt(2.0 * rate)
    decay = jnp.exp(-rate)
    decay_s[...] = decay
    power = weight
    for i in range(CHUNK):
        row = jnp.sum(power, axis=0, keepdims=True)
        taps_s[i : i + 1, :] = row + skip[...] if i == 0 else row
        power = power * decay

    for c in copies:
        c.wait()

    @pl.loop(0, COLS // 256)
    def _(n):
        cols = pl.ds(pl.multiple_of(n * 256, 256), 256)
        proj[:, cols] = rounded(jnp.dot(lhs[...], w[:, cols], preferred_element_type=F32))

    sub = lax.broadcasted_iota(jnp.int32, (8, LANES), 0)

    def down(v, by):
        return jnp.where(sub >= by, pltpu.roll(v, by, 0), 0.0)

    @pl.loop(0, CH // LANES)
    def _(l):
        lane0 = pl.multiple_of(l * LANES, LANES)
        here = pl.ds(lane0, LANES)
        carry[...] = jnp.zeros_like(carry)

        @pl.loop(0, PIECES)
        def _(p):
            row0 = pl.multiple_of(p * HERE, 16)

            def featured(s):
                lanes = pl.ds(pl.multiple_of(s * CH + lane0, LANES), LANES)
                before = [proj[pl.ds(row0 + 8 * i, 8), lanes] for i in range(2)]
                rows = [proj[pl.ds(row0 + HALO + 8 * j, 8), lanes] for j in range(CHUNK)]
                t = [taps[i : i + 1, lanes] for i in range(3)]
                prev = [
                    jnp.where(sub == 0, pltpu.roll(before[i], 1, 0), pltpu.roll(rows[14 + i], 1, 0))
                    for i in range(2)
                ]
                ext = prev + rows
                return [
                    t[0] * ext[j + 2] + t[1] * ext[j + 1] + t[2] * ext[j] for j in range(CHUNK)
                ]

            queries = featured(0)
            for j in range(0, CHUNK, 2):
                gate_ref[pl.ds(pl.multiple_of(row0 + 8 * j, 16), 16), here] = jnp.concatenate(
                    queries[j : j + 2], axis=0
                ).astype(BF16)
            keys, values = featured(1), featured(2)
            carried = [rounded(a * b) for a, b in zip(keys, values)]

            k = [taps_s[i : i + 1, here] for i in range(CHUNK)]
            for j in range(CHUNK):
                acc = k[0] * carried[j]
                for i in range(j):
                    acc = acc + k[j - i] * carried[i]
                local_ref[pl.ds(row0 + 8 * j, 8), here] = acc

            for m in range(POLES):
                e = decay_s[m : m + 1, here]
                s = carried[0]
                for j in range(1, CHUNK):
                    s = s * e + carried[j]
                a1 = jnp.exp(-float(CHUNK) * rates[m : m + 1, here])
                a2 = a1 * a1
                a4 = a2 * a2
                s = s + a1 * down(s, 1)
                s = s + a2 * down(s, 2)
                s = s + a4 * down(s, 4)
                start = carry[m]
                s = s + jnp.exp(
                    -float(CHUNK) * rates[m : m + 1, here] * (sub + 1).astype(F32)
                ) * start
                chunk_ref[m, pl.ds(pl.multiple_of(p * 8, 8), 8), here] = jnp.where(
                    sub == 0, start, pltpu.roll(s, 1, 0)
                )
                carry[m] = jnp.broadcast_to(s[7:8, :], (8, LANES))

        for m in range(POLES):
            state_ref[m : m + 1, here] = carry[m, 0:1, :]


def project(normed, halo, weights, taps, rates, residues, skip):
    any_spec = pl.BlockSpec(memory_space=pl.ANY)
    vmem = pl.BlockSpec(memory_space=pltpu.VMEM)
    return pl.pallas_call(
        project_kernel,
        in_specs=[any_spec] * 13 + [vmem] * 4,
        out_specs=[vmem] * 4,
        out_shape=[
            jax.ShapeDtypeStruct((SPAN, CH), BF16),
            jax.ShapeDtypeStruct((SPAN, CH), F32),
            jax.ShapeDtypeStruct((POLES, SPAN // CHUNK, CH), F32),
            jax.ShapeDtypeStruct((POLES, CH), F32),
        ],
        scratch_shapes=[
            pltpu.VMEM((ROWS, D), BF16),
            pltpu.VMEM((D, COLS), BF16),
            pltpu.VMEM((ROWS, COLS), F32),
            pltpu.VMEM((POLES, CH), F32),
            pltpu.VMEM((CHUNK, CH), F32),
            pltpu.VMEM((POLES, 8, LANES), F32),
            pltpu.SemaphoreType.DMA((13,)),
        ],
        compiler_params=params(),
        cost_estimate=pl.CostEstimate(
            flops=2 * ROWS * D * COLS, bytes_accessed=12_000_000, transcendentals=0
        ),
    )(*normed, halo, *weights, taps, rates, residues, skip)


def finish_kernel(
    states, rates, residues, local, chunk, gate, out, scr, start_s, decay_s, weight_s
):
    z = lax.axis_index("z")
    rate = rates[...]
    span = jnp.exp(-float(SPAN) * rate)
    total = jnp.zeros((POLES, CH), F32)
    for i in range(NZ - 1):
        total = jnp.where(i < z, total * span + states[i], total)
    start_s[...] = total
    decay = jnp.exp(-rate)
    decay_s[...] = decay
    weight_s[...] = residues[...] * jnp.sqrt(2.0 * rate) * decay
    sub = lax.broadcasted_iota(jnp.int32, (8, LANES), 0)

    @pl.loop(0, PIECES)
    def _(p):
        @pl.loop(0, CH // LANES)
        def _(l):
            here = pl.ds(pl.multiple_of(l * LANES, LANES), LANES)
            row0 = pl.multiple_of(p * HERE, 16)
            age = -float(CHUNK) * (p * 8 + sub).astype(F32)
            v, e = [], []
            for m in range(POLES):
                fade = jnp.exp(rates[m : m + 1, here] * age)
                at = chunk[m, pl.ds(pl.multiple_of(p * 8, 8), 8), here]
                v.append((at + fade * start_s[m : m + 1, here]) * weight_s[m : m + 1, here])
                e.append(decay_s[m : m + 1, here])
            for j in range(0, CHUNK, 2):
                gates = gate[pl.ds(pl.multiple_of(row0 + 8 * j, 16), 16), here].astype(F32)
                for i in range(2):
                    parts = list(v)
                    while len(parts) > 1:
                        parts = [a + b for a, b in zip(parts[::2], parts[1::2])]
                    response = rounded(local[pl.ds(row0 + 8 * (j + i), 8), here] + parts[0])
                    scr[pl.ds(j + i, 8, stride=CHUNK), :] = gates[8 * i : 8 * i + 8] * response
                    v = [a * b for a, b in zip(v, e)]
            out[p, here, :] = scr[...].T.astype(BF16)


def finish(states, rates, residues, local, chunk, gate):
    vmem = pl.BlockSpec(memory_space=pltpu.VMEM)
    return pl.pallas_call(
        finish_kernel,
        in_specs=[vmem] * 6,
        out_specs=vmem,
        out_shape=jax.ShapeDtypeStruct((PIECES, CH, HERE), BF16),
        scratch_shapes=[
            pltpu.VMEM((HERE, LANES), F32),
            pltpu.VMEM((POLES, CH), F32),
            pltpu.VMEM((POLES, CH), F32),
            pltpu.VMEM((POLES, CH), F32),
        ],
        compiler_params=params(),
    )(states, rates, residues, local, chunk, gate)


def place_kernel(pieces, out):
    for g in range(PIECES):
        for i in range(NZ):
            out[i, g] = pieces[g, 32 * i : 32 * i + 32, :]


def place(pieces):
    out = pl.pallas_call(
        place_kernel,
        out_shape=jax.ShapeDtypeStruct((NZ, PIECES, 32, HERE), BF16),
        compiler_params=params(),
    )(pieces)
    return out.reshape(1, NZ * PIECES * 32, HERE)


def ring(size, by):
    return [(i, (i + by) % size) for i in range(size)]


def along_x(value):
    got = {d: lax.ppermute(value, "x", ring(NX, d)) for d in (2, 1, 3)}
    return [value] + [got[d] for d in (1, 2, 3)]


def spread(value):
    return jnp.broadcast_to(value[None], (NZ,) + value.shape)


def swap(value, axes):
    return lax.all_to_all(value, axes, split_axis=0, concat_axis=0, tiled=True)


def body(tokens, norm_gain, in_weight, short_filter, rates, residues, skip):
    x, yh = lax.axis_index("x"), lax.axis_index("yh")
    own = normalise(tokens[0], norm_gain[None, :])
    own_row = along_x(own)
    partner = lax.ppermute(own, "yh", ring(2, 1))

    blocks = in_weight.reshape(8, 3, NZ, PIECES, 32).transpose(3, 0, 1, 2, 4)
    blocks = spread(blocks.reshape(PIECES, 8, COLS)).reshape(NZ * PIECES, 8, COLS)
    plane = swap(blocks, ("z", "yh", "x")).reshape(512, COLS)
    partner, plane = lax.optimization_barrier((partner, plane))

    other_plane = lax.ppermute(plane, "yl", ring(2, 1))
    partner_row = along_x(partner)
    sibling = lax.ppermute(plane, "co", ring(2, 1))
    other_sibling = lax.ppermute(other_plane, "co", ring(2, 1))
    weights = [plane, other_plane, sibling, other_sibling]
    normed = own_row + partner_row

    tails = jnp.stack([piece[HERE - HALO :] for piece in normed])
    last = (1 - yh) * NX + lax.rem(x + 1, NX)
    tail = lax.dynamic_index_in_dim(tails, last, 0, keepdims=False)
    halo = lax.ppermute(tail, "z", [(i, i + 1) for i in range(NZ - 1)])

    rates, residues, skip, plane = lax.optimization_barrier((rates, residues, skip, plane))
    mine = jnp.concatenate(
        [
            rates.T.reshape(4, LANES),
            residues.T.reshape(4, LANES),
            jnp.pad(skip, (0, LANES - 32)).reshape(1, LANES),
        ]
    )
    table = swap(spread(mine), "z")
    rate_table = table[:, 0:4].reshape(NZ, POLES, 32).transpose(1, 0, 2).reshape(POLES, CH)
    residue_table = table[:, 4:8].reshape(NZ, POLES, 32).transpose(1, 0, 2).reshape(POLES, CH)
    skip_row = table[:, 8, :32].reshape(1, CH)
    taps = short_filter.reshape(3, 3, NZ, PIECES, 32)
    taps = lax.dynamic_index_in_dim(taps, yh * NX + x, 3, keepdims=False).reshape(3, COLS)

    gate, local, chunk, state = project(
        normed, halo, weights, taps, rate_table, residue_table, skip_row
    )
    states = swap(spread(state), "z")
    pieces = finish(states, rate_table, residue_table, local, chunk, gate)
    return place(swap(pieces, ("yh", "x")))


def solution(mesh):
    fine = Mesh(mesh.devices.reshape(2, 2, NZ, 2, NX), ("yl", "co", "z", "yh", "x"))
    fsdp, ctx = ("yl", "co"), ("z", "yh", "x")
    in_specs = (
        P(fsdp, ctx, None),
        P(),
        P(fsdp + ctx, None),
        P(),
        P(ctx, None),
        P(ctx, None),
        P(ctx),
    )
    return jax.shard_map(
        body, mesh=fine, in_specs=in_specs, out_specs=P(fsdp, None, ctx), check_vma=False
    )
```

```python
import functools

import jax
import jax.numpy as jnp
from jax import lax
from jax.experimental import pallas as pl
from jax.experimental.pallas import tpu as pltpu
from jax.sharding import Mesh, PartitionSpec as P

F32 = jnp.float32
BF16 = jnp.bfloat16
NX, NZ = 4, 8
PIECES = 8
POLES = 16
HERE = 128
CHUNK = 16
LANES = 128
CH = 256
HALO = 16
SPAN = PIECES * HERE
ROWS = HALO + SPAN
D = 2048
COLS = 3 * CH
MIB = 1024 * 1024


def params(mib):
    return pltpu.CompilerParams(vmem_limit_bytes=mib * MIB)


def norm_kernel(tok_ref, gain_ref, out_ref, scr):
    x = tok_ref[...].astype(F32)
    inv = lax.rsqrt(jnp.mean(x * x, axis=1, keepdims=True) + 1e-6)
    for k in range(D // LANES):
        lanes = slice(k * LANES, (k + 1) * LANES)
        scr[k] = x[:, lanes] * inv * gain_ref[:, lanes]
    for k in range(D // LANES):
        for j in range(0, CHUNK, 2):
            pair = [scr[k, pl.ds(j + i, 8, stride=CHUNK), :] for i in range(2)]
            out_ref[8 * j : 8 * j + 16, k * LANES : (k + 1) * LANES] = jnp.concatenate(
                pair, axis=0
            ).astype(BF16)


def normalise(tokens, gain):
    return pl.pallas_call(
        norm_kernel,
        out_shape=jax.ShapeDtypeStruct((HERE, D), BF16),
        scratch_shapes=[pltpu.VMEM((D // LANES, HERE, LANES), F32)],
        compiler_params=params(10),
    )(tokens, gain)


def rounded(v):
    return v.astype(BF16).astype(F32)


def filtered(ext, t, sub):
    prev = [
        jnp.where(sub == 0, pltpu.roll(ext[i], 1, 0), pltpu.roll(ext[CHUNK + i], 1, 0))
        for i in range(2)
    ]
    ext = prev + ext[2:]
    return [t[0] * ext[j + 2] + t[1] * ext[j + 1] + t[2] * ext[j] for j in range(CHUNK)]


def project_kernel(
    a0, a1, a2, a3, b0, b1, b2, b3, halo, w00, w01, w10, w11,
    taps, rates,
    query_ref, carried_ref, chunk_ref, state_ref,
    lhs, w, proj, decay_s, carry, sems,
):
    x = lax.axis_index("x")
    yh = lax.axis_index("yh")
    yl = lax.axis_index("yl")
    core = lax.axis_index("co")
    copies = []

    def copy(src, dst):
        c = pltpu.make_async_copy(src, dst, sems.at[len(copies)])
        c.start()
        copies.append(c)

    for r, pieces in enumerate(((w00, w01), (w10, w11))):
        for e, piece in enumerate(pieces):
            row = lax.rem(yl + e, 2) * 1024 + lax.rem(core + r, 2) * 512
            copy(piece, w.at[pl.ds(pl.multiple_of(row, 512), 512)])
    copy(halo, lhs.at[pl.ds(0, HALO)])
    for e, pieces in enumerate(((a0, a1, a2, a3), (b0, b1, b2, b3))):
        for d, piece in enumerate(pieces):
            at = lax.rem(yh + e, 2) * NX + lax.rem(x + NX - d, NX)
            copy(piece, lhs.at[pl.ds(pl.multiple_of(HALO + at * HERE, 16), HERE)])

    decay_s[...] = jnp.exp(-rates[...])
    for c in copies:
        c.wait()

    for s in (1, 2, 0):
        cols = slice(s * CH, (s + 1) * CH)
        product = jnp.dot(lhs[...], w[:, cols], preferred_element_type=F32).astype(BF16)
        if s == 0:
            query_ref[...] = product
        else:
            proj[:, (s - 1) * CH : s * CH] = product.astype(F32)

    sub = lax.broadcasted_iota(jnp.int32, (8, LANES), 0)

    def down(v, by):
        return jnp.where(sub >= by, pltpu.roll(v, by, 0), 0.0)

    @pl.loop(0, CH // LANES)
    def _(l):
        lane0 = pl.multiple_of(l * LANES, LANES)
        here = pl.ds(lane0, LANES)
        carry[...] = jnp.zeros_like(carry)

        @pl.loop(0, PIECES)
        def _(p):
            row0 = pl.multiple_of(p * HERE, 16)

            def featured(s):
                lanes = pl.ds(pl.multiple_of(s * CH + lane0, LANES), LANES)
                first = pl.ds(pl.multiple_of((s + 1) * CH + lane0, LANES), LANES)
                ext = [proj[pl.ds(row0 + 8 * i, 8), lanes] for i in range(2 + CHUNK)]
                return filtered(ext, [taps[i : i + 1, first] for i in range(3)], sub)

            keys, values = featured(0), featured(1)
            pairs = [(a * b).astype(BF16) for a, b in zip(keys, values)]
            for j in range(0, CHUNK, 2):
                carried_ref[pl.ds(pl.multiple_of(row0 + 8 * j, 16), 16), here] = jnp.concatenate(
                    pairs[j : j + 2], axis=0
                )
            carried = [a.astype(F32) for a in pairs]

            for m in range(POLES):
                e = decay_s[m : m + 1, here]
                s = carried[0]
                for j in range(1, CHUNK):
                    s = s * e + carried[j]
                a1 = jnp.exp(-float(CHUNK) * rates[m : m + 1, here])
                a2 = a1 * a1
                a4 = a2 * a2
                s = s + a1 * down(s, 1)
                s = s + a2 * down(s, 2)
                s = s + a4 * down(s, 4)
                start = carry[m]
                s = s + jnp.exp(
                    -float(CHUNK) * rates[m : m + 1, here] * (sub + 1).astype(F32)
                ) * start
                chunk_ref[m, pl.ds(pl.multiple_of(p * 8, 8), 8), here] = jnp.where(
                    sub == 0, start, pltpu.roll(s, 1, 0)
                )
                carry[m] = jnp.broadcast_to(s[7:8, :], (8, LANES))

        for m in range(POLES):
            state_ref[m : m + 1, here] = carry[m, 0:1, :]


def project(normed, halo, weights, taps, rates):
    any_spec = pl.BlockSpec(memory_space=pl.ANY)
    vmem = pl.BlockSpec(memory_space=pltpu.VMEM)
    return pl.pallas_call(
        project_kernel,
        in_specs=[any_spec] * 13 + [vmem] * 2,
        out_specs=[vmem] * 4,
        out_shape=[
            jax.ShapeDtypeStruct((ROWS, CH), BF16),
            jax.ShapeDtypeStruct((SPAN, CH), BF16),
            jax.ShapeDtypeStruct((POLES, SPAN // CHUNK, CH), F32),
            jax.ShapeDtypeStruct((POLES, CH), F32),
        ],
        scratch_shapes=[
            pltpu.VMEM((ROWS, D), BF16),
            pltpu.VMEM((D, COLS), BF16),
            pltpu.VMEM((ROWS, 2 * CH), F32),
            pltpu.VMEM((POLES, CH), F32),
            pltpu.VMEM((POLES, 8, LANES), F32),
            pltpu.SemaphoreType.DMA((13,)),
        ],
        compiler_params=params(28),
        cost_estimate=pl.CostEstimate(
            flops=2 * ROWS * D * COLS, bytes_accessed=10_000_000, transcendentals=0
        ),
    )(*normed, halo, *weights, taps, rates)


def direct_kernel(query, carried, taps, rates, residues, skip, gate_ref, local_ref, taps_s):
    decay = jnp.exp(-rates[...])
    power = residues[...] * jnp.sqrt(2.0 * rates[...])
    for i in range(CHUNK):
        row = jnp.sum(power, axis=0, keepdims=True)
        taps_s[i : i + 1, :] = row + skip[...] if i == 0 else row
        power = power * decay
    sub = lax.broadcasted_iota(jnp.int32, (8, LANES), 0)

    @pl.loop(0, CH // LANES)
    def _(l):
        here = pl.ds(pl.multiple_of(l * LANES, LANES), LANES)

        @pl.loop(0, PIECES)
        def _(p):
            row0 = pl.multiple_of(p * HERE, 16)

            def rows(ref, count):
                pairs = [
                    ref[pl.ds(pl.multiple_of(row0 + 16 * i, 16), 16), here].astype(F32)
                    for i in range(count)
                ]
                return [half for pair in pairs for half in (pair[:8], pair[8:])]

            t = [taps[i : i + 1, here] for i in range(3)]
            queries = filtered(rows(query, 9), t, sub)
            for j in range(0, CHUNK, 2):
                gate_ref[pl.ds(pl.multiple_of(row0 + 8 * j, 16), 16), here] = jnp.concatenate(
                    queries[j : j + 2], axis=0
                ).astype(BF16)
            x = rows(carried, 8)
            k = [taps_s[i : i + 1, here] for i in range(CHUNK)]
            for j in range(CHUNK):
                acc = k[0] * x[j]
                for i in range(j):
                    acc = acc + k[j - i] * x[i]
                local_ref[pl.ds(row0 + 8 * j, 8), here] = acc


def direct(query, carried, taps, rates, residues, skip):
    vmem = pl.BlockSpec(memory_space=pltpu.VMEM)
    return pl.pallas_call(
        direct_kernel,
        in_specs=[vmem] * 6,
        out_specs=[vmem] * 2,
        out_shape=[
            jax.ShapeDtypeStruct((SPAN, CH), BF16),
            jax.ShapeDtypeStruct((SPAN, CH), F32),
        ],
        scratch_shapes=[pltpu.VMEM((CHUNK, CH), F32)],
        compiler_params=params(10),
        cost_estimate=pl.CostEstimate(
            flops=40 * SPAN * CH, bytes_accessed=3_000_000, transcendentals=0
        ),
    )(query, carried, taps, rates, residues, skip)


def finish_kernel(
    states, rates, residues, local, chunk, gate, out, scr, start_s, decay_s, weight_s
):
    z = lax.axis_index("z")
    rate = rates[...]
    span = jnp.exp(-float(SPAN) * rate)
    total = jnp.zeros((POLES, CH), F32)
    for i in range(NZ - 1):
        total = jnp.where(i < z, total * span + states[i], total)
    start_s[...] = total
    decay = jnp.exp(-rate)
    decay_s[...] = decay
    weight_s[...] = residues[...] * jnp.sqrt(2.0 * rate) * decay
    sub = lax.broadcasted_iota(jnp.int32, (8, LANES), 0)

    @pl.loop(0, PIECES)
    def _(p):
        @pl.loop(0, CH // LANES)
        def _(l):
            here = pl.ds(pl.multiple_of(l * LANES, LANES), LANES)
            row0 = pl.multiple_of(p * HERE, 16)
            age = -float(CHUNK) * (p * 8 + sub).astype(F32)
            v, e = [], []
            for m in range(POLES):
                fade = jnp.exp(rates[m : m + 1, here] * age)
                at = chunk[m, pl.ds(pl.multiple_of(p * 8, 8), 8), here]
                v.append((at + fade * start_s[m : m + 1, here]) * weight_s[m : m + 1, here])
                e.append(decay_s[m : m + 1, here])
            for j in range(0, CHUNK, 2):
                gates = gate[pl.ds(pl.multiple_of(row0 + 8 * j, 16), 16), here].astype(F32)
                for i in range(2):
                    parts = list(v)
                    while len(parts) > 1:
                        parts = [a + b for a, b in zip(parts[::2], parts[1::2])]
                    response = rounded(local[pl.ds(row0 + 8 * (j + i), 8), here] + parts[0])
                    scr[pl.ds(j + i, 8, stride=CHUNK), :] = gates[8 * i : 8 * i + 8] * response
                    v = [a * b for a, b in zip(v, e)]
            out[p, here, :] = scr[...].T.astype(BF16)


def finish(states, rates, residues, local, chunk, gate):
    vmem = pl.BlockSpec(memory_space=pltpu.VMEM)
    return pl.pallas_call(
        finish_kernel,
        in_specs=[vmem] * 6,
        out_specs=vmem,
        out_shape=jax.ShapeDtypeStruct((PIECES, CH, HERE), BF16),
        scratch_shapes=[
            pltpu.VMEM((HERE, LANES), F32),
            pltpu.VMEM((POLES, CH), F32),
            pltpu.VMEM((POLES, CH), F32),
            pltpu.VMEM((POLES, CH), F32),
        ],
        compiler_params=params(10),
    )(states, rates, residues, local, chunk, gate)


def place_kernel(pieces, out):
    for g in range(PIECES):
        for i in range(NZ):
            out[i, g] = pieces[g, 32 * i : 32 * i + 32, :]


def place(pieces):
    out = pl.pallas_call(
        place_kernel,
        out_shape=jax.ShapeDtypeStruct((NZ, PIECES, 32, HERE), BF16),
        compiler_params=params(10),
    )(pieces)
    return out.reshape(1, NZ * PIECES * 32, HERE)


def ring(size, by):
    return [(i, (i + by) % size) for i in range(size)]


def along_x(value):
    got = {d: lax.ppermute(value, "x", ring(NX, d)) for d in (2, 1, 3)}
    return [value] + [got[d] for d in (1, 2, 3)]


def spread(value):
    return jnp.broadcast_to(value[None], (NZ,) + value.shape)


def swap(value, axes):
    return lax.all_to_all(value, axes, split_axis=0, concat_axis=0, tiled=True)


def tail_kernel(a0, a1, a2, a3, out, sem):
    which = lax.rem(lax.axis_index("x") + 1, NX)
    for d, piece in enumerate((a0, a1, a2, a3)):

        @pl.when(which == d)
        def _(piece=piece):
            copy = pltpu.make_async_copy(piece.at[pl.ds(HERE - HALO, HALO)], out, sem)
            copy.start()
            copy.wait()


def last_rows(row):
    any_spec = pl.BlockSpec(memory_space=pl.ANY)
    return pl.pallas_call(
        tail_kernel,
        in_specs=[any_spec] * NX,
        out_specs=any_spec,
        out_shape=jax.ShapeDtypeStruct((HALO, D), BF16),
        scratch_shapes=[pltpu.SemaphoreType.DMA],
        compiler_params=params(10),
    )(*row)


def body(tokens, norm_gain, in_weight, short_filter, rates, residues, skip):
    x, yh = lax.axis_index("x"), lax.axis_index("yh")
    own = normalise(tokens[0], norm_gain[None, :])
    partner = lax.ppermute(own, "yh", ring(2, 1))
    own_row = along_x(own)

    blocks = in_weight.reshape(8, 3, NZ, PIECES, 32).transpose(3, 0, 1, 2, 4)
    blocks = spread(blocks.reshape(PIECES, 8, COLS)).reshape(NZ * PIECES, 8, COLS)
    plane = swap(blocks, ("z", "yh", "x")).reshape(512, COLS)

    other_plane = lax.ppermute(plane, "yl", ring(2, 1))
    partner_row = along_x(partner)
    sibling = lax.ppermute(plane, "co", ring(2, 1))
    other_sibling = lax.ppermute(other_plane, "co", ring(2, 1))
    weights = [plane, other_plane, sibling, other_sibling]

    tail = last_rows(own_row)
    halo = 0
    for to in range(2):
        pairs = [(2 * z + 1, 2 * z + 2 + to) for z in range(NZ - 1)]
        halo = halo + lax.ppermute(tail, ("z", "yh"), pairs)

    rates, residues, skip, _ = lax.optimization_barrier((rates, residues, skip, plane))
    mine = jnp.concatenate(
        [
            rates.T.reshape(4, LANES),
            residues.T.reshape(4, LANES),
            jnp.pad(skip, (0, LANES - 32)).reshape(1, LANES),
        ]
    )
    table = swap(spread(mine), "z")
    rate_table = table[:, 0:4].reshape(NZ, POLES, 32).transpose(1, 0, 2).reshape(POLES, CH)
    residue_table = table[:, 4:8].reshape(NZ, POLES, 32).transpose(1, 0, 2).reshape(POLES, CH)
    skip_row = table[:, 8, :32].reshape(1, CH)
    taps = short_filter.reshape(3, 3, NZ, PIECES, 32)
    taps = lax.dynamic_index_in_dim(taps, yh * NX + x, 3, keepdims=False).reshape(3, COLS)

    query, carried, chunk, state = project(own_row + partner_row, halo, weights, taps, rate_table)
    states = swap(spread(state), "z")
    gate, local = direct(query, carried, taps, rate_table, residue_table, skip_row)
    pieces = finish(states, rate_table, residue_table, local, chunk, gate)
    return place(swap(pieces, ("yh", "x")))


def solution(mesh):
    fine = Mesh(mesh.devices.reshape(2, 2, NZ, 2, NX), ("yl", "co", "z", "yh", "x"))
    fsdp, ctx = ("yl", "co"), ("z", "yh", "x")
    in_specs = (
        P(fsdp, ctx, None),
        P(),
        P(fsdp + ctx, None),
        P(),
        P(ctx, None),
        P(ctx, None),
        P(ctx),
    )
    return jax.shard_map(
        body, mesh=fine, in_specs=in_specs, out_specs=P(fsdp, None, ctx), check_vma=False
    )
```

```python
import functools

import jax
import jax.numpy as jnp
from jax import lax
from jax.experimental import pallas as pl
from jax.experimental.pallas import tpu as pltpu
from jax.sharding import Mesh, PartitionSpec as P

F32 = jnp.float32
BF16 = jnp.bfloat16
NX, NZ = 4, 8
PIECES = 8
POLES = 16
HERE = 128
CHUNK = 16
LANES = 128
CH = 256
HALO = 16
SPAN = PIECES * HERE
ROWS = HALO + SPAN
D = 2048
COLS = 3 * CH
WIDE = 2 * CH
MIB = 1024 * 1024


def params(mib):
    return pltpu.CompilerParams(vmem_limit_bytes=mib * MIB)


def norm_kernel(tok_ref, gain_ref, out_ref, scr):
    x = tok_ref[...].astype(F32)
    inv = lax.rsqrt(jnp.mean(x * x, axis=1, keepdims=True) + 1e-6)
    for k in range(D // LANES):
        lanes = slice(k * LANES, (k + 1) * LANES)
        scr[k] = x[:, lanes] * inv * gain_ref[:, lanes]
    for k in range(D // LANES):
        for j in range(0, CHUNK, 2):
            pair = [scr[k, pl.ds(j + i, 8, stride=CHUNK), :] for i in range(2)]
            out_ref[8 * j : 8 * j + 16, k * LANES : (k + 1) * LANES] = jnp.concatenate(
                pair, axis=0
            ).astype(BF16)


def normalise(tokens, gain):
    return pl.pallas_call(
        norm_kernel,
        out_shape=jax.ShapeDtypeStruct((HERE, D), BF16),
        scratch_shapes=[pltpu.VMEM((D // LANES, HERE, LANES), F32)],
        compiler_params=params(10),
    )(tokens, gain)


def rounded(v):
    return v.astype(BF16).astype(F32)


def filtered(ext, t, sub):
    prev = [
        jnp.where(sub == 0, pltpu.roll(ext[i], 1, 0), pltpu.roll(ext[CHUNK + i], 1, 0))
        for i in range(2)
    ]
    ext = prev + ext[2:]
    return [t[0] * ext[j + 2] + t[1] * ext[j + 1] + t[2] * ext[j] for j in range(CHUNK)]


def copier(sems):
    copies = []

    def copy(src, dst):
        c = pltpu.make_async_copy(src, dst, sems.at[len(copies)])
        c.start()
        copies.append(c)

    return copies, copy


def copy_rows(copy, pieces, halo, lhs):
    x, yh = lax.axis_index("x"), lax.axis_index("yh")
    copy(halo, lhs.at[pl.ds(0, HALO)])
    for i, piece in enumerate(pieces):
        at = lax.rem(yh + i // NX, 2) * NX + lax.rem(x + NX - i % NX, NX)
        copy(piece, lhs.at[pl.ds(pl.multiple_of(HALO + at * HERE, 16), HERE)])


def project_kernel(
    a0, a1, a2, a3, b0, b1, b2, b3, halo, w00, w01, w10, w11, taps, rates,
    carried_ref, chunk_ref, state_ref,
    lhs, w, proj, decay_s, carry, sems,
):
    yl, core = lax.axis_index("yl"), lax.axis_index("co")
    copies, copy = copier(sems)
    for r, pieces in enumerate(((w00, w01), (w10, w11))):
        for e, piece in enumerate(pieces):
            row = lax.rem(yl + e, 2) * 1024 + lax.rem(core + r, 2) * 512
            copy(piece, w.at[pl.ds(pl.multiple_of(row, 512), 512)])
    copy_rows(copy, (a0, a1, a2, a3, b0, b1, b2, b3), halo, lhs)

    decay_s[...] = jnp.exp(-rates[...])
    for c in copies:
        c.wait()

    for s in range(2):
        cols = slice(s * CH, (s + 1) * CH)
        product = jnp.dot(lhs[...], w[:, cols], preferred_element_type=F32)
        proj[:, cols] = rounded(product)

    sub = lax.broadcasted_iota(jnp.int32, (8, LANES), 0)

    def down(v, by):
        return jnp.where(sub >= by, pltpu.roll(v, by, 0), 0.0)

    @pl.loop(0, CH // LANES)
    def _(l):
        lane0 = pl.multiple_of(l * LANES, LANES)
        here = pl.ds(lane0, LANES)
        carry[...] = jnp.zeros_like(carry)

        @pl.loop(0, PIECES)
        def _(p):
            row0 = pl.multiple_of(p * HERE, 16)

            def featured(s):
                lanes = pl.ds(pl.multiple_of(s * CH + lane0, LANES), LANES)
                first = pl.ds(pl.multiple_of((s + 1) * CH + lane0, LANES), LANES)
                ext = [proj[pl.ds(row0 + 8 * i, 8), lanes] for i in range(2 + CHUNK)]
                return filtered(ext, [taps[i : i + 1, first] for i in range(3)], sub)

            keys, values = featured(0), featured(1)
            pairs = [(a * b).astype(BF16) for a, b in zip(keys, values)]
            for j in range(0, CHUNK, 2):
                carried_ref[pl.ds(pl.multiple_of(row0 + 8 * j, 16), 16), here] = jnp.concatenate(
                    pairs[j : j + 2], axis=0
                )
            carried = [a.astype(F32) for a in pairs]

            for m in range(POLES):
                e = decay_s[m : m + 1, here]
                s = carried[0]
                for j in range(1, CHUNK):
                    s = s * e + carried[j]
                a1 = jnp.exp(-float(CHUNK) * rates[m : m + 1, here])
                a2 = a1 * a1
                a4 = a2 * a2
                s = s + a1 * down(s, 1)
                s = s + a2 * down(s, 2)
                s = s + a4 * down(s, 4)
                start = carry[m]
                s = s + jnp.exp(
                    -float(CHUNK) * rates[m : m + 1, here] * (sub + 1).astype(F32)
                ) * start
                chunk_ref[m, pl.ds(pl.multiple_of(p * 8, 8), 8), here] = jnp.where(
                    sub == 0, start, pltpu.roll(s, 1, 0)
                )
                carry[m] = jnp.broadcast_to(s[7:8, :], (8, LANES))

        for m in range(POLES):
            state_ref[m : m + 1, here] = carry[m, 0:1, :]


def project(normed, halo, weights, taps, rates):
    any_spec = pl.BlockSpec(memory_space=pl.ANY)
    vmem = pl.BlockSpec(memory_space=pltpu.VMEM)
    return pl.pallas_call(
        project_kernel,
        in_specs=[any_spec] * 13 + [vmem] * 2,
        out_specs=[vmem] * 3,
        out_shape=[
            jax.ShapeDtypeStruct((SPAN, CH), BF16),
            jax.ShapeDtypeStruct((POLES, SPAN // CHUNK, CH), F32),
            jax.ShapeDtypeStruct((POLES, CH), F32),
        ],
        scratch_shapes=[
            pltpu.VMEM((ROWS, D), BF16),
            pltpu.VMEM((D, WIDE), BF16),
            pltpu.VMEM((ROWS, WIDE), F32),
            pltpu.VMEM((POLES, CH), F32),
            pltpu.VMEM((POLES, 8, LANES), F32),
            pltpu.SemaphoreType.DMA((13,)),
        ],
        compiler_params=params(50),
        cost_estimate=pl.CostEstimate(
            flops=2 * ROWS * D * WIDE, bytes_accessed=10_000_000, transcendentals=0
        ),
    )(*normed, halo, *weights, taps, rates)


def direct_kernel(
    a0, a1, a2, a3, b0, b1, b2, b3, halo, wq, carried, taps, rates, residues, skip,
    gate_ref, local_ref,
    lhs, w, query, taps_s, sems,
):
    copies, copy = copier(sems)
    copy(wq, w)
    copy_rows(copy, (a0, a1, a2, a3, b0, b1, b2, b3), halo, lhs)
    decay = jnp.exp(-rates[...])
    power = residues[...] * jnp.sqrt(2.0 * rates[...])
    for i in range(CHUNK):
        row = jnp.sum(power, axis=0, keepdims=True)
        taps_s[i : i + 1, :] = row + skip[...] if i == 0 else row
        power = power * decay
    sub = lax.broadcasted_iota(jnp.int32, (8, LANES), 0)
    for c in copies:
        c.wait()
    query[...] = rounded(jnp.dot(lhs[...], w[...], preferred_element_type=F32))

    @pl.loop(0, CH // LANES)
    def _(l):
        here = pl.ds(pl.multiple_of(l * LANES, LANES), LANES)

        @pl.loop(0, PIECES)
        def _(p):
            row0 = pl.multiple_of(p * HERE, 16)

            t = [taps[i : i + 1, here] for i in range(3)]
            ext = [query[pl.ds(row0 + 8 * i, 8), here] for i in range(2 + CHUNK)]
            queries = filtered(ext, t, sub)
            for j in range(0, CHUNK, 2):
                gate_ref[pl.ds(pl.multiple_of(row0 + 8 * j, 16), 16), here] = jnp.concatenate(
                    queries[j : j + 2], axis=0
                ).astype(BF16)
            pairs = [
                carried[pl.ds(pl.multiple_of(row0 + 8 * j, 16), 16), here].astype(F32)
                for j in range(0, CHUNK, 2)
            ]
            x = [half for pair in pairs for half in (pair[:8], pair[8:])]
            k = [taps_s[i : i + 1, here] for i in range(CHUNK)]
            for j in range(CHUNK):
                acc = k[0] * x[j]
                for i in range(j):
                    acc = acc + k[j - i] * x[i]
                local_ref[pl.ds(row0 + 8 * j, 8), here] = acc


def direct(normed, halo, weight, carried, taps, rates, residues, skip):
    any_spec = pl.BlockSpec(memory_space=pl.ANY)
    vmem = pl.BlockSpec(memory_space=pltpu.VMEM)
    return pl.pallas_call(
        direct_kernel,
        in_specs=[any_spec] * 10 + [vmem] * 5,
        out_specs=[vmem] * 2,
        out_shape=[
            jax.ShapeDtypeStruct((SPAN, CH), BF16),
            jax.ShapeDtypeStruct((SPAN, CH), F32),
        ],
        scratch_shapes=[
            pltpu.VMEM((ROWS, D), BF16),
            pltpu.VMEM((D, CH), BF16),
            pltpu.VMEM((ROWS, CH), F32),
            pltpu.VMEM((CHUNK, CH), F32),
            pltpu.SemaphoreType.DMA((10,)),
        ],
        compiler_params=params(50),
        cost_estimate=pl.CostEstimate(
            flops=2 * ROWS * D * CH, bytes_accessed=8_000_000, transcendentals=0
        ),
    )(*normed, halo, weight, carried, taps, rates, residues, skip)


def finish_kernel(
    states, rates, residues, local, chunk, gate, out, scr, start_s, decay_s, weight_s
):
    z = lax.axis_index("z")
    rate = rates[...]
    span = jnp.exp(-float(SPAN) * rate)
    total = jnp.zeros((POLES, CH), F32)
    for i in range(NZ - 1):
        total = jnp.where(i < z, total * span + states[i], total)
    start_s[...] = total
    decay = jnp.exp(-rate)
    decay_s[...] = decay
    weight_s[...] = residues[...] * jnp.sqrt(2.0 * rate) * decay
    sub = lax.broadcasted_iota(jnp.int32, (8, LANES), 0)

    @pl.loop(0, PIECES)
    def _(p):
        @pl.loop(0, CH // LANES)
        def _(l):
            here = pl.ds(pl.multiple_of(l * LANES, LANES), LANES)
            row0 = pl.multiple_of(p * HERE, 16)
            age = -float(CHUNK) * (p * 8 + sub).astype(F32)
            v, e = [], []
            for m in range(POLES):
                fade = jnp.exp(rates[m : m + 1, here] * age)
                at = chunk[m, pl.ds(pl.multiple_of(p * 8, 8), 8), here]
                v.append((at + fade * start_s[m : m + 1, here]) * weight_s[m : m + 1, here])
                e.append(decay_s[m : m + 1, here])
            for j in range(0, CHUNK, 2):
                gates = gate[pl.ds(pl.multiple_of(row0 + 8 * j, 16), 16), here].astype(F32)
                for i in range(2):
                    parts = list(v)
                    while len(parts) > 1:
                        parts = [a + b for a, b in zip(parts[::2], parts[1::2])]
                    response = rounded(local[pl.ds(row0 + 8 * (j + i), 8), here] + parts[0])
                    scr[pl.ds(j + i, 8, stride=CHUNK), :] = gates[8 * i : 8 * i + 8] * response
                    v = [a * b for a, b in zip(v, e)]
            out[p, here, :] = scr[...].T.astype(BF16)


def finish(states, rates, residues, local, chunk, gate):
    vmem = pl.BlockSpec(memory_space=pltpu.VMEM)
    return pl.pallas_call(
        finish_kernel,
        in_specs=[vmem] * 6,
        out_specs=vmem,
        out_shape=jax.ShapeDtypeStruct((PIECES, CH, HERE), BF16),
        scratch_shapes=[
            pltpu.VMEM((HERE, LANES), F32),
            pltpu.VMEM((POLES, CH), F32),
            pltpu.VMEM((POLES, CH), F32),
            pltpu.VMEM((POLES, CH), F32),
        ],
        compiler_params=params(10),
    )(states, rates, residues, local, chunk, gate)


def place_kernel(pieces, out):
    for g in range(PIECES):
        for i in range(NZ):
            out[i, g] = pieces[g, 32 * i : 32 * i + 32, :]


def place(pieces):
    out = pl.pallas_call(
        place_kernel,
        out_shape=jax.ShapeDtypeStruct((NZ, PIECES, 32, HERE), BF16),
        compiler_params=params(10),
    )(pieces)
    return out.reshape(1, NZ * PIECES * 32, HERE)


def ring(size, by):
    return [(i, (i + by) % size) for i in range(size)]


def along_x(value):
    got = {d: lax.ppermute(value, "x", ring(NX, d)) for d in (2, 1, 3)}
    return [value] + [got[d] for d in (1, 2, 3)]


def spread(value):
    return jnp.broadcast_to(value[None], (NZ,) + value.shape)


def swap(value, axes):
    return lax.all_to_all(value, axes, split_axis=0, concat_axis=0, tiled=True)


def tail_kernel(a0, a1, a2, a3, out, sem):
    which = lax.rem(lax.axis_index("x") + 1, NX)
    for d, piece in enumerate((a0, a1, a2, a3)):

        @pl.when(which == d)
        def _(piece=piece):
            copy = pltpu.make_async_copy(piece.at[pl.ds(HERE - HALO, HALO)], out, sem)
            copy.start()
            copy.wait()


def last_rows(row):
    any_spec = pl.BlockSpec(memory_space=pl.ANY)
    return pl.pallas_call(
        tail_kernel,
        in_specs=[any_spec] * NX,
        out_specs=any_spec,
        out_shape=jax.ShapeDtypeStruct((HALO, D), BF16),
        scratch_shapes=[pltpu.SemaphoreType.DMA],
        compiler_params=params(10),
    )(*row)


def body(tokens, norm_gain, in_weight, short_filter, rates, residues, skip):
    x, yh = lax.axis_index("x"), lax.axis_index("yh")
    own = normalise(tokens[0], norm_gain[None, :])

    blocks = in_weight.reshape(8, 3, NZ, PIECES, 32).transpose(3, 0, 1, 2, 4)
    unit = swap(blocks.reshape(PIECES, 8, COLS), ("yh", "x")).reshape(64, COLS)
    own, unit = lax.optimization_barrier((own, unit))

    partner = lax.ppermute(own, "yh", ring(2, 1))
    own_row = along_x(own)
    plane = swap(spread(unit[:, CH:]), "z").reshape(512, WIDE)
    query_weight = lax.all_gather(unit[:, :CH], ("yl", "co", "z"), axis=0, tiled=True)

    other_plane = lax.ppermute(plane, "yl", ring(2, 1))
    partner_row = along_x(partner)
    sibling = lax.ppermute(plane, "co", ring(2, 1))
    other_sibling = lax.ppermute(other_plane, "co", ring(2, 1))
    weights = [plane, other_plane, sibling, other_sibling]
    normed = own_row + partner_row

    tail = last_rows(own_row)
    halo = 0
    for to in range(2):
        pairs = [(2 * z + 1, 2 * z + 2 + to) for z in range(NZ - 1)]
        halo = halo + lax.ppermute(tail, ("z", "yh"), pairs)

    rates, residues, skip, _ = lax.optimization_barrier((rates, residues, skip, plane))
    mine = jnp.concatenate(
        [
            rates.T.reshape(4, LANES),
            residues.T.reshape(4, LANES),
            jnp.pad(skip, (0, LANES - 32)).reshape(1, LANES),
        ]
    )
    table = swap(spread(mine), "z")
    rate_table = table[:, 0:4].reshape(NZ, POLES, 32).transpose(1, 0, 2).reshape(POLES, CH)
    residue_table = table[:, 4:8].reshape(NZ, POLES, 32).transpose(1, 0, 2).reshape(POLES, CH)
    skip_row = table[:, 8, :32].reshape(1, CH)
    taps = short_filter.reshape(3, 3, NZ, PIECES, 32)
    taps = lax.dynamic_index_in_dim(taps, yh * NX + x, 3, keepdims=False).reshape(3, COLS)

    carried, chunk, state = project(normed, halo, weights, taps, rate_table)
    states = swap(spread(state), "z")
    gate, local = direct(
        normed, halo, query_weight, carried, taps, rate_table, residue_table, skip_row
    )
    pieces = finish(states, rate_table, residue_table, local, chunk, gate)
    return place(swap(pieces, ("yh", "x")))


def solution(mesh):
    fine = Mesh(mesh.devices.reshape(2, 2, NZ, 2, NX), ("yl", "co", "z", "yh", "x"))
    fsdp, ctx = ("yl", "co"), ("z", "yh", "x")
    in_specs = (
        P(fsdp, ctx, None),
        P(),
        P(fsdp + ctx, None),
        P(),
        P(ctx, None),
        P(ctx, None),
        P(ctx),
    )
    return jax.shard_map(
        body, mesh=fine, in_specs=in_specs, out_specs=P(fsdp, None, ctx), check_vma=False
    )
```

```python
import functools

import jax
import jax.numpy as jnp
from jax import lax
from jax.experimental import pallas as pl
from jax.experimental.pallas import tpu as pltpu
from jax.sharding import Mesh, PartitionSpec as P

F32 = jnp.float32
BF16 = jnp.bfloat16
NX, NZ = 4, 8
PIECES = 8
POLES = 16
HERE = 128
CHUNK = 16
LANES = 128
CH = 256
HALO = 16
SPAN = PIECES * HERE
ROWS = HALO + SPAN
D = 2048
UNIT = 128
NEAR = (0, 1, 2, 3, 5, 6, 7)
TABLE = 16
COLS = 3 * CH
MIB = 1024 * 1024


def params(mib):
    return pltpu.CompilerParams(vmem_limit_bytes=mib * MIB)


def norm_kernel(tok_ref, gain_ref, out_ref, scr):
    x = tok_ref[...].astype(F32)
    inv = lax.rsqrt(jnp.mean(x * x, axis=1, keepdims=True) + 1e-6)
    for k in range(D // LANES):
        lanes = slice(k * LANES, (k + 1) * LANES)
        scr[k] = x[:, lanes] * inv * gain_ref[:, lanes]
    for k in range(D // LANES):
        for j in range(0, CHUNK, 2):
            pair = [scr[k, pl.ds(j + i, 8, stride=CHUNK), :] for i in range(2)]
            out_ref[8 * j : 8 * j + 16, k * LANES : (k + 1) * LANES] = jnp.concatenate(
                pair, axis=0
            ).astype(BF16)


def normalise(tokens, gain):
    return pl.pallas_call(
        norm_kernel,
        out_shape=jax.ShapeDtypeStruct((HERE, D), BF16),
        scratch_shapes=[pltpu.VMEM((D // LANES, HERE, LANES), F32)],
        compiler_params=params(10),
    )(tokens, gain)


def rounded(v):
    return v.astype(BF16).astype(F32)


def filtered(ext, t, sub):
    prev = [
        jnp.where(sub == 0, pltpu.roll(ext[i], 1, 0), pltpu.roll(ext[CHUNK + i], 1, 0))
        for i in range(2)
    ]
    ext = prev + ext[2:]
    return [t[0] * ext[j + 2] + t[1] * ext[j + 1] + t[2] * ext[j] for j in range(CHUNK)]


class Copier:
    def __init__(self, sems):
        self.sems, self.copies = sems, []

    def __call__(self, src, dst):
        c = pltpu.make_async_copy(src, dst, self.sems.at[len(self.copies)])
        c.start()
        self.copies.append(c)

    def one_of(self, which, sources, dst):
        sem = self.sems.at[len(self.copies)]
        for i, src in enumerate(sources):
            c = pltpu.make_async_copy(src, dst, sem)
            pl.when(which == i)(c.start)
        self.copies.append(c)

    def wait(self):
        for c in self.copies:
            c.wait()


HALF = HERE // 2
PIECE_LIST = (
    (0, 0, 0, HERE, 0, 0),
    (0, 1, 0, HERE, 1, 0),
    (0, 3, 0, HERE, 2, 0),
    (1, 0, 0, HERE, 3, 0),
    (1, 1, 0, HERE, 4, 0),
    (0, 2, 0, HALF, 4, HERE),
    (1, 3, 0, HERE, 5, 0),
    (0, 2, HALF, HALF, 5, HERE),
    (1, 2, 0, HALF, 6, 0),
    (1, 2, HALF, HALF, 7, 0),
)
PIECE_ARRAYS = 8


def copy_rows(copy, arrays, halo, lhs):
    x, yh = lax.axis_index("x"), lax.axis_index("yh")
    copy.one_of(yh, halo, lhs.at[pl.ds(0, HALO)])
    for other, by, first, rows, array, at in PIECE_LIST:
        place = lax.rem(yh + other, 2) * NX + lax.rem(x + NX - by, NX)
        row = pl.multiple_of(HALO + place * HERE + first, 16)
        copy(arrays[array].at[pl.ds(at, rows)], lhs.at[pl.ds(row, rows)])


def copy_weights(copy, planes, w):
    z, core = lax.axis_index("z"), lax.axis_index("co")
    for r in range(2):
        most, last = planes[2 * r], planes[2 * r + 1]
        for i, d in enumerate(NEAR + (NZ // 2,)):
            place = last if d == NZ // 2 else most.at[i]
            row = lax.rem(core + r, 2) * 512 + lax.rem(z + NZ - d, NZ) * 64
            for yl in range(2):
                to = pl.ds(pl.multiple_of(yl * 1024 + row, 64), 64)
                copy(place.at[pl.ds(yl * 64, 64)], w.at[to])


def decode(blocks, out):
    z = lax.axis_index("z")
    halves = [jnp.zeros((TABLE, COLS), F32)] * 2
    for i, d in enumerate(NEAR + (NZ // 2,)):
        block = blocks[i].astype(F32)
        low = lax.rem(z + NZ - d, NZ) < NZ // 2
        halves[0] = halves[0] + jnp.where(low, block, 0.0)
        halves[1] = halves[1] + jnp.where(low, 0.0, block)
    for h, block in enumerate(halves):
        tile = [block[:, i * LANES : (i + 1) * LANES] for i in range(6)]
        lanes = slice(h * LANES, (h + 1) * LANES)
        out[0:16, lanes] = tile[0] + tile[1] + tile[2]
        out[16:32, lanes] = tile[3] + tile[4]
        skip = tile[5][0:1] + tile[5][1:2] + tile[5][2:3]
        out[32:40, lanes] = jnp.broadcast_to(skip, (8, LANES))


def project_kernel(
    *refs,
):
    arrays, refs = refs[:PIECE_ARRAYS], refs[PIECE_ARRAYS:]
    halo, planes, refs = refs[:2], refs[2:6], refs[6:]
    taps, query_ref, carried_ref, chunk_ref, state_ref, rates = refs[:6]
    lhs, w, proj, blocks, decay_s, carry, sems = refs[6:]
    copy = Copier(sems)
    copy_weights(copy, planes, w)
    copy(planes[0].at[:, pl.ds(UNIT, TABLE)], blocks.at[pl.ds(0, NZ - 1)])
    copy(planes[1].at[pl.ds(UNIT, TABLE)], blocks.at[NZ - 1])
    copy_rows(copy, arrays, halo, lhs)
    copy.wait()
    decode(blocks, rates)
    decay_s[...] = jnp.exp(-rates[0:16, :])
    for s in (1, 2, 0):
        cols = slice(s * CH, (s + 1) * CH)
        product = jnp.dot(lhs[...], w[:, cols], preferred_element_type=F32).astype(BF16)
        if s == 0:
            query_ref[...] = product
        else:
            proj[:, (s - 1) * CH : s * CH] = product.astype(F32)

    sub = lax.broadcasted_iota(jnp.int32, (8, LANES), 0)

    def down(v, by):
        return jnp.where(sub >= by, pltpu.roll(v, by, 0), 0.0)

    @pl.loop(0, CH // LANES)
    def _(l):
        lane0 = pl.multiple_of(l * LANES, LANES)
        here = pl.ds(lane0, LANES)
        carry[...] = jnp.zeros_like(carry)

        @pl.loop(0, PIECES)
        def _(p):
            row0 = pl.multiple_of(p * HERE, 16)

            def featured(s):
                lanes = pl.ds(pl.multiple_of(s * CH + lane0, LANES), LANES)
                first = pl.ds(pl.multiple_of((s + 1) * CH + lane0, LANES), LANES)
                ext = [proj[pl.ds(row0 + 8 * i, 8), lanes] for i in range(2 + CHUNK)]
                return filtered(ext, [taps[i : i + 1, first] for i in range(3)], sub)

            keys, values = featured(0), featured(1)
            pairs = [(a * b).astype(BF16) for a, b in zip(keys, values)]
            for j in range(0, CHUNK, 2):
                carried_ref[pl.ds(pl.multiple_of(row0 + 8 * j, 16), 16), here] = jnp.concatenate(
                    pairs[j : j + 2], axis=0
                )
            carried = [a.astype(F32) for a in pairs]

            for m in range(POLES):
                e = decay_s[m : m + 1, here]
                s = carried[0]
                for j in range(1, CHUNK):
                    s = s * e + carried[j]
                a1 = jnp.exp(-float(CHUNK) * rates[m : m + 1, here])
                a2 = a1 * a1
                a4 = a2 * a2
                s = s + a1 * down(s, 1)
                s = s + a2 * down(s, 2)
                s = s + a4 * down(s, 4)
                start = carry[m]
                s = s + jnp.exp(
                    -float(CHUNK) * rates[m : m + 1, here] * (sub + 1).astype(F32)
                ) * start
                chunk_ref[m, pl.ds(pl.multiple_of(p * 8, 8), 8), here] = jnp.where(
                    sub == 0, start, pltpu.roll(s, 1, 0)
                )
                carry[m] = jnp.broadcast_to(s[7:8, :], (8, LANES))

        for m in range(POLES):
            for i in range(NZ):
                state_ref[i, m : m + 1, here] = carry[m, 0:1, :]


def project(arrays, halo, weights, taps):
    any_spec = pl.BlockSpec(memory_space=pl.ANY)
    vmem = pl.BlockSpec(memory_space=pltpu.VMEM)
    return pl.pallas_call(
        project_kernel,
        in_specs=[any_spec] * (PIECE_ARRAYS + 6) + [vmem],
        out_specs=[vmem] * 5,
        out_shape=[
            jax.ShapeDtypeStruct((ROWS, CH), BF16),
            jax.ShapeDtypeStruct((SPAN, CH), BF16),
            jax.ShapeDtypeStruct((POLES, SPAN // CHUNK, CH), F32),
            jax.ShapeDtypeStruct((NZ, POLES, CH), F32),
            jax.ShapeDtypeStruct((40, CH), F32),
        ],
        scratch_shapes=[
            pltpu.VMEM((ROWS, D), BF16),
            pltpu.VMEM((D, COLS), BF16),
            pltpu.VMEM((ROWS, 2 * CH), F32),
            pltpu.VMEM((NZ, TABLE, COLS), BF16),
            pltpu.VMEM((POLES, CH), F32),
            pltpu.VMEM((POLES, 8, LANES), F32),
            pltpu.SemaphoreType.DMA((len(PIECE_LIST) + 35,)),
        ],
        compiler_params=params(60),
        cost_estimate=pl.CostEstimate(
            flops=2 * ROWS * D * COLS, bytes_accessed=10_000_000, transcendentals=0
        ),
    )(*arrays, *halo, *weights, taps)


def direct_kernel(query, carried, taps, table, gate_ref, local_ref, taps_s):
    rate = table[0:16, :]
    decay = jnp.exp(-rate)
    power = table[16:32, :] * jnp.sqrt(2.0 * rate)
    skip = table[32:33, :]
    for i in range(CHUNK):
        row = jnp.sum(power, axis=0, keepdims=True)
        taps_s[i : i + 1, :] = row + skip if i == 0 else row
        power = power * decay
    sub = lax.broadcasted_iota(jnp.int32, (8, LANES), 0)

    @pl.loop(0, CH // LANES)
    def _(l):
        here = pl.ds(pl.multiple_of(l * LANES, LANES), LANES)

        @pl.loop(0, PIECES)
        def _(p):
            row0 = pl.multiple_of(p * HERE, 16)

            t = [taps[i : i + 1, here] for i in range(3)]

            def rows(ref, count):
                pairs = [
                    ref[pl.ds(pl.multiple_of(row0 + 16 * i, 16), 16), here].astype(F32)
                    for i in range(count)
                ]
                return [half for pair in pairs for half in (pair[:8], pair[8:])]

            queries = filtered(rows(query, 9), t, sub)
            for j in range(0, CHUNK, 2):
                gate_ref[pl.ds(pl.multiple_of(row0 + 8 * j, 16), 16), here] = jnp.concatenate(
                    queries[j : j + 2], axis=0
                ).astype(BF16)
            x = rows(carried, 8)
            k = [taps_s[i : i + 1, here] for i in range(CHUNK)]
            for j in range(CHUNK):
                acc = k[0] * x[j]
                for i in range(j):
                    acc = acc + k[j - i] * x[i]
                local_ref[pl.ds(row0 + 8 * j, 8), here] = acc


def direct(query, carried, taps, table):
    vmem = pl.BlockSpec(memory_space=pltpu.VMEM)
    return pl.pallas_call(
        direct_kernel,
        in_specs=[vmem] * 4,
        out_specs=[vmem] * 2,
        out_shape=[
            jax.ShapeDtypeStruct((SPAN, CH), BF16),
            jax.ShapeDtypeStruct((SPAN, CH), F32),
        ],
        scratch_shapes=[pltpu.VMEM((CHUNK, CH), F32)],
        compiler_params=params(10),
        cost_estimate=pl.CostEstimate(
            flops=40 * SPAN * CH, bytes_accessed=3_000_000, transcendentals=0
        ),
    )(query, carried, taps, table)


def finish_kernel(
    states, table, local, chunk, gate, out, scr, rates, start_s, decay_s, weight_s
):
    z = lax.axis_index("z")
    rate = table[0:16, :]
    rates[...] = rate
    span = jnp.exp(-float(SPAN) * rate)
    total = jnp.zeros((POLES, CH), F32)
    for i in range(NZ - 1):
        total = jnp.where(i < z, total * span + states[i], total)
    start_s[...] = total
    decay = jnp.exp(-rate)
    decay_s[...] = decay
    weight_s[...] = table[16:32, :] * jnp.sqrt(2.0 * rate) * decay
    sub = lax.broadcasted_iota(jnp.int32, (8, LANES), 0)

    @pl.loop(0, PIECES)
    def _(p):
        @pl.loop(0, CH // LANES)
        def _(l):
            here = pl.ds(pl.multiple_of(l * LANES, LANES), LANES)
            row0 = pl.multiple_of(p * HERE, 16)
            age = -float(CHUNK) * (p * 8 + sub).astype(F32)
            v, e = [], []
            for m in range(POLES):
                fade = jnp.exp(rates[m : m + 1, here] * age)
                at = chunk[m, pl.ds(pl.multiple_of(p * 8, 8), 8), here]
                v.append((at + fade * start_s[m : m + 1, here]) * weight_s[m : m + 1, here])
                e.append(decay_s[m : m + 1, here])
            for j in range(0, CHUNK, 2):
                gates = gate[pl.ds(pl.multiple_of(row0 + 8 * j, 16), 16), here].astype(F32)
                for i in range(2):
                    parts = list(v)
                    while len(parts) > 1:
                        parts = [a + b for a, b in zip(parts[::2], parts[1::2])]
                    response = rounded(local[pl.ds(row0 + 8 * (j + i), 8), here] + parts[0])
                    scr[pl.ds(j + i, 8, stride=CHUNK), :] = gates[8 * i : 8 * i + 8] * response
                    v = [a * b for a, b in zip(v, e)]
            out[p, here, :] = scr[...].T.astype(BF16)


def finish(states, table, local, chunk, gate):
    vmem = pl.BlockSpec(memory_space=pltpu.VMEM)
    return pl.pallas_call(
        finish_kernel,
        in_specs=[vmem] * 5,
        out_specs=vmem,
        out_shape=jax.ShapeDtypeStruct((PIECES, CH, HERE), BF16),
        scratch_shapes=[
            pltpu.VMEM((HERE, LANES), F32),
            pltpu.VMEM((POLES, CH), F32),
            pltpu.VMEM((POLES, CH), F32),
            pltpu.VMEM((POLES, CH), F32),
            pltpu.VMEM((POLES, CH), F32),
        ],
        compiler_params=params(10),
    )(states, table, local, chunk, gate)


def place_kernel(pieces, out):
    for g in range(PIECES):
        for i in range(NZ):
            out[i, g] = pieces[g, 32 * i : 32 * i + 32, :]


def place(pieces):
    out = pl.pallas_call(
        place_kernel,
        out_shape=jax.ShapeDtypeStruct((NZ, PIECES, 32, HERE), BF16),
        compiler_params=params(10),
    )(pieces)
    return out.reshape(1, NZ * PIECES * 32, HERE)


def ring(size, by):
    return [(i, (i + by) % size) for i in range(size)]


def shift(value, axis, by):
    return lax.ppermute(value, axis, ring(lax.axis_size(axis), by))


def spread(value, count=NZ):
    return jnp.broadcast_to(value[None], (count,) + value.shape)


def swap(value, axes):
    return lax.all_to_all(value, axes, split_axis=0, concat_axis=0, tiled=True)


def tail_kernel(own, behind, ahead, mixed, out, sem):
    x = lax.axis_index("x")
    for at, piece in ((3, own), (0, behind), (2, ahead), (1, mixed)):

        @pl.when(x == at)
        def _(piece=piece):
            rows = pl.ds(piece.shape[0] - HALO, HALO)
            copy = pltpu.make_async_copy(piece.at[rows], out, sem)
            copy.start()
            copy.wait()


def last_rows(row):
    any_spec = pl.BlockSpec(memory_space=pl.ANY)
    return pl.pallas_call(
        tail_kernel,
        in_specs=[any_spec] * NX,
        out_specs=any_spec,
        out_shape=jax.ShapeDtypeStruct((HALO, D), BF16),
        scratch_shapes=[pltpu.SemaphoreType.DMA],
        compiler_params=params(10),
    )(*row)


def coded(values, parts):
    out = []
    for _ in range(parts):
        part = lax.reduce_precision(values, 8, 7)
        out.append(part)
        values = values - part
    return out


def body(tokens, norm_gain, in_weight, short_filter, rates, residues, skip):
    x, yh, z = lax.axis_index("x"), lax.axis_index("yh"), lax.axis_index("z")
    together = lax.optimization_barrier

    taps = short_filter.reshape(3, 3, NZ, PIECES, 32)
    taps = lax.dynamic_index_in_dim(taps, yh * NX + x, 3, keepdims=False).reshape(3, COLS)
    skips = jnp.pad(jnp.stack(coded(skip, 3)), ((0, TABLE - 3), (0, 0)))
    mine = jnp.stack(coded(rates.T, 3) + coded(residues.T, 2) + [skips], axis=1)
    mine = jnp.tile(mine, (1, 1, 4)).reshape(TABLE, COLS)
    lane = jnp.arange(COLS)[None, :] % LANES
    mine = jnp.where(lane // 32 == z % 4, mine, 0.0).astype(BF16)

    blocks = in_weight.reshape(8, 3, NZ, PIECES, 32).transpose(3, 0, 1, 2, 4)
    blocks = spread(blocks.reshape(PIECES, 8, COLS), 2).reshape(2 * PIECES, 8, COLS)
    tokens, blocks = together((tokens, blocks))
    unit = swap(blocks, ("yl", "yh", "x")).reshape(UNIT, COLS)
    unit = jnp.concatenate([unit, mine])
    own = normalise(tokens[0], norm_gain[None, :])
    partner = shift(own, "yh", 1)
    own_1, own_3 = shift(own, "x", 1), shift(own, "x", -1)

    def step(up, down):
        return shift(up, "z", 1), shift(down, "z", -1)

    up_1, down_1 = step(unit, unit)
    up_1, down_1, partner, own_1, own_3, taps = together(
        (up_1, down_1, partner, own_1, own_3, taps)
    )
    mixed_1 = shift(jnp.concatenate([partner, own_1[:HALF]]), "x", 1)
    mixed_3 = shift(jnp.concatenate([partner, own_3[HALF:]]), "x", -1)
    up_2, down_2 = step(up_1, down_1)
    up_3, down_3 = step(up_2, down_2)
    up_3, down_3, mixed_1, mixed_3 = together((up_3, down_3, mixed_1, mixed_3))
    first = shift(mixed_1[:HALF], "x", 1)
    second = shift(mixed_3[HALF:HERE], "x", -1)
    tail = last_rows((own, own_1, own_3, mixed_3))
    halo = [
        lax.ppermute(tail, ("z", "yh"), [(2 * i + 1, 2 * i + 2 + to) for i in range(NZ - 1)])
        for to in range(2)
    ]
    near = jnp.stack([unit, up_1, up_2, up_3, down_3, down_2, down_1])
    last = shift(up_3, "z", 1)
    near_sibling = shift(near, "co", 1)
    last, first, second, near_sibling, *halo = together((last, first, second, near_sibling, *halo))
    weights = [near, last, near_sibling, shift(last, "co", 1)]
    arrays = [own, own_1, own_3, partner, mixed_1, mixed_3, first, second]

    query, carried, chunk, state, table = project(arrays, halo, weights, taps)
    states = swap(state, "z")
    gate, local = direct(query, carried, taps, table)
    pieces = finish(states, table, local, chunk, gate)
    return place(swap(pieces, ("yh", "x")))


def solution(mesh):
    fine = Mesh(mesh.devices.reshape(2, 2, NZ, 2, NX), ("yl", "co", "z", "yh", "x"))
    fsdp, ctx = ("yl", "co"), ("z", "yh", "x")
    in_specs = (
        P(fsdp, ctx, None),
        P(),
        P(fsdp + ctx, None),
        P(),
        P(ctx, None),
        P(ctx, None),
        P(ctx),
    )
    return jax.shard_map(
        body, mesh=fine, in_specs=in_specs, out_specs=P(fsdp, None, ctx), check_vma=False
    )
```

```python
import functools

import jax
import jax.numpy as jnp
from jax import lax
from jax.experimental import pallas as pl
from jax.experimental.pallas import tpu as pltpu
from jax.sharding import Mesh, PartitionSpec as P

F32 = jnp.float32
BF16 = jnp.bfloat16
NX, NZ = 4, 8
PIECES = 8
POLES = 16
HERE = 128
CHUNK = 16
LANES = 128
CH = 256
HALO = 16
SPAN = PIECES * HERE
ROWS = HALO + SPAN
D = 2048
UNIT = 128
PLACES = (0, 1, 2, 3, 4, 5, 6, 7)
TABLE = 16
COLS = 3 * CH
MIB = 1024 * 1024


def params(mib):
    return pltpu.CompilerParams(vmem_limit_bytes=mib * MIB)


def norm_kernel(tok_ref, gain_ref, out_ref, scr):
    x = tok_ref[...].astype(F32)
    inv = lax.rsqrt(jnp.mean(x * x, axis=1, keepdims=True) + 1e-6)
    for k in range(D // LANES):
        lanes = slice(k * LANES, (k + 1) * LANES)
        scr[k] = x[:, lanes] * inv * gain_ref[:, lanes]
    for k in range(D // LANES):
        for j in range(0, CHUNK, 2):
            pair = [scr[k, pl.ds(j + i, 8, stride=CHUNK), :] for i in range(2)]
            out_ref[8 * j : 8 * j + 16, k * LANES : (k + 1) * LANES] = jnp.concatenate(
                pair, axis=0
            ).astype(BF16)


def normalise(tokens, gain):
    return pl.pallas_call(
        norm_kernel,
        out_shape=jax.ShapeDtypeStruct((HERE, D), BF16),
        scratch_shapes=[pltpu.VMEM((D // LANES, HERE, LANES), F32)],
        compiler_params=params(10),
    )(tokens, gain)


def rounded(v):
    return v.astype(BF16).astype(F32)


def filtered(ext, t, sub):
    prev = [
        jnp.where(sub == 0, pltpu.roll(ext[i], 1, 0), pltpu.roll(ext[CHUNK + i], 1, 0))
        for i in range(2)
    ]
    ext = prev + ext[2:]
    return [t[0] * ext[j + 2] + t[1] * ext[j + 1] + t[2] * ext[j] for j in range(CHUNK)]


class Copier:
    def __init__(self, sems):
        self.sems, self.copies = sems, []

    def __call__(self, src, dst):
        c = pltpu.make_async_copy(src, dst, self.sems.at[len(self.copies)])
        c.start()
        self.copies.append(c)

    def one_of(self, which, sources, dst):
        sem = self.sems.at[len(self.copies)]
        for i, src in enumerate(sources):
            c = pltpu.make_async_copy(src, dst, sem)
            pl.when(which == i)(c.start)
        self.copies.append(c)

    def wait(self):
        for c in self.copies:
            c.wait()


HALF = HERE // 2
PIECE_LIST = (
    (0, 0, 0, HERE, 0, 0),
    (0, 1, 0, HERE, 1, 0),
    (0, 3, 0, HERE, 2, 0),
    (1, 0, 0, HERE, 3, 0),
    (1, 1, 0, HERE, 4, 0),
    (0, 2, 0, HALF, 4, HERE),
    (1, 3, 0, HERE, 5, 0),
    (0, 2, HALF, HALF, 5, HERE),
    (1, 2, 0, HALF, 6, 0),
    (1, 2, HALF, HALF, 7, 0),
)
PIECE_ARRAYS = 8


def place_rows(arrays, halo, lhs):
    x, yh = lax.axis_index("x"), lax.axis_index("yh")
    for i, source in enumerate(halo):

        @pl.when(yh == i)
        def _(source=source):
            lhs[0:HALO, :] = source[...]

    for other, by, first, rows, array, at in PIECE_LIST:
        place = lax.rem(yh + other, 2) * NX + lax.rem(x + NX - by, NX)
        row = pl.multiple_of(HALO + place * HERE + first, 16)
        lhs[pl.ds(row, rows), :] = arrays[array][at : at + rows, :]


def place_weights(planes, w):
    z, core = lax.axis_index("z"), lax.axis_index("co")
    for r, plane in enumerate(planes):
        for i, d in enumerate(PLACES):
            row = lax.rem(core + r, 2) * 512 + lax.rem(z + NZ - d, NZ) * 64
            for yl in range(2):
                to = pl.ds(pl.multiple_of(yl * 1024 + row, 64), 64)
                w[to, :] = plane[i, yl * 64 : yl * 64 + 64, :]


def decode(plane, out):
    z = lax.axis_index("z")
    halves = [jnp.zeros((TABLE, COLS), F32)] * 2
    for i, d in enumerate(PLACES):
        block = plane[i, UNIT:, :].astype(F32)
        low = lax.rem(z + NZ - d, NZ) < NZ // 2
        halves[0] = halves[0] + jnp.where(low, block, 0.0)
        halves[1] = halves[1] + jnp.where(low, 0.0, block)
    for h, block in enumerate(halves):
        tile = [block[:, i * LANES : (i + 1) * LANES] for i in range(6)]
        lanes = slice(h * LANES, (h + 1) * LANES)
        out[0:16, lanes] = tile[0] + tile[1] + tile[2]
        out[16:32, lanes] = tile[3] + tile[4]
        skip = tile[5][0:1] + tile[5][1:2] + tile[5][2:3]
        out[32:40, lanes] = jnp.broadcast_to(skip, (8, LANES))


def project_kernel(
    *refs,
):
    arrays, refs = refs[:PIECE_ARRAYS], refs[PIECE_ARRAYS:]
    halo, planes, refs = refs[:2], refs[2:4], refs[4:]
    taps, query_ref, carried_ref, chunk_ref, state_ref, rates = refs[:6]
    lhs, w, proj, decay_s, carry = refs[6:]
    place_weights(planes, w)
    place_rows(arrays, halo, lhs)
    decode(planes[0], rates)
    decay_s[...] = jnp.exp(-rates[0:16, :])
    for s in (1, 2, 0):
        cols = slice(s * CH, (s + 1) * CH)
        product = jnp.dot(lhs[...], w[:, cols], preferred_element_type=F32).astype(BF16)
        if s == 0:
            query_ref[...] = product
        else:
            proj[:, (s - 1) * CH : s * CH] = product.astype(F32)

    sub = lax.broadcasted_iota(jnp.int32, (8, LANES), 0)

    def down(v, by):
        return jnp.where(sub >= by, pltpu.roll(v, by, 0), 0.0)

    @pl.loop(0, CH // LANES)
    def _(l):
        lane0 = pl.multiple_of(l * LANES, LANES)
        here = pl.ds(lane0, LANES)
        carry[...] = jnp.zeros_like(carry)

        @pl.loop(0, PIECES)
        def _(p):
            row0 = pl.multiple_of(p * HERE, 16)

            def featured(s):
                lanes = pl.ds(pl.multiple_of(s * CH + lane0, LANES), LANES)
                first = pl.ds(pl.multiple_of((s + 1) * CH + lane0, LANES), LANES)
                ext = [proj[pl.ds(row0 + 8 * i, 8), lanes] for i in range(2 + CHUNK)]
                return filtered(ext, [taps[i : i + 1, first] for i in range(3)], sub)

            keys, values = featured(0), featured(1)
            pairs = [(a * b).astype(BF16) for a, b in zip(keys, values)]
            for j in range(0, CHUNK, 2):
                carried_ref[pl.ds(pl.multiple_of(row0 + 8 * j, 16), 16), here] = jnp.concatenate(
                    pairs[j : j + 2], axis=0
                )
            carried = [a.astype(F32) for a in pairs]

            for m in range(POLES):
                e = decay_s[m : m + 1, here]
                s = carried[0]
                for j in range(1, CHUNK):
                    s = s * e + carried[j]
                a1 = jnp.exp(-float(CHUNK) * rates[m : m + 1, here])
                a2 = a1 * a1
                a4 = a2 * a2
                s = s + a1 * down(s, 1)
                s = s + a2 * down(s, 2)
                s = s + a4 * down(s, 4)
                start = carry[m]
                s = s + jnp.exp(
                    -float(CHUNK) * rates[m : m + 1, here] * (sub + 1).astype(F32)
                ) * start
                chunk_ref[m, pl.ds(pl.multiple_of(p * 8, 8), 8), here] = jnp.where(
                    sub == 0, start, pltpu.roll(s, 1, 0)
                )
                carry[m] = jnp.broadcast_to(s[7:8, :], (8, LANES))

        for m in range(POLES):
            for i in range(NZ):
                state_ref[i, m : m + 1, here] = carry[m, 0:1, :]


def project(arrays, halo, weights, taps):
    vmem = pl.BlockSpec(memory_space=pltpu.VMEM)
    return pl.pallas_call(
        project_kernel,
        in_specs=[vmem] * (PIECE_ARRAYS + 5),
        out_specs=[vmem] * 5,
        out_shape=[
            jax.ShapeDtypeStruct((ROWS, CH), BF16),
            jax.ShapeDtypeStruct((SPAN, CH), BF16),
            jax.ShapeDtypeStruct((POLES, SPAN // CHUNK, CH), F32),
            jax.ShapeDtypeStruct((NZ, POLES, CH), F32),
            jax.ShapeDtypeStruct((40, CH), F32),
        ],
        scratch_shapes=[
            pltpu.VMEM((ROWS, D), BF16),
            pltpu.VMEM((D, COLS), BF16),
            pltpu.VMEM((ROWS, 2 * CH), F32),
            pltpu.VMEM((POLES, CH), F32),
            pltpu.VMEM((POLES, 8, LANES), F32),
        ],
        compiler_params=params(36),
        cost_estimate=pl.CostEstimate(
            flops=2 * ROWS * D * COLS, bytes_accessed=10_000_000, transcendentals=0
        ),
    )(*arrays, *halo, *weights, taps)


def direct_kernel(query, carried, taps, table, gate_ref, local_ref, taps_s):
    rate = table[0:16, :]
    decay = jnp.exp(-rate)
    power = table[16:32, :] * jnp.sqrt(2.0 * rate)
    skip = table[32:33, :]
    for i in range(CHUNK):
        row = jnp.sum(power, axis=0, keepdims=True)
        taps_s[i : i + 1, :] = row + skip if i == 0 else row
        power = power * decay
    sub = lax.broadcasted_iota(jnp.int32, (8, LANES), 0)

    @pl.loop(0, CH // LANES)
    def _(l):
        here = pl.ds(pl.multiple_of(l * LANES, LANES), LANES)

        @pl.loop(0, PIECES)
        def _(p):
            row0 = pl.multiple_of(p * HERE, 16)

            t = [taps[i : i + 1, here] for i in range(3)]

            def rows(ref, count):
                pairs = [
                    ref[pl.ds(pl.multiple_of(row0 + 16 * i, 16), 16), here].astype(F32)
                    for i in range(count)
                ]
                return [half for pair in pairs for half in (pair[:8], pair[8:])]

            queries = filtered(rows(query, 9), t, sub)
            for j in range(0, CHUNK, 2):
                gate_ref[pl.ds(pl.multiple_of(row0 + 8 * j, 16), 16), here] = jnp.concatenate(
                    queries[j : j + 2], axis=0
                ).astype(BF16)
            x = rows(carried, 8)
            k = [taps_s[i : i + 1, here] for i in range(CHUNK)]
            for j in range(CHUNK):
                acc = k[0] * x[j]
                for i in range(j):
                    acc = acc + k[j - i] * x[i]
                local_ref[pl.ds(row0 + 8 * j, 8), here] = acc


def direct(query, carried, taps, table):
    vmem = pl.BlockSpec(memory_space=pltpu.VMEM)
    return pl.pallas_call(
        direct_kernel,
        in_specs=[vmem] * 4,
        out_specs=[vmem] * 2,
        out_shape=[
            jax.ShapeDtypeStruct((SPAN, CH), BF16),
            jax.ShapeDtypeStruct((SPAN, CH), F32),
        ],
        scratch_shapes=[pltpu.VMEM((CHUNK, CH), F32)],
        compiler_params=params(10),
        cost_estimate=pl.CostEstimate(
            flops=40 * SPAN * CH, bytes_accessed=3_000_000, transcendentals=0
        ),
    )(query, carried, taps, table)


def finish_kernel(
    states, table, local, chunk, gate, out, scr, rates, start_s, decay_s, weight_s
):
    z = lax.axis_index("z")
    rate = table[0:16, :]
    rates[...] = rate
    span = jnp.exp(-float(SPAN) * rate)
    total = jnp.zeros((POLES, CH), F32)
    for i in range(NZ - 1):
        total = jnp.where(i < z, total * span + states[i], total)
    start_s[...] = total
    decay = jnp.exp(-rate)
    decay_s[...] = decay
    weight_s[...] = table[16:32, :] * jnp.sqrt(2.0 * rate) * decay
    sub = lax.broadcasted_iota(jnp.int32, (8, LANES), 0)

    @pl.loop(0, PIECES)
    def _(p):
        @pl.loop(0, CH // LANES)
        def _(l):
            here = pl.ds(pl.multiple_of(l * LANES, LANES), LANES)
            row0 = pl.multiple_of(p * HERE, 16)
            age = -float(CHUNK) * (p * 8 + sub).astype(F32)
            v, e = [], []
            for m in range(POLES):
                fade = jnp.exp(rates[m : m + 1, here] * age)
                at = chunk[m, pl.ds(pl.multiple_of(p * 8, 8), 8), here]
                v.append((at + fade * start_s[m : m + 1, here]) * weight_s[m : m + 1, here])
                e.append(decay_s[m : m + 1, here])
            for j in range(0, CHUNK, 2):
                gates = gate[pl.ds(pl.multiple_of(row0 + 8 * j, 16), 16), here].astype(F32)
                for i in range(2):
                    parts = list(v)
                    while len(parts) > 1:
                        parts = [a + b for a, b in zip(parts[::2], parts[1::2])]
                    response = rounded(local[pl.ds(row0 + 8 * (j + i), 8), here] + parts[0])
                    scr[pl.ds(j + i, 8, stride=CHUNK), :] = gates[8 * i : 8 * i + 8] * response
                    v = [a * b for a, b in zip(v, e)]
            out[p, here, :] = scr[...].T.astype(BF16)


def finish(states, table, local, chunk, gate):
    vmem = pl.BlockSpec(memory_space=pltpu.VMEM)
    return pl.pallas_call(
        finish_kernel,
        in_specs=[vmem] * 5,
        out_specs=vmem,
        out_shape=jax.ShapeDtypeStruct((PIECES, CH, HERE), BF16),
        scratch_shapes=[
            pltpu.VMEM((HERE, LANES), F32),
            pltpu.VMEM((POLES, CH), F32),
            pltpu.VMEM((POLES, CH), F32),
            pltpu.VMEM((POLES, CH), F32),
            pltpu.VMEM((POLES, CH), F32),
        ],
        compiler_params=params(10),
    )(states, table, local, chunk, gate)


def place_kernel(pieces, out):
    for g in range(PIECES):
        for i in range(NZ):
            out[i, g] = pieces[g, 32 * i : 32 * i + 32, :]


def place(pieces):
    out = pl.pallas_call(
        place_kernel,
        out_shape=jax.ShapeDtypeStruct((NZ, PIECES, 32, HERE), BF16),
        compiler_params=params(10),
    )(pieces)
    return out.reshape(1, NZ * PIECES * 32, HERE)


def ring(size, by):
    return [(i, (i + by) % size) for i in range(size)]


def shift(value, axis, by):
    return lax.ppermute(value, axis, ring(lax.axis_size(axis), by))


def spread(value, count=NZ):
    return jnp.broadcast_to(value[None], (count,) + value.shape)


def swap(value, axes):
    return lax.all_to_all(value, axes, split_axis=0, concat_axis=0, tiled=True)


def tail_kernel(own, behind, ahead, mixed, out, sem):
    x = lax.axis_index("x")
    for at, piece in ((3, own), (0, behind), (2, ahead), (1, mixed)):

        @pl.when(x == at)
        def _(piece=piece):
            rows = pl.ds(piece.shape[0] - HALO, HALO)
            copy = pltpu.make_async_copy(piece.at[rows], out, sem)
            copy.start()
            copy.wait()


def last_rows(row):
    any_spec = pl.BlockSpec(memory_space=pl.ANY)
    return pl.pallas_call(
        tail_kernel,
        in_specs=[any_spec] * NX,
        out_specs=any_spec,
        out_shape=jax.ShapeDtypeStruct((HALO, D), BF16),
        scratch_shapes=[pltpu.SemaphoreType.DMA],
        compiler_params=params(10),
    )(*row)


def coded(values, parts):
    out = []
    for _ in range(parts):
        part = lax.reduce_precision(values, 8, 7)
        out.append(part)
        values = values - part
    return out


def body(tokens, norm_gain, in_weight, short_filter, rates, residues, skip):
    x, yh, z = lax.axis_index("x"), lax.axis_index("yh"), lax.axis_index("z")
    together = lax.optimization_barrier

    taps = short_filter.reshape(3, 3, NZ, PIECES, 32)
    taps = lax.dynamic_index_in_dim(taps, yh * NX + x, 3, keepdims=False).reshape(3, COLS)
    skips = jnp.pad(jnp.stack(coded(skip, 3)), ((0, TABLE - 3), (0, 0)))
    mine = jnp.stack(coded(rates.T, 3) + coded(residues.T, 2) + [skips], axis=1)
    mine = jnp.tile(mine, (1, 1, 4)).reshape(TABLE, COLS)
    lane = jnp.arange(COLS)[None, :] % LANES
    mine = jnp.where(lane // 32 == z % 4, mine, 0.0).astype(BF16)

    blocks = in_weight.reshape(8, 3, NZ, PIECES, 32).transpose(3, 0, 1, 2, 4)
    blocks = spread(blocks.reshape(PIECES, 8, COLS), 2).reshape(2 * PIECES, 8, COLS)
    unit = swap(blocks, ("yl", "yh", "x")).reshape(UNIT, COLS)
    unit = jnp.concatenate([unit, mine])
    own = normalise(tokens[0], norm_gain[None, :])
    own, unit, taps = together((own, unit, taps))

    def step(up, down):
        return shift(up, "z", 1), shift(down, "z", -1)

    partner = shift(own, "yh", 1)
    own_1, own_3 = shift(own, "x", 1), shift(own, "x", -1)
    up_1, down_1 = step(unit, unit)
    up_1, down_1, partner, own_1, own_3 = together((up_1, down_1, partner, own_1, own_3))

    mixed_1 = shift(jnp.concatenate([partner, own_1[:HALF]]), "x", 1)
    mixed_3 = shift(jnp.concatenate([partner, own_3[HALF:]]), "x", -1)
    up_2, down_2 = step(up_1, down_1)
    up_3, down_3 = step(up_2, down_2)
    up_4 = shift(up_3, "z", 1)
    up_4, mixed_1, mixed_3 = together((up_4, mixed_1, mixed_3))

    first = shift(mixed_1[:HALF], "x", 1)
    second = shift(mixed_3[HALF:HERE], "x", -1)
    tail = last_rows((own, own_1, own_3, mixed_3))
    halo = [
        lax.ppermute(tail, ("z", "yh"), [(2 * i + 1, 2 * i + 2 + to) for i in range(NZ - 1)])
        for to in range(2)
    ]
    plane = jnp.stack([unit, up_1, up_2, up_3, up_4, down_3, down_2, down_1])
    weights = [plane, shift(plane, "co", 1)]
    arrays = [own, own_1, own_3, partner, mixed_1, mixed_3, first, second]

    query, carried, chunk, state, table = project(arrays, halo, weights, taps)
    states = swap(state, "z")
    gate, local = direct(query, carried, taps, table)
    pieces = finish(states, table, local, chunk, gate)
    return place(swap(pieces, ("yh", "x")))


def solution(mesh):
    fine = Mesh(mesh.devices.reshape(2, 2, NZ, 2, NX), ("yl", "co", "z", "yh", "x"))
    fsdp, ctx = ("yl", "co"), ("z", "yh", "x")
    in_specs = (
        P(fsdp, ctx, None),
        P(),
        P(fsdp + ctx, None),
        P(),
        P(ctx, None),
        P(ctx, None),
        P(ctx),
    )
    return jax.shard_map(
        body, mesh=fine, in_specs=in_specs, out_specs=P(fsdp, None, ctx), check_vma=False
    )
```

```python
import functools

import jax
import jax.numpy as jnp
from jax import lax
from jax.experimental import pallas as pl
from jax.experimental.pallas import tpu as pltpu
from jax.sharding import Mesh, PartitionSpec as P

F32 = jnp.float32
BF16 = jnp.bfloat16
NX, NZ = 4, 8
PIECES = 8
POLES = 16
HERE = 128
CHUNK = 16
LANES = 128
CH = 256
HALO = 16
SPAN = PIECES * HERE
ROWS = HALO + SPAN
D = 2048
UNIT = 128
PLACES = (0, 1, 2, 3, 4, 5, 6, 7)
TABLE = 16
COLS = 3 * CH
MIB = 1024 * 1024


def params(mib):
    return pltpu.CompilerParams(vmem_limit_bytes=mib * MIB)


def coded(values, parts):
    out = []
    for _ in range(parts):
        part = values.astype(BF16).astype(F32)
        out.append(part)
        values = values - part
    return out


def norm_kernel(tok_ref, gain_ref, rates, residues, skip, out_ref, table_ref, scr):
    shape = (TABLE, LANES)
    mine = lax.broadcasted_iota(jnp.int32, shape, 1) // 32 == lax.rem(lax.axis_index("z"), 4)
    row = lax.broadcasted_iota(jnp.int32, shape, 0)
    last = jnp.zeros(shape, F32)
    for i, part in enumerate(coded(skip[...], 3)):
        last = jnp.where(row == i, jnp.broadcast_to(part, shape), last)
    tiles = coded(rates[...], 3) + coded(residues[...], 2) + [last]
    for i, tile in enumerate(tiles):
        table_ref[:, i * LANES : (i + 1) * LANES] = jnp.where(mine, tile, 0.0).astype(BF16)
    x = tok_ref[...].astype(F32)
    inv = lax.rsqrt(jnp.mean(x * x, axis=1, keepdims=True) + 1e-6)
    for k in range(D // LANES):
        lanes = slice(k * LANES, (k + 1) * LANES)
        scr[k] = x[:, lanes] * inv * gain_ref[:, lanes]
    for k in range(D // LANES):
        for j in range(0, CHUNK, 2):
            pair = [scr[k, pl.ds(j + i, 8, stride=CHUNK), :] for i in range(2)]
            out_ref[8 * j : 8 * j + 16, k * LANES : (k + 1) * LANES] = jnp.concatenate(
                pair, axis=0
            ).astype(BF16)


def normalise(tokens, gain, rates, residues, skip):
    wide = [jnp.tile(v, (1, LANES // 32)) for v in (rates.T, residues.T, skip[None, :])]
    return pl.pallas_call(
        norm_kernel,
        out_shape=[
            jax.ShapeDtypeStruct((HERE, D), BF16),
            jax.ShapeDtypeStruct((TABLE, COLS), BF16),
        ],
        scratch_shapes=[pltpu.VMEM((D // LANES, HERE, LANES), F32)],
        compiler_params=params(10),
    )(tokens, gain, *wide)


def columns_kernel(w_ref, out_ref):
    lane = lax.broadcasted_iota(jnp.int32, (8, LANES), 1) // 32
    for s in range(3):
        for half in range(2):
            to = slice(s * CH + half * LANES, s * CH + (half + 1) * LANES)
            for high in range(2):
                tiles = []
                for k in range(4):
                    first = s * NZ * CH + (4 * half + k) * CH + high * LANES
                    tiles.append(w_ref[:, first : first + LANES].astype(F32))
                for low in range(4):
                    total = pltpu.roll(tiles[0], (-32 * low) % LANES, 1)
                    for k in range(1, 4):
                        turned = pltpu.roll(tiles[k], (32 * (k - low)) % LANES, 1)
                        total = jnp.where(lane == k, turned, total)
                    for yl in range(2):
                        out_ref[yl * PIECES + 4 * high + low, :, to] = total.astype(BF16)


def columns_by_place(weight):
    return pl.pallas_call(
        columns_kernel,
        out_shape=jax.ShapeDtypeStruct((2 * PIECES, 8, COLS), BF16),
        compiler_params=params(10),
    )(weight)


def rounded(v):
    return v.astype(BF16).astype(F32)


def filtered(ext, t, sub):
    prev = [
        jnp.where(sub == 0, pltpu.roll(ext[i], 1, 0), pltpu.roll(ext[CHUNK + i], 1, 0))
        for i in range(2)
    ]
    ext = prev + ext[2:]
    return [t[0] * ext[j + 2] + t[1] * ext[j + 1] + t[2] * ext[j] for j in range(CHUNK)]


class Copier:
    def __init__(self, sems):
        self.sems, self.copies = sems, []

    def __call__(self, src, dst):
        c = pltpu.make_async_copy(src, dst, self.sems.at[len(self.copies)])
        c.start()
        self.copies.append(c)

    def one_of(self, which, sources, dst):
        sem = self.sems.at[len(self.copies)]
        for i, src in enumerate(sources):
            c = pltpu.make_async_copy(src, dst, sem)
            pl.when(which == i)(c.start)
        self.copies.append(c)

    def wait(self):
        for c in self.copies:
            c.wait()


HALF = HERE // 2
PIECE_LIST = (
    (0, 0, 0, HERE, 0, 0),
    (0, 1, 0, HERE, 1, 0),
    (0, 3, 0, HERE, 2, 0),
    (1, 0, 0, HERE, 3, 0),
    (1, 1, 0, HERE, 4, 0),
    (0, 2, 0, HALF, 4, HERE),
    (1, 3, 0, HERE, 5, 0),
    (0, 2, HALF, HALF, 5, HERE),
    (1, 2, 0, HALF, 6, 0),
    (1, 2, HALF, HALF, 7, 0),
)
PIECE_ARRAYS = 8


def place_rows(arrays, halo, lhs):
    x, yh = lax.axis_index("x"), lax.axis_index("yh")
    for i, source in enumerate(halo):

        @pl.when(yh == i)
        def _(source=source):
            lhs[0:HALO, :] = source[...]

    for other, by, first, rows, array, at in PIECE_LIST:
        place = lax.rem(yh + other, 2) * NX + lax.rem(x + NX - by, NX)
        row = pl.multiple_of(HALO + place * HERE + first, 16)
        lhs[pl.ds(row, rows), :] = arrays[array][at : at + rows, :]


def place_weights(planes, w):
    z, core = lax.axis_index("z"), lax.axis_index("co")
    for r, plane in enumerate(planes):
        for i, d in enumerate(PLACES):
            row = lax.rem(core + r, 2) * 512 + lax.rem(z + NZ - d, NZ) * 64
            for yl in range(2):
                to = pl.ds(pl.multiple_of(yl * 1024 + row, 64), 64)
                w[to, :] = plane[i, yl * 64 : yl * 64 + 64, :]


def decode(plane, out):
    z = lax.axis_index("z")
    halves = [jnp.zeros((TABLE, COLS), F32)] * 2
    for i, d in enumerate(PLACES):
        block = plane[i, UNIT:, :].astype(F32)
        low = lax.rem(z + NZ - d, NZ) < NZ // 2
        halves[0] = halves[0] + jnp.where(low, block, 0.0)
        halves[1] = halves[1] + jnp.where(low, 0.0, block)
    for h, block in enumerate(halves):
        tile = [block[:, i * LANES : (i + 1) * LANES] for i in range(6)]
        lanes = slice(h * LANES, (h + 1) * LANES)
        out[0:16, lanes] = tile[0] + tile[1] + tile[2]
        out[16:32, lanes] = tile[3] + tile[4]
        skip = tile[5][0:1] + tile[5][1:2] + tile[5][2:3]
        out[32:40, lanes] = jnp.broadcast_to(skip, (8, LANES))


def project_kernel(
    *refs,
):
    arrays, refs = refs[:PIECE_ARRAYS], refs[PIECE_ARRAYS:]
    halo, planes, refs = refs[:2], refs[2:4], refs[4:]
    taps, query_ref, carried_ref, chunk_ref, state_ref, rates = refs[:6]
    lhs, w, proj, decay_s, carry = refs[6:]
    place_weights(planes, w)
    place_rows(arrays, halo, lhs)
    decode(planes[0], rates)
    decay_s[...] = jnp.exp(-rates[0:16, :])
    for s in (1, 2, 0):
        cols = slice(s * CH, (s + 1) * CH)
        product = jnp.dot(lhs[...], w[:, cols], preferred_element_type=F32).astype(BF16)
        if s == 0:
            query_ref[...] = product
        else:
            proj[:, (s - 1) * CH : s * CH] = product.astype(F32)

    sub = lax.broadcasted_iota(jnp.int32, (8, LANES), 0)

    def down(v, by):
        return jnp.where(sub >= by, pltpu.roll(v, by, 0), 0.0)

    @pl.loop(0, CH // LANES)
    def _(l):
        lane0 = pl.multiple_of(l * LANES, LANES)
        here = pl.ds(lane0, LANES)
        carry[...] = jnp.zeros_like(carry)

        @pl.loop(0, PIECES)
        def _(p):
            row0 = pl.multiple_of(p * HERE, 16)

            def featured(s):
                lanes = pl.ds(pl.multiple_of(s * CH + lane0, LANES), LANES)
                first = pl.ds(pl.multiple_of((s + 1) * CH + lane0, LANES), LANES)
                ext = [proj[pl.ds(row0 + 8 * i, 8), lanes] for i in range(2 + CHUNK)]
                return filtered(ext, [taps[i : i + 1, first] for i in range(3)], sub)

            keys, values = featured(0), featured(1)
            pairs = [(a * b).astype(BF16) for a, b in zip(keys, values)]
            for j in range(0, CHUNK, 2):
                carried_ref[pl.ds(pl.multiple_of(row0 + 8 * j, 16), 16), here] = jnp.concatenate(
                    pairs[j : j + 2], axis=0
                )
            carried = [a.astype(F32) for a in pairs]

            for m in range(POLES):
                e = decay_s[m : m + 1, here]
                s = carried[0]
                for j in range(1, CHUNK):
                    s = s * e + carried[j]
                a1 = jnp.exp(-float(CHUNK) * rates[m : m + 1, here])
                a2 = a1 * a1
                a4 = a2 * a2
                s = s + a1 * down(s, 1)
                s = s + a2 * down(s, 2)
                s = s + a4 * down(s, 4)
                start = carry[m]
                s = s + jnp.exp(
                    -float(CHUNK) * rates[m : m + 1, here] * (sub + 1).astype(F32)
                ) * start
                chunk_ref[m, pl.ds(pl.multiple_of(p * 8, 8), 8), here] = jnp.where(
                    sub == 0, start, pltpu.roll(s, 1, 0)
                )
                carry[m] = jnp.broadcast_to(s[7:8, :], (8, LANES))

        for m in range(POLES):
            for i in range(NZ):
                state_ref[i, m : m + 1, here] = carry[m, 0:1, :]


def project(arrays, halo, weights, taps):
    vmem = pl.BlockSpec(memory_space=pltpu.VMEM)
    return pl.pallas_call(
        project_kernel,
        in_specs=[vmem] * (PIECE_ARRAYS + 5),
        out_specs=[vmem] * 5,
        out_shape=[
            jax.ShapeDtypeStruct((ROWS, CH), BF16),
            jax.ShapeDtypeStruct((SPAN, CH), BF16),
            jax.ShapeDtypeStruct((POLES, SPAN // CHUNK, CH), F32),
            jax.ShapeDtypeStruct((NZ, POLES, CH), F32),
            jax.ShapeDtypeStruct((40, CH), F32),
        ],
        scratch_shapes=[
            pltpu.VMEM((ROWS, D), BF16),
            pltpu.VMEM((D, COLS), BF16),
            pltpu.VMEM((ROWS, 2 * CH), F32),
            pltpu.VMEM((POLES, CH), F32),
            pltpu.VMEM((POLES, 8, LANES), F32),
        ],
        compiler_params=params(36),
        cost_estimate=pl.CostEstimate(
            flops=2 * ROWS * D * COLS, bytes_accessed=10_000_000, transcendentals=0
        ),
    )(*arrays, *halo, *weights, taps)


def direct_kernel(query, carried, taps, table, gate_ref, local_ref, taps_s):
    rate = table[0:16, :]
    decay = jnp.exp(-rate)
    power = table[16:32, :] * jnp.sqrt(2.0 * rate)
    skip = table[32:33, :]
    for i in range(CHUNK):
        row = jnp.sum(power, axis=0, keepdims=True)
        taps_s[i : i + 1, :] = row + skip if i == 0 else row
        power = power * decay
    sub = lax.broadcasted_iota(jnp.int32, (8, LANES), 0)

    @pl.loop(0, CH // LANES)
    def _(l):
        here = pl.ds(pl.multiple_of(l * LANES, LANES), LANES)

        @pl.loop(0, PIECES)
        def _(p):
            row0 = pl.multiple_of(p * HERE, 16)

            t = [taps[i : i + 1, here] for i in range(3)]

            def rows(ref, count):
                pairs = [
                    ref[pl.ds(pl.multiple_of(row0 + 16 * i, 16), 16), here].astype(F32)
                    for i in range(count)
                ]
                return [half for pair in pairs for half in (pair[:8], pair[8:])]

            queries = filtered(rows(query, 9), t, sub)
            for j in range(0, CHUNK, 2):
                gate_ref[pl.ds(pl.multiple_of(row0 + 8 * j, 16), 16), here] = jnp.concatenate(
                    queries[j : j + 2], axis=0
                ).astype(BF16)
            x = rows(carried, 8)
            k = [taps_s[i : i + 1, here] for i in range(CHUNK)]
            for j in range(CHUNK):
                acc = k[0] * x[j]
                for i in range(j):
                    acc = acc + k[j - i] * x[i]
                local_ref[pl.ds(row0 + 8 * j, 8), here] = acc


def direct(query, carried, taps, table):
    vmem = pl.BlockSpec(memory_space=pltpu.VMEM)
    return pl.pallas_call(
        direct_kernel,
        in_specs=[vmem] * 4,
        out_specs=[vmem] * 2,
        out_shape=[
            jax.ShapeDtypeStruct((SPAN, CH), BF16),
            jax.ShapeDtypeStruct((SPAN, CH), F32),
        ],
        scratch_shapes=[pltpu.VMEM((CHUNK, CH), F32)],
        compiler_params=params(10),
        cost_estimate=pl.CostEstimate(
            flops=40 * SPAN * CH, bytes_accessed=3_000_000, transcendentals=0
        ),
    )(query, carried, taps, table)


def finish_kernel(
    states, table, local, chunk, gate, out, scr, rates, start_s, decay_s, weight_s
):
    z = lax.axis_index("z")
    rate = table[0:16, :]
    rates[...] = rate
    span = jnp.exp(-float(SPAN) * rate)
    total = jnp.zeros((POLES, CH), F32)
    for i in range(NZ - 1):
        total = jnp.where(i < z, total * span + states[i], total)
    start_s[...] = total
    decay = jnp.exp(-rate)
    decay_s[...] = decay
    weight_s[...] = table[16:32, :] * jnp.sqrt(2.0 * rate) * decay
    sub = lax.broadcasted_iota(jnp.int32, (8, LANES), 0)

    @pl.loop(0, PIECES)
    def _(p):
        @pl.loop(0, CH // LANES)
        def _(l):
            here = pl.ds(pl.multiple_of(l * LANES, LANES), LANES)
            row0 = pl.multiple_of(p * HERE, 16)
            age = -float(CHUNK) * (p * 8 + sub).astype(F32)
            v, e = [], []
            for m in range(POLES):
                fade = jnp.exp(rates[m : m + 1, here] * age)
                at = chunk[m, pl.ds(pl.multiple_of(p * 8, 8), 8), here]
                v.append((at + fade * start_s[m : m + 1, here]) * weight_s[m : m + 1, here])
                e.append(decay_s[m : m + 1, here])
            for j in range(0, CHUNK, 2):
                gates = gate[pl.ds(pl.multiple_of(row0 + 8 * j, 16), 16), here].astype(F32)
                for i in range(2):
                    parts = list(v)
                    while len(parts) > 1:
                        parts = [a + b for a, b in zip(parts[::2], parts[1::2])]
                    response = rounded(local[pl.ds(row0 + 8 * (j + i), 8), here] + parts[0])
                    scr[pl.ds(j + i, 8, stride=CHUNK), :] = gates[8 * i : 8 * i + 8] * response
                    v = [a * b for a, b in zip(v, e)]
            out[p, here, :] = scr[...].T.astype(BF16)


def finish(states, table, local, chunk, gate):
    vmem = pl.BlockSpec(memory_space=pltpu.VMEM)
    return pl.pallas_call(
        finish_kernel,
        in_specs=[vmem] * 5,
        out_specs=vmem,
        out_shape=jax.ShapeDtypeStruct((PIECES, CH, HERE), BF16),
        scratch_shapes=[
            pltpu.VMEM((HERE, LANES), F32),
            pltpu.VMEM((POLES, CH), F32),
            pltpu.VMEM((POLES, CH), F32),
            pltpu.VMEM((POLES, CH), F32),
            pltpu.VMEM((POLES, CH), F32),
        ],
        compiler_params=params(10),
    )(states, table, local, chunk, gate)


def place_kernel(pieces, out):
    for g in range(PIECES):
        for i in range(NZ):
            out[i, g] = pieces[g, 32 * i : 32 * i + 32, :]


def place(pieces):
    out = pl.pallas_call(
        place_kernel,
        out_shape=jax.ShapeDtypeStruct((NZ, PIECES, 32, HERE), BF16),
        compiler_params=params(10),
    )(pieces)
    return out.reshape(1, NZ * PIECES * 32, HERE)


def ring(size, by):
    return [(i, (i + by) % size) for i in range(size)]


def shift(value, axis, by):
    return lax.ppermute(value, axis, ring(lax.axis_size(axis), by))


def spread(value, count=NZ):
    return jnp.broadcast_to(value[None], (count,) + value.shape)


def swap(value, axes):
    return lax.all_to_all(value, axes, split_axis=0, concat_axis=0, tiled=True)


def tail_kernel(own, behind, ahead, mixed, out, sem):
    x = lax.axis_index("x")
    for at, piece in ((3, own), (0, behind), (2, ahead), (1, mixed)):

        @pl.when(x == at)
        def _(piece=piece):
            rows = pl.ds(piece.shape[0] - HALO, HALO)
            copy = pltpu.make_async_copy(piece.at[rows], out, sem)
            copy.start()
            copy.wait()


def last_rows(row):
    any_spec = pl.BlockSpec(memory_space=pl.ANY)
    return pl.pallas_call(
        tail_kernel,
        in_specs=[any_spec] * NX,
        out_specs=any_spec,
        out_shape=jax.ShapeDtypeStruct((HALO, D), BF16),
        scratch_shapes=[pltpu.SemaphoreType.DMA],
        compiler_params=params(10),
    )(*row)


def body(tokens, norm_gain, in_weight, short_filter, rates, residues, skip):
    x, yh, z = lax.axis_index("x"), lax.axis_index("yh"), lax.axis_index("z")
    together = lax.optimization_barrier

    taps = short_filter.reshape(3, 3, NZ, PIECES, 32)
    taps = lax.dynamic_index_in_dim(taps, yh * NX + x, 3, keepdims=False).reshape(3, COLS)
    blocks = columns_by_place(in_weight)
    unit = swap(blocks, ("yl", "yh", "x")).reshape(UNIT, COLS)
    own, mine = normalise(tokens[0], norm_gain[None, :], rates, residues, skip)
    own, unit, taps = together((own, jnp.concatenate([unit, mine]), taps))

    def step(up, down):
        return shift(up, "z", 1), shift(down, "z", -1)

    partner = shift(own, "yh", 1)
    own_1, own_3 = shift(own, "x", 1), shift(own, "x", -1)
    up_1, down_1 = step(unit, unit)
    up_2, down_2 = step(up_1, down_1)
    up_2, down_2, partner, own_1, own_3 = together((up_2, down_2, partner, own_1, own_3))

    mixed_1 = shift(jnp.concatenate([partner, own_1[:HALF]]), "x", 1)
    mixed_3 = shift(jnp.concatenate([partner, own_3[HALF:]]), "x", -1)
    up_3, down_3 = step(up_2, down_2)
    up_4 = shift(up_3, "z", 1)
    up_4, mixed_1, mixed_3 = together((up_4, mixed_1, mixed_3))

    first = shift(mixed_1[:HALF], "x", 1)
    second = shift(mixed_3[HALF:HERE], "x", -1)
    tail = last_rows((own, own_1, own_3, mixed_3))
    halo = [
        lax.ppermute(tail, ("z", "yh"), [(2 * i + 1, 2 * i + 2 + to) for i in range(NZ - 1)])
        for to in range(2)
    ]
    plane = jnp.stack([unit, up_1, up_2, up_3, up_4, down_3, down_2, down_1])
    weights = [plane, shift(plane, "co", 1)]
    arrays = [own, own_1, own_3, partner, mixed_1, mixed_3, first, second]

    query, carried, chunk, state, table = project(arrays, halo, weights, taps)
    states = swap(state, "z")
    gate, local = direct(query, carried, taps, table)
    pieces = finish(states, table, local, chunk, gate)
    return place(swap(pieces, ("yh", "x")))


def solution(mesh):
    fine = Mesh(mesh.devices.reshape(2, 2, NZ, 2, NX), ("yl", "co", "z", "yh", "x"))
    fsdp, ctx = ("yl", "co"), ("z", "yh", "x")
    in_specs = (
        P(fsdp, ctx, None),
        P(),
        P(fsdp + ctx, None),
        P(),
        P(ctx, None),
        P(ctx, None),
        P(ctx),
    )
    return jax.shard_map(
        body, mesh=fine, in_specs=in_specs, out_specs=P(fsdp, None, ctx), check_vma=False
    )
```

```python
import functools

import jax
import jax.numpy as jnp
from jax import lax
from jax.experimental import pallas as pl
from jax.experimental.pallas import tpu as pltpu
from jax.sharding import Mesh, PartitionSpec as P

F32 = jnp.float32
BF16 = jnp.bfloat16
NX, NZ = 4, 8
PIECES = 8
POLES = 16
HERE = 128
CHUNK = 16
LANES = 128
CH = 256
HALO = 16
SPAN = PIECES * HERE
ROWS = HALO + SPAN
D = 2048
UNIT = 128
PLACES = (0, 1, 2, 3, 4, 5, 6, 7)
TABLE = 16
COLS = 3 * CH
MIB = 1024 * 1024


def params(mib):
    return pltpu.CompilerParams(vmem_limit_bytes=mib * MIB)


def coded(values, parts):
    out = []
    for _ in range(parts):
        part = values.astype(BF16).astype(F32)
        out.append(part)
        values = values - part
    return out


def norm_kernel(tok_ref, gain_ref, rates, residues, skip, out_ref, table_ref, scr):
    shape = (TABLE, LANES)
    mine = lax.broadcasted_iota(jnp.int32, shape, 1) // 32 == lax.rem(lax.axis_index("z"), 4)
    row = lax.broadcasted_iota(jnp.int32, shape, 0)
    last = jnp.zeros(shape, F32)
    for i, part in enumerate(coded(skip[...], 3)):
        last = jnp.where(row == i, jnp.broadcast_to(part, shape), last)
    tiles = coded(rates[...], 3) + coded(residues[...], 2) + [last]
    for i, tile in enumerate(tiles):
        table_ref[:, i * LANES : (i + 1) * LANES] = jnp.where(mine, tile, 0.0).astype(BF16)
    x = tok_ref[...].astype(F32)
    inv = lax.rsqrt(jnp.mean(x * x, axis=1, keepdims=True) + 1e-6)
    for k in range(D // LANES):
        lanes = slice(k * LANES, (k + 1) * LANES)
        scr[k] = x[:, lanes] * inv * gain_ref[:, lanes]
    for k in range(D // LANES):
        for j in range(0, CHUNK, 2):
            pair = [scr[k, pl.ds(j + i, 8, stride=CHUNK), :] for i in range(2)]
            out_ref[8 * j : 8 * j + 16, k * LANES : (k + 1) * LANES] = jnp.concatenate(
                pair, axis=0
            ).astype(BF16)


def normalise(tokens, gain, rates, residues, skip):
    wide = [jnp.tile(v, (1, LANES // 32)) for v in (rates.T, residues.T, skip[None, :])]
    return pl.pallas_call(
        norm_kernel,
        out_shape=[
            jax.ShapeDtypeStruct((HERE, D), BF16),
            jax.ShapeDtypeStruct((TABLE, COLS), BF16),
        ],
        scratch_shapes=[pltpu.VMEM((D // LANES, HERE, LANES), F32)],
        compiler_params=params(10),
    )(tokens, gain, *wide)


def columns_kernel(w_ref, out_ref):
    lane = lax.broadcasted_iota(jnp.int32, (8, LANES), 1) // 32
    for s in range(3):
        for half in range(2):
            to = slice(s * CH + half * LANES, s * CH + (half + 1) * LANES)
            for high in range(2):
                tiles = []
                for k in range(4):
                    first = s * NZ * CH + (4 * half + k) * CH + high * LANES
                    tiles.append(w_ref[:, first : first + LANES].astype(F32))
                for low in range(4):
                    total = pltpu.roll(tiles[0], (-32 * low) % LANES, 1)
                    for k in range(1, 4):
                        turned = pltpu.roll(tiles[k], (32 * (k - low)) % LANES, 1)
                        total = jnp.where(lane == k, turned, total)
                    for yl in range(2):
                        out_ref[yl * PIECES + 4 * high + low, :, to] = total.astype(BF16)


def columns_by_place(weight):
    return pl.pallas_call(
        columns_kernel,
        out_shape=jax.ShapeDtypeStruct((2 * PIECES, 8, COLS), BF16),
        compiler_params=params(10),
    )(weight)


def rounded(v):
    return v.astype(BF16).astype(F32)


def filtered(ext, t, sub):
    prev = [
        jnp.where(sub == 0, pltpu.roll(ext[i], 1, 0), pltpu.roll(ext[CHUNK + i], 1, 0))
        for i in range(2)
    ]
    ext = prev + ext[2:]
    return [t[0] * ext[j + 2] + t[1] * ext[j + 1] + t[2] * ext[j] for j in range(CHUNK)]


class Copier:
    def __init__(self, sems):
        self.sems, self.copies = sems, []

    def __call__(self, src, dst):
        c = pltpu.make_async_copy(src, dst, self.sems.at[len(self.copies)])
        c.start()
        self.copies.append(c)

    def one_of(self, which, sources, dst):
        sem = self.sems.at[len(self.copies)]
        for i, src in enumerate(sources):
            c = pltpu.make_async_copy(src, dst, sem)
            pl.when(which == i)(c.start)
        self.copies.append(c)

    def wait(self):
        for c in self.copies:
            c.wait()


HALF = HERE // 2
PIECE_LIST = (
    (0, 0, 0, HERE, 0, 0),
    (0, 1, 0, HERE, 1, 0),
    (0, 3, 0, HERE, 2, 0),
    (1, 0, 0, HERE, 3, 0),
    (1, 1, 0, HERE, 4, 0),
    (0, 2, 0, HALF, 4, HERE),
    (1, 3, 0, HERE, 5, 0),
    (0, 2, HALF, HALF, 5, HERE),
)
PIECE_ARRAYS = 6


def place_rows(arrays, lhs):
    x, yh = lax.axis_index("x"), lax.axis_index("yh")
    for other, by, first, rows, array, at in PIECE_LIST:
        place = lax.rem(yh + other, 2) * NX + lax.rem(x + NX - by, NX)
        row = pl.multiple_of(place * HERE + first, 16)
        lhs[pl.ds(row, rows), :] = arrays[array][at : at + rows, :]


def place_weights(planes, w):
    z, core = lax.axis_index("z"), lax.axis_index("co")
    for r, plane in enumerate(planes):
        for i, d in enumerate(PLACES):
            row = lax.rem(core + r, 2) * 512 + lax.rem(z + NZ - d, NZ) * 64
            for yl in range(2):
                to = pl.ds(pl.multiple_of(yl * 1024 + row, 64), 64)
                w[to, :] = plane[i, yl * 64 : yl * 64 + 64, :]


def decode(plane, out):
    z = lax.axis_index("z")
    halves = [jnp.zeros((TABLE, COLS), F32)] * 2
    for i, d in enumerate(PLACES):
        block = plane[i, UNIT:, :].astype(F32)
        low = lax.rem(z + NZ - d, NZ) < NZ // 2
        halves[0] = halves[0] + jnp.where(low, block, 0.0)
        halves[1] = halves[1] + jnp.where(low, 0.0, block)
    for h, block in enumerate(halves):
        tile = [block[:, i * LANES : (i + 1) * LANES] for i in range(6)]
        lanes = slice(h * LANES, (h + 1) * LANES)
        out[0:16, lanes] = tile[0] + tile[1] + tile[2]
        out[16:32, lanes] = tile[3] + tile[4]
        skip = tile[5][0:1] + tile[5][1:2] + tile[5][2:3]
        out[32:40, lanes] = jnp.broadcast_to(skip, (8, LANES))


def multiply_kernel(*refs):
    arrays, refs = refs[:PIECE_ARRAYS], refs[PIECE_ARRAYS:]
    planes, (w, proj, rates, lhs) = refs[:2], refs[2:]
    place_weights(planes, w)
    place_rows(arrays, lhs)
    decode(planes[0], rates)
    for s in range(3):
        cols = slice(s * CH, (s + 1) * CH)
        product = jnp.dot(lhs[...], w[:, cols], preferred_element_type=F32)
        proj[:, cols] = product.astype(BF16)


def multiply(arrays, weights):
    vmem = pl.BlockSpec(memory_space=pltpu.VMEM)
    return pl.pallas_call(
        multiply_kernel,
        in_specs=[vmem] * (PIECE_ARRAYS + 2),
        out_specs=[vmem] * 3,
        out_shape=[
            jax.ShapeDtypeStruct((D, COLS), BF16),
            jax.ShapeDtypeStruct((SPAN, COLS), BF16),
            jax.ShapeDtypeStruct((40, CH), F32),
        ],
        scratch_shapes=[pltpu.VMEM((SPAN, D), BF16)],
        compiler_params=params(24),
        cost_estimate=pl.CostEstimate(
            flops=2 * SPAN * D * COLS // 8, bytes_accessed=1_000_000, transcendentals=0
        ),
    )(*arrays, *weights)


def project_kernel(
    first, second, halo_0, halo_1, w, done, taps, rates,
    query_ref, carried_ref, chunk_ref, state_ref,
    lhs, proj, decay_s, carry,
):
    x, yh = lax.axis_index("x"), lax.axis_index("yh")
    for i, source in enumerate((halo_0, halo_1)):

        @pl.when(yh == i)
        def _(source=source):
            lhs[0:HALO, :] = source[...]

    lhs[HALO : HALO + HALF, :] = first[...]
    lhs[HALO + HALF :, :] = second[...]
    decay_s[...] = jnp.exp(-rates[0:16, :])
    place = lax.rem(yh + 1, 2) * NX + lax.rem(x + 2, NX)
    rows = pl.ds(pl.multiple_of(HALO + place * HERE, 16), HERE)
    for s in range(3):
        cols = slice(s * CH, (s + 1) * CH)
        late = jnp.dot(lhs[...], w[:, cols], preferred_element_type=F32).astype(BF16)
        if s == 0:
            query_ref[HALO:, :] = done[:, cols]
            query_ref[0:HALO, :] = late[0:HALO]
            query_ref[rows, :] = late[HALO:]
        else:
            to = slice((s - 1) * CH, s * CH)
            proj[HALO:, to] = done[:, cols].astype(F32)
            proj[0:HALO, to] = late[0:HALO].astype(F32)
            proj[rows, to] = late[HALO:].astype(F32)

    sub = lax.broadcasted_iota(jnp.int32, (8, LANES), 0)

    def down(v, by):
        return jnp.where(sub >= by, pltpu.roll(v, by, 0), 0.0)

    @pl.loop(0, CH // LANES)
    def _(l):
        lane0 = pl.multiple_of(l * LANES, LANES)
        here = pl.ds(lane0, LANES)
        carry[...] = jnp.zeros_like(carry)

        @pl.loop(0, PIECES)
        def _(p):
            row0 = pl.multiple_of(p * HERE, 16)

            def featured(s):
                lanes = pl.ds(pl.multiple_of(s * CH + lane0, LANES), LANES)
                first = pl.ds(pl.multiple_of((s + 1) * CH + lane0, LANES), LANES)
                ext = [proj[pl.ds(row0 + 8 * i, 8), lanes] for i in range(2 + CHUNK)]
                return filtered(ext, [taps[i : i + 1, first] for i in range(3)], sub)

            keys, values = featured(0), featured(1)
            pairs = [(a * b).astype(BF16) for a, b in zip(keys, values)]
            for j in range(0, CHUNK, 2):
                carried_ref[pl.ds(pl.multiple_of(row0 + 8 * j, 16), 16), here] = jnp.concatenate(
                    pairs[j : j + 2], axis=0
                )
            carried = [a.astype(F32) for a in pairs]

            for m in range(POLES):
                e = decay_s[m : m + 1, here]
                s = carried[0]
                for j in range(1, CHUNK):
                    s = s * e + carried[j]
                a1 = jnp.exp(-float(CHUNK) * rates[m : m + 1, here])
                a2 = a1 * a1
                a4 = a2 * a2
                s = s + a1 * down(s, 1)
                s = s + a2 * down(s, 2)
                s = s + a4 * down(s, 4)
                start = carry[m]
                s = s + jnp.exp(
                    -float(CHUNK) * rates[m : m + 1, here] * (sub + 1).astype(F32)
                ) * start
                chunk_ref[m, pl.ds(pl.multiple_of(p * 8, 8), 8), here] = jnp.where(
                    sub == 0, start, pltpu.roll(s, 1, 0)
                )
                carry[m] = jnp.broadcast_to(s[7:8, :], (8, LANES))

        for m in range(POLES):
            for i in range(NZ):
                state_ref[i, m : m + 1, here] = carry[m, 0:1, :]


def project(first, second, halo, w, done, taps, rates):
    vmem = pl.BlockSpec(memory_space=pltpu.VMEM)
    return pl.pallas_call(
        project_kernel,
        in_specs=[vmem] * 8,
        out_specs=[vmem] * 4,
        out_shape=[
            jax.ShapeDtypeStruct((ROWS, CH), BF16),
            jax.ShapeDtypeStruct((SPAN, CH), BF16),
            jax.ShapeDtypeStruct((POLES, SPAN // CHUNK, CH), F32),
            jax.ShapeDtypeStruct((NZ, POLES, CH), F32),
        ],
        scratch_shapes=[
            pltpu.VMEM((HALO + HERE, D), BF16),
            pltpu.VMEM((ROWS, 2 * CH), F32),
            pltpu.VMEM((POLES, CH), F32),
            pltpu.VMEM((POLES, 8, LANES), F32),
        ],
        compiler_params=params(20),
        cost_estimate=pl.CostEstimate(
            flops=2 * (HALO + HERE) * D * COLS, bytes_accessed=7_000_000, transcendentals=0
        ),
    )(first, second, *halo, w, done, taps, rates)


def direct_kernel(query, carried, taps, table, gate_ref, local_ref, taps_s):
    rate = table[0:16, :]
    decay = jnp.exp(-rate)
    power = table[16:32, :] * jnp.sqrt(2.0 * rate)
    skip = table[32:33, :]
    for i in range(CHUNK):
        row = jnp.sum(power, axis=0, keepdims=True)
        taps_s[i : i + 1, :] = row + skip if i == 0 else row
        power = power * decay
    sub = lax.broadcasted_iota(jnp.int32, (8, LANES), 0)

    @pl.loop(0, CH // LANES)
    def _(l):
        here = pl.ds(pl.multiple_of(l * LANES, LANES), LANES)

        @pl.loop(0, PIECES)
        def _(p):
            row0 = pl.multiple_of(p * HERE, 16)

            t = [taps[i : i + 1, here] for i in range(3)]

            def rows(ref, count):
                pairs = [
                    ref[pl.ds(pl.multiple_of(row0 + 16 * i, 16), 16), here].astype(F32)
                    for i in range(count)
                ]
                return [half for pair in pairs for half in (pair[:8], pair[8:])]

            queries = filtered(rows(query, 9), t, sub)
            for j in range(0, CHUNK, 2):
                gate_ref[pl.ds(pl.multiple_of(row0 + 8 * j, 16), 16), here] = jnp.concatenate(
                    queries[j : j + 2], axis=0
                ).astype(BF16)
            x = rows(carried, 8)
            k = [taps_s[i : i + 1, here] for i in range(CHUNK)]
            for j in range(CHUNK):
                acc = k[0] * x[j]
                for i in range(j):
                    acc = acc + k[j - i] * x[i]
                local_ref[pl.ds(row0 + 8 * j, 8), here] = acc


def direct(query, carried, taps, table):
    vmem = pl.BlockSpec(memory_space=pltpu.VMEM)
    return pl.pallas_call(
        direct_kernel,
        in_specs=[vmem] * 4,
        out_specs=[vmem] * 2,
        out_shape=[
            jax.ShapeDtypeStruct((SPAN, CH), BF16),
            jax.ShapeDtypeStruct((SPAN, CH), F32),
        ],
        scratch_shapes=[pltpu.VMEM((CHUNK, CH), F32)],
        compiler_params=params(10),
        cost_estimate=pl.CostEstimate(
            flops=40 * SPAN * CH, bytes_accessed=3_000_000, transcendentals=0
        ),
    )(query, carried, taps, table)


def finish_kernel(
    states, table, local, chunk, gate, out, scr, rates, start_s, decay_s, weight_s
):
    z = lax.axis_index("z")
    rate = table[0:16, :]
    rates[...] = rate
    span = jnp.exp(-float(SPAN) * rate)
    total = jnp.zeros((POLES, CH), F32)
    for i in range(NZ - 1):
        total = jnp.where(i < z, total * span + states[i], total)
    start_s[...] = total
    decay = jnp.exp(-rate)
    decay_s[...] = decay
    weight_s[...] = table[16:32, :] * jnp.sqrt(2.0 * rate) * decay
    sub = lax.broadcasted_iota(jnp.int32, (8, LANES), 0)

    @pl.loop(0, PIECES)
    def _(p):
        @pl.loop(0, CH // LANES)
        def _(l):
            here = pl.ds(pl.multiple_of(l * LANES, LANES), LANES)
            row0 = pl.multiple_of(p * HERE, 16)
            age = -float(CHUNK) * (p * 8 + sub).astype(F32)
            v, e = [], []
            for m in range(POLES):
                fade = jnp.exp(rates[m : m + 1, here] * age)
                at = chunk[m, pl.ds(pl.multiple_of(p * 8, 8), 8), here]
                v.append((at + fade * start_s[m : m + 1, here]) * weight_s[m : m + 1, here])
                e.append(decay_s[m : m + 1, here])
            for j in range(0, CHUNK, 2):
                gates = gate[pl.ds(pl.multiple_of(row0 + 8 * j, 16), 16), here].astype(F32)
                for i in range(2):
                    parts = list(v)
                    while len(parts) > 1:
                        parts = [a + b for a, b in zip(parts[::2], parts[1::2])]
                    response = rounded(local[pl.ds(row0 + 8 * (j + i), 8), here] + parts[0])
                    scr[pl.ds(j + i, 8, stride=CHUNK), :] = gates[8 * i : 8 * i + 8] * response
                    v = [a * b for a, b in zip(v, e)]
            out[p, here, :] = scr[...].T.astype(BF16)


def finish(states, table, local, chunk, gate):
    vmem = pl.BlockSpec(memory_space=pltpu.VMEM)
    return pl.pallas_call(
        finish_kernel,
        in_specs=[vmem] * 5,
        out_specs=vmem,
        out_shape=jax.ShapeDtypeStruct((PIECES, CH, HERE), BF16),
        scratch_shapes=[
            pltpu.VMEM((HERE, LANES), F32),
            pltpu.VMEM((POLES, CH), F32),
            pltpu.VMEM((POLES, CH), F32),
            pltpu.VMEM((POLES, CH), F32),
            pltpu.VMEM((POLES, CH), F32),
        ],
        compiler_params=params(10),
    )(states, table, local, chunk, gate)


def place_kernel(pieces, out):
    for g in range(PIECES):
        for i in range(NZ):
            out[i, g] = pieces[g, 32 * i : 32 * i + 32, :]


def place(pieces):
    out = pl.pallas_call(
        place_kernel,
        out_shape=jax.ShapeDtypeStruct((NZ, PIECES, 32, HERE), BF16),
        compiler_params=params(10),
    )(pieces)
    return out.reshape(1, NZ * PIECES * 32, HERE)


def ring(size, by):
    return [(i, (i + by) % size) for i in range(size)]


def shift(value, axis, by):
    return lax.ppermute(value, axis, ring(lax.axis_size(axis), by))


def spread(value, count=NZ):
    return jnp.broadcast_to(value[None], (count,) + value.shape)


def swap(value, axes):
    return lax.all_to_all(value, axes, split_axis=0, concat_axis=0, tiled=True)


def tail_kernel(own, behind, ahead, mixed, out, sem):
    x = lax.axis_index("x")
    for at, piece in ((3, own), (0, behind), (2, ahead), (1, mixed)):

        @pl.when(x == at)
        def _(piece=piece):
            rows = pl.ds(piece.shape[0] - HALO, HALO)
            copy = pltpu.make_async_copy(piece.at[rows], out, sem)
            copy.start()
            copy.wait()


def last_rows(row):
    any_spec = pl.BlockSpec(memory_space=pl.ANY)
    return pl.pallas_call(
        tail_kernel,
        in_specs=[any_spec] * NX,
        out_specs=any_spec,
        out_shape=jax.ShapeDtypeStruct((HALO, D), BF16),
        scratch_shapes=[pltpu.SemaphoreType.DMA],
        compiler_params=params(10),
    )(*row)


def body(tokens, norm_gain, in_weight, short_filter, rates, residues, skip):
    x, yh, z = lax.axis_index("x"), lax.axis_index("yh"), lax.axis_index("z")
    together = lax.optimization_barrier

    taps = short_filter.reshape(3, 3, NZ, PIECES, 32)
    taps = lax.dynamic_index_in_dim(taps, yh * NX + x, 3, keepdims=False).reshape(3, COLS)
    blocks = columns_by_place(in_weight)
    unit = swap(blocks, ("yl", "yh", "x")).reshape(UNIT, COLS)
    own, mine = normalise(tokens[0], norm_gain[None, :], rates, residues, skip)
    own, unit, taps = together((own, jnp.concatenate([unit, mine]), taps))

    def step(up, down):
        return shift(up, "z", 1), shift(down, "z", -1)

    partner = shift(own, "yh", 1)
    own_1, own_3 = shift(own, "x", 1), shift(own, "x", -1)
    up_1, down_1 = step(unit, unit)
    up_2, down_2 = step(up_1, down_1)
    up_2, down_2, partner, own_1, own_3 = together((up_2, down_2, partner, own_1, own_3))

    mixed_1 = shift(jnp.concatenate([partner, own_1[:HALF]]), "x", 1)
    mixed_3 = shift(jnp.concatenate([partner, own_3[HALF:]]), "x", -1)
    up_3, down_3 = step(up_2, down_2)
    up_4 = shift(up_3, "z", 1)
    up_4, mixed_1, mixed_3 = together((up_4, mixed_1, mixed_3))

    first = shift(mixed_1[:HALF], "x", 1)
    second = shift(mixed_3[HALF:HERE], "x", -1)
    tail = last_rows((own, own_1, own_3, mixed_3))
    halo = [
        lax.ppermute(tail, ("z", "yh"), [(2 * i + 1, 2 * i + 2 + to) for i in range(NZ - 1)])
        for to in range(2)
    ]
    plane = jnp.stack([unit, up_1, up_2, up_3, up_4, down_3, down_2, down_1])
    weights = [plane, shift(plane, "co", 1)]
    arrays = [own, own_1, own_3, partner, mixed_1, mixed_3]

    w, done, table = multiply(arrays, weights)
    query, carried, chunk, state = project(first, second, halo, w, done, taps, table)
    states = swap(state, "z")
    gate, local = direct(query, carried, taps, table)
    pieces = finish(states, table, local, chunk, gate)
    return place(swap(pieces, ("yh", "x")))


def solution(mesh):
    fine = Mesh(mesh.devices.reshape(2, 2, NZ, 2, NX), ("yl", "co", "z", "yh", "x"))
    fsdp, ctx = ("yl", "co"), ("z", "yh", "x")
    in_specs = (
        P(fsdp, ctx, None),
        P(),
        P(fsdp + ctx, None),
        P(),
        P(ctx, None),
        P(ctx, None),
        P(ctx),
    )
    return jax.shard_map(
        body, mesh=fine, in_specs=in_specs, out_specs=P(fsdp, None, ctx), check_vma=False
    )
```

```python
import functools

import jax
import jax.numpy as jnp
from jax import lax
from jax.experimental import pallas as pl
from jax.experimental.pallas import tpu as pltpu
from jax.sharding import Mesh, PartitionSpec as P

F32 = jnp.float32
BF16 = jnp.bfloat16
NX, NZ = 4, 8
PIECES = 8
POLES = 16
HERE = 128
CHUNK = 16
LANES = 128
CH = 256
HALO = 16
SPAN = PIECES * HERE
ROWS = HALO + SPAN
D = 2048
UNIT = 128
PLACES = (0, 1, 2, 3, 4, 5, 6, 7)
TABLE = 16
COLS = 3 * CH
MIB = 1024 * 1024


def params(mib):
    return pltpu.CompilerParams(vmem_limit_bytes=mib * MIB)


def coded(values, parts):
    out = []
    for _ in range(parts):
        part = values.astype(BF16).astype(F32)
        out.append(part)
        values = values - part
    return out


def norm_kernel(tok_ref, gain_ref, rates, residues, skip, out_ref, table_ref, scr):
    shape = (TABLE, LANES)
    mine = lax.broadcasted_iota(jnp.int32, shape, 1) // 32 == lax.rem(lax.axis_index("z"), 4)
    row = lax.broadcasted_iota(jnp.int32, shape, 0)
    last = jnp.zeros(shape, F32)
    for i, part in enumerate(coded(skip[...], 3)):
        last = jnp.where(row == i, jnp.broadcast_to(part, shape), last)
    tiles = coded(rates[...], 3) + coded(residues[...], 2) + [last]
    for i, tile in enumerate(tiles):
        table_ref[:, i * LANES : (i + 1) * LANES] = jnp.where(mine, tile, 0.0).astype(BF16)
    x = tok_ref[...].astype(F32)
    inv = lax.rsqrt(jnp.mean(x * x, axis=1, keepdims=True) + 1e-6)
    for k in range(D // LANES):
        lanes = slice(k * LANES, (k + 1) * LANES)
        scr[k] = x[:, lanes] * inv * gain_ref[:, lanes]
    for k in range(D // LANES):
        for j in range(0, CHUNK, 2):
            pair = [scr[k, pl.ds(j + i, 8, stride=CHUNK), :] for i in range(2)]
            out_ref[8 * j : 8 * j + 16, k * LANES : (k + 1) * LANES] = jnp.concatenate(
                pair, axis=0
            ).astype(BF16)


def normalise(tokens, gain, rates, residues, skip):
    wide = [jnp.tile(v, (1, LANES // 32)) for v in (rates.T, residues.T, skip[None, :])]
    return pl.pallas_call(
        norm_kernel,
        out_shape=[
            jax.ShapeDtypeStruct((HERE, D), BF16),
            jax.ShapeDtypeStruct((TABLE, COLS), BF16),
        ],
        scratch_shapes=[pltpu.VMEM((D // LANES, HERE, LANES), F32)],
        compiler_params=params(10),
    )(tokens, gain, *wide)


def columns_kernel(w_ref, out_ref):
    lane = lax.broadcasted_iota(jnp.int32, (8, LANES), 1) // 32
    for s in range(3):
        for half in range(2):
            to = slice(s * CH + half * LANES, s * CH + (half + 1) * LANES)
            for high in range(2):
                tiles = []
                for k in range(4):
                    first = s * NZ * CH + (4 * half + k) * CH + high * LANES
                    tiles.append(w_ref[:, first : first + LANES].astype(F32))
                for low in range(4):
                    total = pltpu.roll(tiles[0], (-32 * low) % LANES, 1)
                    for k in range(1, 4):
                        turned = pltpu.roll(tiles[k], (32 * (k - low)) % LANES, 1)
                        total = jnp.where(lane == k, turned, total)
                    for yl in range(2):
                        out_ref[yl * PIECES + 4 * high + low, :, to] = total.astype(BF16)


def columns_by_place(weight):
    return pl.pallas_call(
        columns_kernel,
        out_shape=jax.ShapeDtypeStruct((2 * PIECES, 8, COLS), BF16),
        compiler_params=params(10),
    )(weight)


def rounded(v):
    return v.astype(BF16).astype(F32)


def filtered(ext, t, sub):
    prev = [
        jnp.where(sub == 0, pltpu.roll(ext[i], 1, 0), pltpu.roll(ext[CHUNK + i], 1, 0))
        for i in range(2)
    ]
    ext = prev + ext[2:]
    return [t[0] * ext[j + 2] + t[1] * ext[j + 1] + t[2] * ext[j] for j in range(CHUNK)]


class Copier:
    def __init__(self, sems):
        self.sems, self.copies = sems, []

    def __call__(self, src, dst):
        c = pltpu.make_async_copy(src, dst, self.sems.at[len(self.copies)])
        c.start()
        self.copies.append(c)

    def one_of(self, which, sources, dst):
        sem = self.sems.at[len(self.copies)]
        for i, src in enumerate(sources):
            c = pltpu.make_async_copy(src, dst, sem)
            pl.when(which == i)(c.start)
        self.copies.append(c)

    def wait(self):
        for c in self.copies:
            c.wait()


HALF = HERE // 2
PIECE_LIST = (
    (0, 0, 0, HERE, 0, 0),
    (0, 1, 0, HERE, 1, 0),
    (0, 3, 0, HERE, 2, 0),
    (1, 0, 0, HERE, 3, 0),
    (1, 1, 0, HERE, 4, 0),
    (0, 2, 0, HALF, 4, HERE),
    (1, 3, 0, HERE, 5, 0),
    (0, 2, HALF, HALF, 5, HERE),
)
PIECE_ARRAYS = 6


def place_rows(arrays, lhs):
    x, yh = lax.axis_index("x"), lax.axis_index("yh")
    for other, by, first, rows, array, at in PIECE_LIST:
        place = lax.rem(yh + other, 2) * NX + lax.rem(x + NX - by, NX)
        row = pl.multiple_of(place * HERE + first, 16)
        lhs[pl.ds(row, rows), :] = arrays[array][at : at + rows, :]


def place_weights(planes, w):
    z, core = lax.axis_index("z"), lax.axis_index("co")
    for r, plane in enumerate(planes):
        for i, d in enumerate(PLACES):
            row = lax.rem(core + r, 2) * 512 + lax.rem(z + NZ - d, NZ) * 64
            for yl in range(2):
                to = pl.ds(pl.multiple_of(yl * 1024 + row, 64), 64)
                w[to, :] = plane[i, yl * 64 : yl * 64 + 64, :]


def decode(plane, out):
    z = lax.axis_index("z")
    halves = [jnp.zeros((TABLE, COLS), F32)] * 2
    for i, d in enumerate(PLACES):
        block = plane[i, UNIT:, :].astype(F32)
        low = lax.rem(z + NZ - d, NZ) < NZ // 2
        halves[0] = halves[0] + jnp.where(low, block, 0.0)
        halves[1] = halves[1] + jnp.where(low, 0.0, block)
    for h, block in enumerate(halves):
        tile = [block[:, i * LANES : (i + 1) * LANES] for i in range(6)]
        lanes = slice(h * LANES, (h + 1) * LANES)
        out[0:16, lanes] = tile[0] + tile[1] + tile[2]
        out[16:32, lanes] = tile[3] + tile[4]
        skip = tile[5][0:1] + tile[5][1:2] + tile[5][2:3]
        out[32:40, lanes] = jnp.broadcast_to(skip, (8, LANES))


def multiply_kernel(*refs):
    arrays, refs = refs[:PIECE_ARRAYS], refs[PIECE_ARRAYS:]
    planes, (w, proj, rates, lhs) = refs[:2], refs[2:]
    place_weights(planes, w)
    place_rows(arrays, lhs)
    decode(planes[0], rates)
    for s in range(3):
        cols = slice(s * CH, (s + 1) * CH)
        product = jnp.dot(lhs[...], w[:, cols], preferred_element_type=F32)
        proj[:, cols] = product.astype(BF16)


def multiply(arrays, weights):
    vmem = pl.BlockSpec(memory_space=pltpu.VMEM)
    return pl.pallas_call(
        multiply_kernel,
        in_specs=[vmem] * (PIECE_ARRAYS + 2),
        out_specs=[vmem] * 3,
        out_shape=[
            jax.ShapeDtypeStruct((D, COLS), BF16),
            jax.ShapeDtypeStruct((SPAN, COLS), BF16),
            jax.ShapeDtypeStruct((40, CH), F32),
        ],
        scratch_shapes=[pltpu.VMEM((SPAN, D), BF16)],
        compiler_params=params(24),
        cost_estimate=pl.CostEstimate(
            flops=2 * SPAN * D * COLS // 8, bytes_accessed=1_000_000, transcendentals=0
        ),
    )(*arrays, *weights)


def project_kernel(
    first, second, halo_0, halo_1, w, done, taps, rates,
    query_ref, carried_ref, chunk_ref, state_ref,
    lhs, proj, decay_s, carry, fade,
):
    x, yh = lax.axis_index("x"), lax.axis_index("yh")
    for i, source in enumerate((halo_0, halo_1)):

        @pl.when(yh == i)
        def _(source=source):
            lhs[0:HALO, :] = source[...]

    lhs[HALO : HALO + HALF, :] = first[...]
    lhs[HALO + HALF :, :] = second[...]
    decay_s[...] = jnp.exp(-rates[0:16, :])
    place = lax.rem(yh + 1, 2) * NX + lax.rem(x + 2, NX)
    rows = pl.ds(pl.multiple_of(HALO + place * HERE, 16), HERE)
    for s in range(3):
        cols = slice(s * CH, (s + 1) * CH)
        late = jnp.dot(lhs[...], w[:, cols], preferred_element_type=F32).astype(BF16)
        if s == 0:
            query_ref[HALO:, :] = done[:, cols]
            query_ref[0:HALO, :] = late[0:HALO]
            query_ref[rows, :] = late[HALO:]
        else:
            to = slice((s - 1) * CH, s * CH)
            proj[HALO:, to] = done[:, cols].astype(F32)
            proj[0:HALO, to] = late[0:HALO].astype(F32)
            proj[rows, to] = late[HALO:].astype(F32)

    sub = lax.broadcasted_iota(jnp.int32, (8, LANES), 0)

    def down(v, by):
        return jnp.where(sub >= by, pltpu.roll(v, by, 0), 0.0)

    @pl.loop(0, CH // LANES)
    def _(l):
        lane0 = pl.multiple_of(l * LANES, LANES)
        here = pl.ds(lane0, LANES)
        carry[...] = jnp.zeros_like(carry)
        for m in range(POLES):
            fade[m] = jnp.exp(-float(CHUNK) * rates[m : m + 1, here] * (sub + 1).astype(F32))

        for p in range(PIECES):
            row0 = p * HERE

            def featured(s):
                lanes = pl.ds(pl.multiple_of(s * CH + lane0, LANES), LANES)
                first = pl.ds(pl.multiple_of((s + 1) * CH + lane0, LANES), LANES)
                ext = [proj[pl.ds(row0 + 8 * i, 8), lanes] for i in range(2 + CHUNK)]
                return filtered(ext, [taps[i : i + 1, first] for i in range(3)], sub)

            keys, values = featured(0), featured(1)
            pairs = [(a * b).astype(BF16) for a, b in zip(keys, values)]
            for j in range(0, CHUNK, 2):
                carried_ref[pl.ds(row0 + 8 * j, 16), here] = jnp.concatenate(
                    pairs[j : j + 2], axis=0
                )
            carried = [a.astype(F32) for a in pairs]

            for m in range(POLES):
                e = decay_s[m : m + 1, here]
                s = carried[0]
                for j in range(1, CHUNK):
                    s = s * e + carried[j]
                a1 = fade[m, 0:1, :]
                a2 = a1 * a1
                a4 = a2 * a2
                s = s + a1 * down(s, 1)
                s = s + a2 * down(s, 2)
                s = s + a4 * down(s, 4)
                start = carry[m]
                s = s + fade[m] * start
                chunk_ref[m, pl.ds(p * 8, 8), here] = jnp.where(
                    sub == 0, start, pltpu.roll(s, 1, 0)
                )
                carry[m] = jnp.broadcast_to(s[7:8, :], (8, LANES))

        for m in range(POLES):
            for i in range(NZ):
                state_ref[i, m : m + 1, here] = carry[m, 0:1, :]


def project(first, second, halo, w, done, taps, rates):
    vmem = pl.BlockSpec(memory_space=pltpu.VMEM)
    return pl.pallas_call(
        project_kernel,
        in_specs=[vmem] * 8,
        out_specs=[vmem] * 4,
        out_shape=[
            jax.ShapeDtypeStruct((ROWS, CH), BF16),
            jax.ShapeDtypeStruct((SPAN, CH), BF16),
            jax.ShapeDtypeStruct((POLES, SPAN // CHUNK, CH), F32),
            jax.ShapeDtypeStruct((NZ, POLES, CH), F32),
        ],
        scratch_shapes=[
            pltpu.VMEM((HALO + HERE, D), BF16),
            pltpu.VMEM((ROWS, 2 * CH), F32),
            pltpu.VMEM((POLES, CH), F32),
            pltpu.VMEM((POLES, 8, LANES), F32),
            pltpu.VMEM((POLES, 8, LANES), F32),
        ],
        compiler_params=params(20),
        cost_estimate=pl.CostEstimate(
            flops=2 * (HALO + HERE) * D * COLS, bytes_accessed=7_000_000, transcendentals=0
        ),
    )(first, second, *halo, w, done, taps, rates)


def direct_kernel(query, carried, taps, table, gate_ref, local_ref, taps_s):
    rate = table[0:16, :]
    decay = jnp.exp(-rate)
    power = table[16:32, :] * jnp.sqrt(2.0 * rate)
    skip = table[32:33, :]
    for i in range(CHUNK):
        row = jnp.sum(power, axis=0, keepdims=True)
        taps_s[i : i + 1, :] = row + skip if i == 0 else row
        power = power * decay
    sub = lax.broadcasted_iota(jnp.int32, (8, LANES), 0)

    @pl.loop(0, CH // LANES)
    def _(l):
        here = pl.ds(pl.multiple_of(l * LANES, LANES), LANES)

        @pl.loop(0, PIECES)
        def _(p):
            row0 = pl.multiple_of(p * HERE, 16)

            t = [taps[i : i + 1, here] for i in range(3)]

            def rows(ref, count):
                pairs = [
                    ref[pl.ds(pl.multiple_of(row0 + 16 * i, 16), 16), here].astype(F32)
                    for i in range(count)
                ]
                return [half for pair in pairs for half in (pair[:8], pair[8:])]

            queries = filtered(rows(query, 9), t, sub)
            for j in range(0, CHUNK, 2):
                gate_ref[pl.ds(pl.multiple_of(row0 + 8 * j, 16), 16), here] = jnp.concatenate(
                    queries[j : j + 2], axis=0
                ).astype(BF16)
            x = rows(carried, 8)
            k = [taps_s[i : i + 1, here] for i in range(CHUNK)]
            for j in range(CHUNK):
                acc = k[0] * x[j]
                for i in range(j):
                    acc = acc + k[j - i] * x[i]
                local_ref[pl.ds(row0 + 8 * j, 8), here] = acc


def direct(query, carried, taps, table):
    vmem = pl.BlockSpec(memory_space=pltpu.VMEM)
    return pl.pallas_call(
        direct_kernel,
        in_specs=[vmem] * 4,
        out_specs=[vmem] * 2,
        out_shape=[
            jax.ShapeDtypeStruct((SPAN, CH), BF16),
            jax.ShapeDtypeStruct((SPAN, CH), F32),
        ],
        scratch_shapes=[pltpu.VMEM((CHUNK, CH), F32)],
        compiler_params=params(10),
        cost_estimate=pl.CostEstimate(
            flops=40 * SPAN * CH, bytes_accessed=3_000_000, transcendentals=0
        ),
    )(query, carried, taps, table)


def finish_kernel(
    states, table, local, chunk, gate, out, scr, begun, rates, start_s, decay_s, weight_s
):
    z = lax.axis_index("z")
    rate = table[0:16, :]
    rates[...] = rate
    span = jnp.exp(-float(SPAN) * rate)
    total = jnp.zeros((POLES, CH), F32)
    for i in range(NZ - 1):
        total = jnp.where(i < z, total * span + states[i], total)
    start_s[...] = total
    decay = jnp.exp(-rate)
    decay_s[...] = decay
    weight_s[...] = table[16:32, :] * jnp.sqrt(2.0 * rate) * decay
    sub = lax.broadcasted_iota(jnp.int32, (8, LANES), 0)

    @pl.loop(0, CH // LANES)
    def _(l):
        here = pl.ds(pl.multiple_of(l * LANES, LANES), LANES)
        for m in range(POLES):
            fade = jnp.exp(-float(CHUNK) * rates[m : m + 1, here] * sub.astype(F32))
            begun[m] = fade * (start_s[m : m + 1, here] * weight_s[m : m + 1, here])
        for p in range(PIECES):
            row0 = p * HERE
            turned = scr.at[p % 2]
            v, e = [], []
            for m in range(POLES):
                at = chunk[m, p * 8 : p * 8 + 8, here]
                v.append(at * weight_s[m : m + 1, here] + begun[m])
                e.append(decay_s[m : m + 1, here])
                if p + 1 < PIECES:
                    begun[m] = begun[m] * jnp.exp(-float(HERE) * rates[m : m + 1, here])
            for j in range(0, CHUNK, 2):
                gates = gate[row0 + 8 * j : row0 + 8 * j + 16, here].astype(F32)
                for i in range(2):
                    parts = list(v)
                    while len(parts) > 1:
                        parts = [a + b for a, b in zip(parts[::2], parts[1::2])]
                    at = row0 + 8 * (j + i)
                    response = rounded(local[at : at + 8, here] + parts[0])
                    turned[pl.ds(j + i, 8, stride=CHUNK), :] = gates[8 * i : 8 * i + 8] * response
                    v = [a * b for a, b in zip(v, e)]
            out[p, here, :] = turned[...].T.astype(BF16)


def finish(states, table, local, chunk, gate):
    vmem = pl.BlockSpec(memory_space=pltpu.VMEM)
    return pl.pallas_call(
        finish_kernel,
        in_specs=[vmem] * 5,
        out_specs=vmem,
        out_shape=jax.ShapeDtypeStruct((PIECES, CH, HERE), BF16),
        scratch_shapes=[
            pltpu.VMEM((2, HERE, LANES), F32),
            pltpu.VMEM((POLES, 8, LANES), F32),
            pltpu.VMEM((POLES, CH), F32),
            pltpu.VMEM((POLES, CH), F32),
            pltpu.VMEM((POLES, CH), F32),
            pltpu.VMEM((POLES, CH), F32),
        ],
        compiler_params=params(10),
    )(states, table, local, chunk, gate)


def place_kernel(pieces, out):
    for g in range(PIECES):
        for i in range(NZ):
            out[i, g] = pieces[g, 32 * i : 32 * i + 32, :]


def place(pieces):
    out = pl.pallas_call(
        place_kernel,
        out_shape=jax.ShapeDtypeStruct((NZ, PIECES, 32, HERE), BF16),
        compiler_params=params(10),
    )(pieces)
    return out.reshape(1, NZ * PIECES * 32, HERE)


def ring(size, by):
    return [(i, (i + by) % size) for i in range(size)]


def shift(value, axis, by):
    return lax.ppermute(value, axis, ring(lax.axis_size(axis), by))


def spread(value, count=NZ):
    return jnp.broadcast_to(value[None], (count,) + value.shape)


def swap(value, axes):
    return lax.all_to_all(value, axes, split_axis=0, concat_axis=0, tiled=True)


def tail_kernel(own, behind, ahead, mixed, out, sem):
    x = lax.axis_index("x")
    for at, piece in ((3, own), (0, behind), (2, ahead), (1, mixed)):

        @pl.when(x == at)
        def _(piece=piece):
            rows = pl.ds(piece.shape[0] - HALO, HALO)
            copy = pltpu.make_async_copy(piece.at[rows], out, sem)
            copy.start()
            copy.wait()


def last_rows(row):
    any_spec = pl.BlockSpec(memory_space=pl.ANY)
    return pl.pallas_call(
        tail_kernel,
        in_specs=[any_spec] * NX,
        out_specs=any_spec,
        out_shape=jax.ShapeDtypeStruct((HALO, D), BF16),
        scratch_shapes=[pltpu.SemaphoreType.DMA],
        compiler_params=params(10),
    )(*row)


def body(tokens, norm_gain, in_weight, short_filter, rates, residues, skip):
    x, yh, z = lax.axis_index("x"), lax.axis_index("yh"), lax.axis_index("z")
    together = lax.optimization_barrier

    taps = short_filter.reshape(3, 3, NZ, PIECES, 32)
    taps = lax.dynamic_index_in_dim(taps, yh * NX + x, 3, keepdims=False).reshape(3, COLS)
    blocks = columns_by_place(in_weight)
    unit = swap(blocks, ("yl", "yh", "x")).reshape(UNIT, COLS)
    own, mine = normalise(tokens[0], norm_gain[None, :], rates, residues, skip)
    own, unit, taps = together((own, jnp.concatenate([unit, mine]), taps))

    def step(up, down):
        return shift(up, "z", 1), shift(down, "z", -1)

    partner = shift(own, "yh", 1)
    own_1, own_3 = shift(own, "x", 1), shift(own, "x", -1)
    up_1, down_1 = step(unit, unit)
    up_2, down_2 = step(up_1, down_1)
    up_2, down_2, partner, own_1, own_3 = together((up_2, down_2, partner, own_1, own_3))

    mixed_1 = shift(jnp.concatenate([partner, own_1[:HALF]]), "x", 1)
    mixed_3 = shift(jnp.concatenate([partner, own_3[HALF:]]), "x", -1)
    up_3, down_3 = step(up_2, down_2)
    up_4 = shift(up_3, "z", 1)
    up_4, mixed_1, mixed_3 = together((up_4, mixed_1, mixed_3))

    first = shift(mixed_1[:HALF], "x", 1)
    second = shift(mixed_3[HALF:HERE], "x", -1)
    tail = last_rows((own, own_1, own_3, mixed_3))
    halo = [
        lax.ppermute(tail, ("z", "yh"), [(2 * i + 1, 2 * i + 2 + to) for i in range(NZ - 1)])
        for to in range(2)
    ]
    plane = jnp.stack([unit, up_1, up_2, up_3, up_4, down_3, down_2, down_1])
    weights = [plane, shift(plane, "co", 1)]
    arrays = [own, own_1, own_3, partner, mixed_1, mixed_3]

    w, done, table = multiply(arrays, weights)
    query, carried, chunk, state = project(first, second, halo, w, done, taps, table)
    states = swap(state, "z")
    gate, local = direct(query, carried, taps, table)
    pieces = finish(states, table, local, chunk, gate)
    return place(swap(pieces, ("yh", "x")))


def solution(mesh):
    fine = Mesh(mesh.devices.reshape(2, 2, NZ, 2, NX), ("yl", "co", "z", "yh", "x"))
    fsdp, ctx = ("yl", "co"), ("z", "yh", "x")
    in_specs = (
        P(fsdp, ctx, None),
        P(),
        P(fsdp + ctx, None),
        P(),
        P(ctx, None),
        P(ctx, None),
        P(ctx),
    )
    return jax.shard_map(
        body, mesh=fine, in_specs=in_specs, out_specs=P(fsdp, None, ctx), check_vma=False
    )
```

```python
import functools

import jax
import jax.numpy as jnp
from jax import lax
from jax.experimental import pallas as pl
from jax.experimental.pallas import tpu as pltpu
from jax.sharding import Mesh, PartitionSpec as P

F32 = jnp.float32
BF16 = jnp.bfloat16
NX, NZ = 4, 8
PIECES = 8
POLES = 16
HERE = 128
CHUNK = 16
LANES = 128
CH = 256
HALO = 16
SPAN = PIECES * HERE
ROWS = HALO + SPAN
D = 2048
UNIT = 128
PLACES = (0, 1, 2, 3, 4, 5, 6, 7)
TABLE = 16
COLS = 3 * CH
MIB = 1024 * 1024


def params(mib):
    return pltpu.CompilerParams(vmem_limit_bytes=mib * MIB)


def coded(values, parts):
    out = []
    for _ in range(parts):
        part = values.astype(BF16).astype(F32)
        out.append(part)
        values = values - part
    return out


def norm_kernel(tok_ref, gain_ref, rates, residues, skip, out_ref, table_ref, scr):
    shape = (TABLE, LANES)
    mine = lax.broadcasted_iota(jnp.int32, shape, 1) // 32 == lax.rem(lax.axis_index("z"), 4)
    row = lax.broadcasted_iota(jnp.int32, shape, 0)
    last = jnp.zeros(shape, F32)
    for i, part in enumerate(coded(skip[...], 3)):
        last = jnp.where(row == i, jnp.broadcast_to(part, shape), last)
    tiles = coded(rates[...], 3) + coded(residues[...], 2) + [last]
    for i, tile in enumerate(tiles):
        table_ref[:, i * LANES : (i + 1) * LANES] = jnp.where(mine, tile, 0.0).astype(BF16)
    x = tok_ref[...].astype(F32)
    inv = lax.rsqrt(jnp.mean(x * x, axis=1, keepdims=True) + 1e-6)
    for k in range(D // LANES):
        lanes = slice(k * LANES, (k + 1) * LANES)
        scr[k] = x[:, lanes] * inv * gain_ref[:, lanes]
    for k in range(D // LANES):
        for j in range(0, CHUNK, 2):
            pair = [scr[k, pl.ds(j + i, 8, stride=CHUNK), :] for i in range(2)]
            out_ref[8 * j : 8 * j + 16, k * LANES : (k + 1) * LANES] = jnp.concatenate(
                pair, axis=0
            ).astype(BF16)


def normalise(tokens, gain, rates, residues, skip):
    wide = [jnp.tile(v, (1, LANES // 32)) for v in (rates.T, residues.T, skip[None, :])]
    return pl.pallas_call(
        norm_kernel,
        out_shape=[
            jax.ShapeDtypeStruct((HERE, D), BF16),
            jax.ShapeDtypeStruct((TABLE, COLS), BF16),
        ],
        scratch_shapes=[pltpu.VMEM((D // LANES, HERE, LANES), F32)],
        compiler_params=params(10),
    )(tokens, gain, *wide)


def columns_kernel(w_ref, out_ref):
    lane = lax.broadcasted_iota(jnp.int32, (8, LANES), 1) // 32
    for s in range(3):
        for half in range(2):
            to = slice(s * CH + half * LANES, s * CH + (half + 1) * LANES)
            for high in range(2):
                tiles = []
                for k in range(4):
                    first = s * NZ * CH + (4 * half + k) * CH + high * LANES
                    tiles.append(w_ref[:, first : first + LANES].astype(F32))
                for low in range(4):
                    total = pltpu.roll(tiles[0], (-32 * low) % LANES, 1)
                    for k in range(1, 4):
                        turned = pltpu.roll(tiles[k], (32 * (k - low)) % LANES, 1)
                        total = jnp.where(lane == k, turned, total)
                    for yl in range(2):
                        out_ref[yl * PIECES + 4 * high + low, :, to] = total.astype(BF16)


def columns_by_place(weight):
    return pl.pallas_call(
        columns_kernel,
        out_shape=jax.ShapeDtypeStruct((2 * PIECES, 8, COLS), BF16),
        compiler_params=params(10),
    )(weight)


def rounded(v):
    return v.astype(BF16).astype(F32)


def filtered(ext, t, sub):
    prev = [
        jnp.where(sub == 0, pltpu.roll(ext[i], 1, 0), pltpu.roll(ext[CHUNK + i], 1, 0))
        for i in range(2)
    ]
    ext = prev + ext[2:]
    return [t[0] * ext[j + 2] + t[1] * ext[j + 1] + t[2] * ext[j] for j in range(CHUNK)]


class Copier:
    def __init__(self, sems):
        self.sems, self.copies = sems, []

    def __call__(self, src, dst):
        c = pltpu.make_async_copy(src, dst, self.sems.at[len(self.copies)])
        c.start()
        self.copies.append(c)

    def one_of(self, which, sources, dst):
        sem = self.sems.at[len(self.copies)]
        for i, src in enumerate(sources):
            c = pltpu.make_async_copy(src, dst, sem)
            pl.when(which == i)(c.start)
        self.copies.append(c)

    def wait(self):
        for c in self.copies:
            c.wait()


HALF = HERE // 2
PIECE_LIST = (
    (0, 0, 0, HERE, 0, 0),
    (0, 1, 0, HERE, 1, 0),
    (0, 3, 0, HERE, 2, 0),
    (1, 0, 0, HERE, 3, 0),
    (1, 1, 0, HERE, 4, 0),
    (0, 2, 0, HALF, 4, HERE),
    (1, 3, 0, HERE, 5, 0),
    (0, 2, HALF, HALF, 5, HERE),
)
PIECE_ARRAYS = 6


def place_rows(arrays, lhs):
    x, yh = lax.axis_index("x"), lax.axis_index("yh")
    for other, by, first, rows, array, at in PIECE_LIST:
        place = lax.rem(yh + other, 2) * NX + lax.rem(x + NX - by, NX)
        row = pl.multiple_of(place * HERE + first, 16)
        lhs[pl.ds(row, rows), :] = arrays[array][at : at + rows, :]


def place_weights(planes, w):
    z, core = lax.axis_index("z"), lax.axis_index("co")
    for r, plane in enumerate(planes):
        for i, d in enumerate(PLACES):
            row = lax.rem(core + r, 2) * 512 + lax.rem(z + NZ - d, NZ) * 64
            for yl in range(2):
                to = pl.ds(pl.multiple_of(yl * 1024 + row, 64), 64)
                w[to, :] = plane[i, yl * 64 : yl * 64 + 64, :]


def decode(plane, out):
    z = lax.axis_index("z")
    halves = [jnp.zeros((TABLE, COLS), F32)] * 2
    for i, d in enumerate(PLACES):
        block = plane[i, UNIT:, :].astype(F32)
        low = lax.rem(z + NZ - d, NZ) < NZ // 2
        halves[0] = halves[0] + jnp.where(low, block, 0.0)
        halves[1] = halves[1] + jnp.where(low, 0.0, block)
    for h, block in enumerate(halves):
        tile = [block[:, i * LANES : (i + 1) * LANES] for i in range(6)]
        lanes = slice(h * LANES, (h + 1) * LANES)
        out[0:16, lanes] = tile[0] + tile[1] + tile[2]
        out[16:32, lanes] = tile[3] + tile[4]
        skip = tile[5][0:1] + tile[5][1:2] + tile[5][2:3]
        out[32:40, lanes] = jnp.broadcast_to(skip, (8, LANES))


def multiply_kernel(*refs):
    arrays, refs = refs[:PIECE_ARRAYS], refs[PIECE_ARRAYS:]
    planes, (w, proj, rates, lhs) = refs[:2], refs[2:]
    place_weights(planes, w)
    place_rows(arrays, lhs)
    decode(planes[0], rates)
    for s in range(3):
        cols = slice(s * CH, (s + 1) * CH)
        product = jnp.dot(lhs[...], w[:, cols], preferred_element_type=F32)
        proj[:, cols] = product.astype(BF16)


def multiply(arrays, weights):
    vmem = pl.BlockSpec(memory_space=pltpu.VMEM)
    return pl.pallas_call(
        multiply_kernel,
        in_specs=[vmem] * (PIECE_ARRAYS + 2),
        out_specs=[vmem] * 3,
        out_shape=[
            jax.ShapeDtypeStruct((D, COLS), BF16),
            jax.ShapeDtypeStruct((SPAN, COLS), BF16),
            jax.ShapeDtypeStruct((40, CH), F32),
        ],
        scratch_shapes=[pltpu.VMEM((SPAN, D), BF16)],
        compiler_params=params(24),
        cost_estimate=pl.CostEstimate(
            flops=2 * SPAN * D * COLS // 8, bytes_accessed=1_000_000, transcendentals=0
        ),
    )(*arrays, *weights)


def project_kernel(
    first, second, halo_0, halo_1, w, done, taps, rates,
    both_ref, chunk_ref, state_ref,
    lhs, proj, decay_s, carry, fade,
):
    x, yh = lax.axis_index("x"), lax.axis_index("yh")
    for i, source in enumerate((halo_0, halo_1)):

        @pl.when(yh == i)
        def _(source=source):
            lhs[0:HALO, :] = source[...]

    lhs[HALO : HALO + HALF, :] = first[...]
    lhs[HALO + HALF :, :] = second[...]
    decay_s[...] = jnp.exp(-rates[0:16, :])
    place = lax.rem(yh + 1, 2) * NX + lax.rem(x + 2, NX)
    rows = pl.ds(pl.multiple_of(HALO + place * HERE, 16), HERE)
    for s in range(3):
        cols = slice(s * CH, (s + 1) * CH)
        late = jnp.dot(lhs[...], w[:, cols], preferred_element_type=F32).astype(BF16)
        if s == 0:
            both_ref[HALO:ROWS, :] = done[:, cols]
            both_ref[0:HALO, :] = late[0:HALO]
            both_ref[rows, :] = late[HALO:]
        else:
            to = slice((s - 1) * CH, s * CH)
            proj[HALO:, to] = done[:, cols].astype(F32)
            proj[0:HALO, to] = late[0:HALO].astype(F32)
            proj[rows, to] = late[HALO:].astype(F32)

    sub = lax.broadcasted_iota(jnp.int32, (8, LANES), 0)

    def down(v, by):
        return jnp.where(sub >= by, pltpu.roll(v, by, 0), 0.0)

    @pl.loop(0, CH // LANES)
    def _(l):
        lane0 = pl.multiple_of(l * LANES, LANES)
        here = pl.ds(lane0, LANES)
        carry[...] = jnp.zeros_like(carry)
        for m in range(POLES):
            fade[m] = jnp.exp(-float(CHUNK) * rates[m : m + 1, here] * (sub + 1).astype(F32))

        for p in range(PIECES):
            row0 = p * HERE

            def featured(s):
                lanes = pl.ds(pl.multiple_of(s * CH + lane0, LANES), LANES)
                first = pl.ds(pl.multiple_of((s + 1) * CH + lane0, LANES), LANES)
                ext = [proj[pl.ds(row0 + 8 * i, 8), lanes] for i in range(2 + CHUNK)]
                return filtered(ext, [taps[i : i + 1, first] for i in range(3)], sub)

            keys, values = featured(0), featured(1)
            pairs = [(a * b).astype(BF16) for a, b in zip(keys, values)]
            for j in range(0, CHUNK, 2):
                both_ref[pl.ds(ROWS + row0 + 8 * j, 16), here] = jnp.concatenate(
                    pairs[j : j + 2], axis=0
                )
            carried = [a.astype(F32) for a in pairs]

            for m in range(POLES):
                e = decay_s[m : m + 1, here]
                s = carried[0]
                for j in range(1, CHUNK):
                    s = s * e + carried[j]
                a1 = fade[m, 0:1, :]
                a2 = a1 * a1
                a4 = a2 * a2
                s = s + a1 * down(s, 1)
                s = s + a2 * down(s, 2)
                s = s + a4 * down(s, 4)
                start = carry[m]
                s = s + fade[m] * start
                chunk_ref[m, pl.ds(p * 8, 8), here] = jnp.where(
                    sub == 0, start, pltpu.roll(s, 1, 0)
                )
                carry[m] = jnp.broadcast_to(s[7:8, :], (8, LANES))

        for m in range(POLES):
            for i in range(NZ):
                state_ref[i, m : m + 1, here] = carry[m, 0:1, :]


def project(first, second, halo, w, done, taps, rates):
    vmem = pl.BlockSpec(memory_space=pltpu.VMEM)
    return pl.pallas_call(
        project_kernel,
        in_specs=[vmem] * 8,
        out_specs=[vmem] * 3,
        out_shape=[
            jax.ShapeDtypeStruct((ROWS + SPAN, CH), BF16),
            jax.ShapeDtypeStruct((POLES, SPAN // CHUNK, CH), F32),
            jax.ShapeDtypeStruct((NZ, POLES, CH), F32),
        ],
        scratch_shapes=[
            pltpu.VMEM((HALO + HERE, D), BF16),
            pltpu.VMEM((ROWS, 2 * CH), F32),
            pltpu.VMEM((POLES, CH), F32),
            pltpu.VMEM((POLES, 8, LANES), F32),
            pltpu.VMEM((POLES, 8, LANES), F32),
        ],
        compiler_params=params(20),
        cost_estimate=pl.CostEstimate(
            flops=2 * (HALO + HERE) * D * COLS, bytes_accessed=7_000_000, transcendentals=0
        ),
    )(first, second, *halo, w, done, taps, rates)


def direct_kernel(both, taps, table, gate_ref, local_ref, taps_s):
    rate = table[0:16, :]
    decay = jnp.exp(-rate)
    power = table[16:32, :] * jnp.sqrt(2.0 * rate)
    skip = table[32:33, :]
    for i in range(CHUNK):
        row = jnp.sum(power, axis=0, keepdims=True)
        taps_s[i : i + 1, :] = row + skip if i == 0 else row
        power = power * decay
    sub = lax.broadcasted_iota(jnp.int32, (8, LANES), 0)

    @pl.loop(0, CH // LANES)
    def _(l):
        here = pl.ds(pl.multiple_of(l * LANES, LANES), LANES)

        @pl.loop(0, PIECES)
        def _(p):
            row0 = pl.multiple_of(p * HERE, 16)

            t = [taps[i : i + 1, here] for i in range(3)]

            def rows(first, count):
                pairs = [
                    both[pl.ds(pl.multiple_of(first + row0 + 16 * i, 16), 16), here].astype(F32)
                    for i in range(count)
                ]
                return [half for pair in pairs for half in (pair[:8], pair[8:])]

            queries = filtered(rows(0, 9), t, sub)
            for j in range(0, CHUNK, 2):
                gate_ref[pl.ds(pl.multiple_of(row0 + 8 * j, 16), 16), here] = jnp.concatenate(
                    queries[j : j + 2], axis=0
                ).astype(BF16)
            x = rows(ROWS, 8)
            k = [taps_s[i : i + 1, here] for i in range(CHUNK)]
            for j in range(CHUNK):
                acc = k[0] * x[j]
                for i in range(j):
                    acc = acc + k[j - i] * x[i]
                local_ref[pl.ds(row0 + 8 * j, 8), here] = acc


def direct(both, taps, table):
    vmem = pl.BlockSpec(memory_space=pltpu.VMEM)
    return pl.pallas_call(
        direct_kernel,
        in_specs=[vmem] * 3,
        out_specs=[vmem] * 2,
        out_shape=[
            jax.ShapeDtypeStruct((SPAN, CH), BF16),
            jax.ShapeDtypeStruct((SPAN, CH), F32),
        ],
        scratch_shapes=[pltpu.VMEM((CHUNK, CH), F32)],
        compiler_params=params(10),
        cost_estimate=pl.CostEstimate(
            flops=40 * SPAN * CH, bytes_accessed=3_000_000, transcendentals=0
        ),
    )(both, taps, table)


def finish_kernel(
    states, table, local, chunk, gate_far, out,
    scr, begun, rates, start_s, decay_s, weight_s, gate, sem,
):
    copy = pltpu.make_async_copy(gate_far, gate, sem)
    copy.start()
    z = lax.axis_index("z")
    rate = table[0:16, :]
    rates[...] = rate
    span = jnp.exp(-float(SPAN) * rate)
    total = jnp.zeros((POLES, CH), F32)
    for i in range(NZ - 1):
        total = jnp.where(i < z, total * span + states[i], total)
    start_s[...] = total
    decay = jnp.exp(-rate)
    decay_s[...] = decay
    weight_s[...] = table[16:32, :] * jnp.sqrt(2.0 * rate) * decay
    sub = lax.broadcasted_iota(jnp.int32, (8, LANES), 0)

    copy.wait()

    @pl.loop(0, CH // LANES)
    def _(l):
        here = pl.ds(pl.multiple_of(l * LANES, LANES), LANES)
        for m in range(POLES):
            fade = jnp.exp(-float(CHUNK) * rates[m : m + 1, here] * sub.astype(F32))
            begun[m] = fade * (start_s[m : m + 1, here] * weight_s[m : m + 1, here])
        for p in range(PIECES):
            row0 = p * HERE
            turned = scr.at[p % 2]
            v, e = [], []
            for m in range(POLES):
                at = chunk[m, p * 8 : p * 8 + 8, here]
                v.append(at * weight_s[m : m + 1, here] + begun[m])
                e.append(decay_s[m : m + 1, here])
                if p + 1 < PIECES:
                    begun[m] = begun[m] * jnp.exp(-float(HERE) * rates[m : m + 1, here])
            for j in range(0, CHUNK, 2):
                gates = gate[row0 + 8 * j : row0 + 8 * j + 16, here].astype(F32)
                for i in range(2):
                    parts = list(v)
                    while len(parts) > 1:
                        parts = [a + b for a, b in zip(parts[::2], parts[1::2])]
                    at = row0 + 8 * (j + i)
                    response = rounded(local[at : at + 8, here] + parts[0])
                    turned[pl.ds(j + i, 8, stride=CHUNK), :] = gates[8 * i : 8 * i + 8] * response
                    v = [a * b for a, b in zip(v, e)]
            out[p, here, :] = turned[...].T.astype(BF16)


def finish(states, table, local, chunk, gate):
    vmem = pl.BlockSpec(memory_space=pltpu.VMEM)
    return pl.pallas_call(
        finish_kernel,
        in_specs=[vmem] * 4 + [pl.BlockSpec(memory_space=pltpu.HBM)],
        out_specs=vmem,
        out_shape=jax.ShapeDtypeStruct((PIECES, CH, HERE), BF16),
        scratch_shapes=[
            pltpu.VMEM((2, HERE, LANES), F32),
            pltpu.VMEM((POLES, 8, LANES), F32),
            pltpu.VMEM((POLES, CH), F32),
            pltpu.VMEM((POLES, CH), F32),
            pltpu.VMEM((POLES, CH), F32),
            pltpu.VMEM((POLES, CH), F32),
            pltpu.VMEM((SPAN, CH), BF16),
            pltpu.SemaphoreType.DMA,
        ],
        compiler_params=params(10),
    )(states, table, local, chunk, gate)


def place_kernel(pieces, out):
    for g in range(PIECES):
        for i in range(NZ):
            out[i, g] = pieces[g, 32 * i : 32 * i + 32, :]


def place(pieces):
    out = pl.pallas_call(
        place_kernel,
        out_shape=jax.ShapeDtypeStruct((NZ, PIECES, 32, HERE), BF16),
        compiler_params=params(10),
    )(pieces)
    return out.reshape(1, NZ * PIECES * 32, HERE)


def ring(size, by):
    return [(i, (i + by) % size) for i in range(size)]


def shift(value, axis, by):
    return lax.ppermute(value, axis, ring(lax.axis_size(axis), by))


def spread(value, count=NZ):
    return jnp.broadcast_to(value[None], (count,) + value.shape)


def swap(value, axes):
    return lax.all_to_all(value, axes, split_axis=0, concat_axis=0, tiled=True)


def tail_kernel(own, behind, ahead, mixed, out, sem):
    x = lax.axis_index("x")
    for at, piece in ((3, own), (0, behind), (2, ahead), (1, mixed)):

        @pl.when(x == at)
        def _(piece=piece):
            rows = pl.ds(piece.shape[0] - HALO, HALO)
            copy = pltpu.make_async_copy(piece.at[rows], out, sem)
            copy.start()
            copy.wait()


def last_rows(row):
    any_spec = pl.BlockSpec(memory_space=pl.ANY)
    return pl.pallas_call(
        tail_kernel,
        in_specs=[any_spec] * NX,
        out_specs=any_spec,
        out_shape=jax.ShapeDtypeStruct((HALO, D), BF16),
        scratch_shapes=[pltpu.SemaphoreType.DMA],
        compiler_params=params(10),
    )(*row)


def body(tokens, norm_gain, in_weight, short_filter, rates, residues, skip):
    x, yh, z = lax.axis_index("x"), lax.axis_index("yh"), lax.axis_index("z")
    together = lax.optimization_barrier

    taps = short_filter.reshape(3, 3, NZ, PIECES, 32)
    taps = lax.dynamic_index_in_dim(taps, yh * NX + x, 3, keepdims=False).reshape(3, COLS)
    blocks = columns_by_place(in_weight)
    unit = swap(blocks, ("yl", "yh", "x")).reshape(UNIT, COLS)
    own, mine = normalise(tokens[0], norm_gain[None, :], rates, residues, skip)
    own, unit, taps = together((own, jnp.concatenate([unit, mine]), taps))

    def step(up, down):
        return shift(up, "z", 1), shift(down, "z", -1)

    partner = shift(own, "yh", 1)
    own_1, own_3 = shift(own, "x", 1), shift(own, "x", -1)
    up_1, down_1 = step(unit, unit)
    up_2, down_2 = step(up_1, down_1)
    up_2, down_2, partner, own_1, own_3 = together((up_2, down_2, partner, own_1, own_3))

    mixed_1 = shift(jnp.concatenate([partner, own_1[:HALF]]), "x", 1)
    mixed_3 = shift(jnp.concatenate([partner, own_3[HALF:]]), "x", -1)
    up_3, down_3 = step(up_2, down_2)
    up_4 = shift(up_3, "z", 1)
    up_4, mixed_1, mixed_3 = together((up_4, mixed_1, mixed_3))

    first = shift(mixed_1[:HALF], "x", 1)
    second = shift(mixed_3[HALF:HERE], "x", -1)
    tail = last_rows((own, own_1, own_3, mixed_3))
    halo = [
        lax.ppermute(tail, ("z", "yh"), [(2 * i + 1, 2 * i + 2 + to) for i in range(NZ - 1)])
        for to in range(2)
    ]
    plane = jnp.stack([unit, up_1, up_2, up_3, up_4, down_3, down_2, down_1])
    weights = [plane, shift(plane, "co", 1)]
    arrays = [own, own_1, own_3, partner, mixed_1, mixed_3]

    w, done, table = multiply(arrays, weights)
    both, chunk, state = project(first, second, halo, w, done, taps, table)
    states = swap(state, "z")
    gate, local = direct(both, taps, table)
    pieces = finish(states, table, local, chunk, gate)
    return place(swap(pieces, ("yh", "x")))


def solution(mesh):
    fine = Mesh(mesh.devices.reshape(2, 2, NZ, 2, NX), ("yl", "co", "z", "yh", "x"))
    fsdp, ctx = ("yl", "co"), ("z", "yh", "x")
    in_specs = (
        P(fsdp, ctx, None),
        P(),
        P(fsdp + ctx, None),
        P(),
        P(ctx, None),
        P(ctx, None),
        P(ctx),
    )
    return jax.shard_map(
        body, mesh=fine, in_specs=in_specs, out_specs=P(fsdp, None, ctx), check_vma=False
    )
```
